32 devices in a mesh: rep: 4 (over y, core), dom: 8 (over z, x).
Axes of the slice: x: 2, y: 2, z: 4, core: 2. Of those that a mesh axis runs over, the one named last changes fastest.
Arguments:
- features: bfloat16 [32768, 768], P(('rep', 'dom')), may hold values from -6 to 6
- cotangent: bfloat16 [32768, 1024], P(('rep', 'dom')), may hold values from -0.032958984 to 0.032958984
- w_self: bfloat16 [768, 1024], P('dom'), may hold values from -0.21875 to 0.21875
- w_neigh: bfloat16 [768, 1024], P('dom'), may hold values from -0.21875 to 0.21875
- tile_vals: bfloat16 [1024, 128, 128], P(('rep', 'dom')), may hold values from 0 to 0.088378906
- tile_src: int32 [1024], P(('rep', 'dom')), may hold values from 0 to 7
- tile_peer: int32 [1024], P(('rep', 'dom')), may hold values from 0 to 7
- in_block: int32 [256], P(('rep', 'dom')), may hold values from 0 to 7
Outputs:
- grad_self: float32 [768, 1024], P('dom')
- grad_neigh: float32 [768, 1024], P('dom')
The draws below stay inside these ranges and needn't reach their ends.
Inputs may be any that keep to these rules, and one draw needn't show every extreme that they name: `in_block`: all tiles that one partition sends to one receiving partition land in the same receiver block.
All inputs are finite; a program needn't handle non-finite values.
Results may differ from the reference program's by a relative error of at most 0.023.
Values may be sent and summed in bfloat16 or wider, within the bound.
No kernel may reach another device: no remote copies, remote signals or barrier semaphores. Data moves between devices by JAX's collectives and lax.ppermute only.
A program may use at most 128 MiB of HBM per device.

```python
import math
import jax
import jax.numpy as jnp
import numpy as np
from jax import lax

F = 768
H = 1024
BLK = 128
BLK_DEV = 8
TILE_DEV = 32
ROWS_DEV = 1024
NODES = 8192
TILES = 256
N_REP = 4
N_DOM = 8


def touch_ends(array, key, least, largest):
    shape = array.shape
    index_at = [jax.random.randint(jax.random.fold_in(key, axis), (), 0, shape[axis]) for axis in range(len(shape))]
    array = array.at[tuple(index_at)].set(least)
    longest = shape.index(max(shape))
    index_at[longest] = (index_at[longest] + 1) % shape[longest]
    return array.at[tuple(index_at)].set(largest)


def raised(entries, own_key, source, target, shards_of, factor):
    def block_of(position):
        return (jnp.arange(entries.shape[position]) // (entries.shape[position] // shards_of)).reshape((-1,) + (1,) * (entries.ndim - 1 - position))

    first = jax.random.permutation(own_key, shards_of)[block_of(target)]
    other_side = (block_of(target) + shards_of // 2) % shards_of
    return jnp.where((block_of(source) == first) | (block_of(source) == other_side), factor * entries, entries)


def level_of(stream_key, shape, cuts, smallest, top_value):
    def one(axis_at, parts):
        draws = jax.random.uniform(jax.random.fold_in(jax.random.fold_in(stream_key, 6), axis_at), (parts,), jnp.float32, smallest / len(cuts), top_value / len(cuts))
        return jnp.repeat(jnp.exp(draws), shape[axis_at] // parts).reshape((-1,) + (1,) * (len(shape) - axis_at - 1))

    loudness = one(*cuts[0])
    for cut in cuts[1:]:
        loudness = loudness * one(*cut)
    return loudness


def rank_table(amount, skew):
    portions = [(1 << 20) // math.isqrt(grade ** skew) + 1 for grade in range(1, amount + 1)]
    spread = 1 + sum(portions) // (1 << 30)
    return np.cumsum(np.array([max(1, weight // spread) for weight in portions]))


def ranked(stream_key, shape, amount, lean):
    listing = rank_table(amount, lean)
    ticket = jax.random.randint(jax.random.fold_in(stream_key, 1), shape, 0, int(listing[amount - 1]))
    grade = jnp.searchsorted(jnp.asarray(listing, jnp.int32), ticket, side="right")
    return jax.random.permutation(jax.random.fold_in(stream_key, 2), amount)[grade].astype(jnp.int32)


def bell_draw(own_key, shape, width, bound, split=(), held_as=jnp.bfloat16):
    drawn = jax.random.normal(own_key, shape, jnp.float32) * width
    if len(split) > 0:
        drawn = level_of(own_key, shape, split, -0.22, 0.18) * drawn
    return jnp.clip(drawn, min=-bound, max=bound).astype(held_as)


def heavy_noise(key, shape, deviation, reach, split, heavy, held_as=jnp.bfloat16):
    array = deviation * jax.random.normal(key, shape, jnp.float32)
    if split:
        array = array * level_of(key, shape, split, -0.22, 0.18)
    return jnp.clip(raised(array, jax.random.fold_in(key, 3), *heavy), -reach, reach).astype(held_as)


def setup_inputs(seed: int = 0) -> dict:
    seeds = jax.random.split(jax.random.key(seed), 9)
    return {
        "features": heavy_noise(seeds[0], (N_REP * NODES, F), 1.0, 6.0, ((0, 32),), (0, 1, 32, 2.75)),
        "cotangent": bell_draw(seeds[1], (N_REP * NODES, H), (1.0 / (N_REP * N_DOM * BLK * BLK_DEV) ** 0.5), 0.032958984, ((0, 32),)),
        "w_self": bell_draw(seeds[2], (F, H), F ** -0.5, 0.21875, ((0, 8),)),
        "w_neigh": bell_draw(seeds[3], (F, H), F ** -0.5, 0.21875, ((0, 8),)),
        "tile_vals": jnp.clip(0.088378906 * jax.random.uniform(seeds[4], (N_REP * TILES, BLK, BLK), jnp.float32) ** level_of(seeds[4], (N_REP * TILES, BLK, BLK), ((0, 32),), -0.2, 0.2), 0.0, 0.088378906).astype(jnp.bfloat16),
        "tile_src": touch_ends(jax.random.randint(seeds[5], (N_REP * TILES,), 0, BLK_DEV), jax.random.fold_in(seeds[5], 1), 0, BLK_DEV - 1).astype(jnp.int32),
        "tile_peer": touch_ends(ranked(seeds[6], (N_REP * TILES,), N_DOM, 2), jax.random.fold_in(seeds[6], 3), 0, N_DOM - 1).astype(jnp.int32),
        "in_block": touch_ends(jax.random.randint(seeds[7], (N_REP * N_DOM * N_DOM,), 0, BLK_DEV), jax.random.fold_in(seeds[7], 1), 0, BLK_DEV - 1).astype(jnp.int32),
    }


def gelu_tanh(value):
    return jax.nn.gelu(value, approximate=True)

def reference(features, cotangent, w_self, w_neigh, tile_vals, tile_src, tile_peer, in_block):
    rows = N_DOM * ROWS_DEV
    tile_total = N_DOM * TILE_DEV
    grad_total = jnp.zeros((F, 2 * H), jnp.float32)
    for replica in range(N_REP):
        feats = features[replica * rows:(replica + 1) * rows]
        blocks = feats.reshape(N_DOM, BLK_DEV, BLK, F)
        tiles = tile_vals[replica * tile_total:(replica + 1) * tile_total].reshape(N_DOM, TILE_DEV, BLK, BLK)
        sources = tile_src[replica * tile_total:(replica + 1) * tile_total].reshape(N_DOM, TILE_DEV)
        peers = tile_peer[replica * tile_total:(replica + 1) * tile_total].reshape(N_DOM, TILE_DEV)
        targets = in_block[replica * N_DOM * N_DOM:(replica + 1) * N_DOM * N_DOM].reshape(N_DOM, N_DOM)
        receivers = jnp.arange(N_DOM, dtype=jnp.int32)

        def add_source(total, sender):
            own = blocks[sender]
            picked = own[sources[sender]]
            product = jnp.einsum('tij,tjf->tif', tiles[sender].astype(jnp.float32), picked.astype(jnp.float32))
            slots = jnp.zeros((N_DOM, BLK, F), jnp.float32).at[peers[sender]].add(product)
            sent = lax.optimization_barrier(slots.astype(jnp.bfloat16)).astype(jnp.float32)
            total = total.at[receivers, targets[:, sender]].add(sent)
            return (total, None)
        start = jnp.zeros((N_DOM, BLK_DEV, BLK, F), jnp.float32)
        aggregate, _ = lax.scan(add_source, start, jnp.arange(N_DOM, dtype=jnp.int32))
        aggregate = aggregate.reshape(rows, F).astype(jnp.bfloat16)
        preact = jnp.dot(feats, w_self, preferred_element_type=jnp.float32) + jnp.dot(aggregate, w_neigh, preferred_element_type=jnp.float32)
        cot = cotangent[replica * rows:(replica + 1) * rows].astype(jnp.float32)
        _, pull = jax.vjp(gelu_tanh, preact)
        grad_pre = pull(cot)[0].astype(jnp.bfloat16)
        feats32 = feats.astype(jnp.float32).reshape(N_DOM, ROWS_DEV, F)
        agg32 = aggregate.astype(jnp.float32).reshape(N_DOM, ROWS_DEV, F)
        pre32 = grad_pre.astype(jnp.float32).reshape(N_DOM, ROWS_DEV, H)
        terms = jnp.concatenate([jnp.einsum('dnf,dnh->dfh', feats32, pre32), jnp.einsum('dnf,dnh->dfh', agg32, pre32)], axis=2)
        rounded = lax.optimization_barrier(terms.astype(jnp.bfloat16)).astype(jnp.float32)
        grad_total = grad_total + lax.optimization_barrier(jnp.sum(rounded, axis=0))
    return (grad_total[:, :H], grad_total[:, H:])
```

```python
import functools

import jax
import jax.numpy as jnp
from jax import lax
from jax.experimental import pallas as pl
from jax.experimental.pallas import tpu as pltpu
from jax.sharding import PartitionSpec as P

F32 = jnp.float32
BF16 = jnp.bfloat16
SCALE = 0.7978845608
CUBIC = 0.044715
MIB = 1 << 20
SMEM = pl.BlockSpec(memory_space=pltpu.SMEM)
VMEM = pl.BlockSpec(memory_space=pltpu.VMEM)


def swap(value, axis, step):
    size = lax.axis_size(axis)
    return lax.ppermute(value, axis, [(index, index ^ step) for index in range(size)])


def slots_kernel(me_ref, src_ref, peer_ref, tiles_ref, features_ref, *refs):
    out_refs, dense = refs[:-1], refs[-1]
    count, block, _ = tiles_ref.shape
    dense[...] = jnp.zeros_like(dense)
    me = me_ref[0]

    def place(tile, carry):
        row = pl.multiple_of((peer_ref[tile] ^ me) * block, block)
        column = pl.multiple_of(src_ref[tile] * block, block)
        at = (pl.ds(row, block), pl.ds(column, block))
        dense[at] = dense[at] + tiles_ref[tile].astype(F32)
        return carry

    lax.fori_loop(0, count, place, 0)
    group = 4
    for first in range(0, len(out_refs), group):
        rows = dense[first * block : (first + group) * block, :].astype(BF16)
        product = jnp.dot(rows, features_ref[...], preferred_element_type=F32).astype(BF16)
        for offset in range(group):
            out_refs[first + offset][...] = product[offset * block : (offset + 1) * block, :]


def self_kernel(core_ref, features_ref, mine_ref, other_ref, out_ref):
    rows = features_ref.shape[0]
    chunk = 256

    def product(weight_ref):
        def body():
            for first in range(0, rows, chunk):
                at = slice(first, first + chunk)
                out_ref[at, :] = jnp.dot(features_ref[at, :], weight_ref[...], preferred_element_type=F32)

        return body

    pl.when(core_ref[0] == 0)(product(mine_ref))
    pl.when(core_ref[0] != 0)(product(other_ref))


def layer_kernel(me_ref, core_ref, into_ref, cotangent_ref, total_ref, mine_ref, other_ref, *refs):
    slot_refs, (aggregate_ref, grad_ref, summed) = refs[:-3], refs[-3:]
    block = slot_refs[0].shape[0]
    rows = aggregate_ref.shape[0]
    me = me_ref[0]
    summed[...] = jnp.zeros_like(summed)
    for step, slot_ref in enumerate(slot_refs):
        at = pl.ds(pl.multiple_of(into_ref[me ^ step] * block, block), block)
        summed[at, :] = summed[at, :] + slot_ref[...].astype(F32)
    aggregate_ref[...] = summed[...].astype(BF16)
    chunk = 256

    def product(weight_ref):
        def body():
            for first in range(0, rows, chunk):
                at = slice(first, first + chunk)
                value = total_ref[at, :] + jnp.dot(
                    aggregate_ref[at, :], weight_ref[...], preferred_element_type=F32
                )
                square = value * value
                bend = jnp.tanh(SCALE * value * (1.0 + CUBIC * square))
                slope = 0.5 * (1.0 + bend) + (0.5 * SCALE) * value * (1.0 - bend * bend) * (
                    1.0 + 3.0 * CUBIC * square
                )
                grad_ref[at, :] = (cotangent_ref[at, :].astype(F32) * slope).astype(BF16)

        return body

    pl.when(core_ref[0] == 0)(product(other_ref))
    pl.when(core_ref[0] != 0)(product(mine_ref))


def term_kernel(use_ref, features_ref, aggregate_ref, grad_ref, out_ref):
    contract = (((0,), (0,)), ((), ()))

    def product(left_ref):
        def body():
            out_ref[...] = lax.dot_general(
                left_ref[...], grad_ref[...], contract, preferred_element_type=F32
            ).astype(BF16)

        return body

    pl.when(use_ref[0] == 0)(product(features_ref))
    pl.when(use_ref[0] != 0)(product(aggregate_ref))


def call(kernel, outs, places, scratch=(), flops=0, moved=0, vmem=48):
    return pl.pallas_call(
        kernel,
        out_shape=outs,
        in_specs=places,
        out_specs=jax.tree.map(lambda _: VMEM, outs),
        scratch_shapes=list(scratch),
        compiler_params=pltpu.CompilerParams(vmem_limit_bytes=vmem * MIB),
        cost_estimate=pl.CostEstimate(flops=flops, bytes_accessed=moved, transcendentals=0),
    )


def gather_weights(w_self, w_neigh, core, high):
    dom_size = lax.axis_size("dom")
    parts = lax.axis_size("rep") // 2
    hidden = w_self.shape[1]
    share = hidden // parts
    own = jnp.where(core == 0, w_self, w_neigh)
    held = lax.dynamic_slice_in_dim(own, high * share, share, 1)[None]
    step = dom_size // 2
    me = lax.axis_index("dom")
    while step:
        other = swap(held, "dom", step)
        upper = (me & step) != 0
        held = jnp.stack([jnp.where(upper, other, held), jnp.where(upper, held, other)], axis=1)
        held = held.reshape((-1,) + held.shape[2:])
        step //= 2
    held = held.reshape(-1, share)
    step = 1
    while step < parts:
        other = swap(held, "rep", 2 * step)
        upper = (high & step) != 0
        held = jnp.concatenate([jnp.where(upper, other, held), jnp.where(upper, held, other)], axis=1)
        step *= 2
    return held, swap(held, "rep", 1)


def added(left, right):
    return (left.astype(F32) + right.astype(F32)).astype(BF16)


def half(value, axis, which):
    size = value.shape[axis] // 2
    return lax.dynamic_slice_in_dim(value, which * size, size, axis)


def reduce_high(value, high):
    parts = lax.axis_size("rep") // 2
    step = parts // 2
    while step:
        upper = (high // step) % 2
        value = added(half(value, 2, upper), swap(half(value, 2, 1 - upper), "rep", 2 * step))
        step //= 2
    return value


def reduce_low(value, low):
    value = value.reshape(value.shape[0] // 2, 2, *value.shape[1:])
    sent = lax.dynamic_index_in_dim(value, 1 - low, 1, keepdims=False)
    kept = lax.dynamic_index_in_dim(value, low, 1, keepdims=False)
    return added(kept, swap(sent, "dom", 1))


def shards(features, cotangent, w_self, w_neigh, tile_vals, tile_src, tile_peer, in_block):
    dom_size = lax.axis_size("dom")
    rows, width = features.shape
    hidden = w_self.shape[1]
    block = tile_vals.shape[1]
    me = lax.axis_index("dom")
    rep = lax.axis_index("rep")
    core, high = rep % 2, rep // 2
    low, place = me % 2, me // 2
    me_arg = me.astype(jnp.int32).reshape(1)
    core_arg = core.astype(jnp.int32).reshape(1)

    mine, other = gather_weights(w_self, w_neigh, core, high)
    slots = call(
        slots_kernel,
        [jax.ShapeDtypeStruct((block, width), BF16)] * dom_size,
        [SMEM, SMEM, SMEM, VMEM, VMEM],
        [pltpu.VMEM((dom_size * block, rows), F32)],
        flops=2 * dom_size * block * rows * width,
        moved=tile_vals.size * 2 + rows * width * 4,
    )(me_arg, tile_src, tile_peer, tile_vals, features)
    received = [slots[0]] + [swap(slots[step], "dom", step) for step in range(1, dom_size)]

    total = call(
        self_kernel,
        jax.ShapeDtypeStruct((rows, hidden), F32),
        [SMEM, VMEM, VMEM, VMEM],
        flops=2 * rows * width * hidden,
        moved=4 * rows * hidden,
    )(core_arg, features, mine, other)
    aggregate, grad = call(
        layer_kernel,
        [jax.ShapeDtypeStruct((rows, width), BF16), jax.ShapeDtypeStruct((rows, hidden), BF16)],
        [SMEM, SMEM, SMEM] + [VMEM] * (4 + dom_size),
        [pltpu.VMEM((rows, width), F32)],
        flops=2 * rows * width * hidden,
        moved=4 * rows * hidden,
    )(me_arg, core_arg, in_block, cotangent, total, mine, other, *received)

    def term(use):
        return call(
            term_kernel,
            jax.ShapeDtypeStruct((width, hidden), BF16),
            [SMEM, VMEM, VMEM, VMEM],
            flops=2 * rows * width * hidden,
            moved=2 * width * hidden,
        )(use, features, aggregate, grad)

    sent = term(1 - core_arg)
    kept = term(core_arg)
    chip = added(kept, swap(sent, "rep", 1)).reshape(dom_size, width // dom_size, hidden)
    first, second = chip[:, :, : hidden // 2], chip[:, :, hidden // 2 :]
    first = reduce_low(first, low)
    second = reduce_high(second, high)
    first = reduce_high(first, high)
    second = reduce_low(second, low)
    both = jnp.concatenate([first, second], axis=2)
    total = lax.dynamic_index_in_dim(both, place, 0, keepdims=False).astype(F32)
    for step in range(1, dom_size // 2):
        total = total + swap(
            lax.dynamic_index_in_dim(both, place ^ step, 0, keepdims=False), "dom", 2 * step
        ).astype(F32)
    share = total.astype(BF16)
    size = share.shape[1] // 2
    step = 1
    parts = [share[:, :size], share[:, size:]]
    while step < lax.axis_size("rep") // 2:
        upper = (high & step) != 0
        others = swap(jnp.concatenate(parts, axis=1), "rep", 2 * step)
        width_now = parts[0].shape[1]
        others = [others[:, :width_now], others[:, width_now:]]
        parts = [
            jnp.concatenate([jnp.where(upper, b, a), jnp.where(upper, a, b)], axis=1)
            for a, b in zip(parts, others)
        ]
        step *= 2
    whole = jnp.concatenate(parts, axis=1)
    opposite = swap(whole, "rep", 1)
    return (
        jnp.where(core == 0, whole, opposite).astype(F32),
        jnp.where(core == 0, opposite, whole).astype(F32),
    )


def solution(mesh):
    in_specs = (
        P(("rep", "dom"), None),
        P(("rep", "dom"), None),
        P("dom", None),
        P("dom", None),
        P(("rep", "dom"), None, None),
        P(("rep", "dom")),
        P(("rep", "dom")),
        P(("rep", "dom")),
    )
    out_specs = (P("dom", None), P("dom", None))
    return jax.shard_map(shards, mesh=mesh, in_specs=in_specs, out_specs=out_specs, check_vma=False)
```

```python
import jax
import jax.numpy as jnp
from jax import lax
from jax.experimental import pallas as pl
from jax.experimental.pallas import tpu as pltpu
from jax.sharding import PartitionSpec as P

F32 = jnp.float32
BF16 = jnp.bfloat16
SCALE = 0.7978845608
CUBIC = 0.044715
MIB = 1 << 20
SMEM = pl.BlockSpec(memory_space=pltpu.SMEM)
VMEM = pl.BlockSpec(memory_space=pltpu.VMEM)


def swap(value, axis, step):
    size = lax.axis_size(axis)
    return lax.ppermute(value, axis, [(index, index ^ step) for index in range(size)])


def slots_kernel(src_ref, peer_ref, tiles_ref, features_ref, out_ref, dense):
    count, block, _ = tiles_ref.shape
    dense[...] = jnp.zeros_like(dense)

    def place(tile, carry):
        row = pl.multiple_of(peer_ref[tile] * block, block)
        column = pl.multiple_of(src_ref[tile] * block, block)
        at = (pl.ds(row, block), pl.ds(column, block))
        dense[at] = dense[at] + tiles_ref[tile].astype(F32)
        return carry

    lax.fori_loop(0, count, place, 0)
    chunk = 4 * block
    for first in range(0, out_ref.shape[0], chunk):
        rows = dense[first : first + chunk, :].astype(BF16)
        out_ref[first : first + chunk, :] = jnp.dot(
            rows, features_ref[...], preferred_element_type=F32
        ).astype(BF16)


def self_kernel(core_ref, features_ref, mine_ref, other_ref, out_ref):
    rows = features_ref.shape[0]
    chunk = 256

    def product(weight_ref):
        def body():
            for first in range(0, rows, chunk):
                at = slice(first, first + chunk)
                out_ref[at, :] = jnp.dot(features_ref[at, :], weight_ref[...], preferred_element_type=F32)

        return body

    pl.when(core_ref[0] == 0)(product(mine_ref))
    pl.when(core_ref[0] != 0)(product(other_ref))


def layer(core_ref, cotangent_ref, total_ref, mine_ref, other_ref, aggregate_ref, grad_ref):
    rows = aggregate_ref.shape[0]
    chunk = 256

    def product(weight_ref):
        def body():
            for first in range(0, rows, chunk):
                at = slice(first, first + chunk)
                value = total_ref[at, :] + jnp.dot(
                    aggregate_ref[at, :], weight_ref[...], preferred_element_type=F32
                )
                square = value * value
                bend = jnp.tanh(value * (SCALE + SCALE * CUBIC * square))
                inner = value * (SCALE + 3.0 * SCALE * CUBIC * square)
                slope = (1.0 + bend) * (0.5 + 0.5 * inner * (1.0 - bend))
                grad_ref[at, :] = (cotangent_ref[at, :].astype(F32) * slope).astype(BF16)

        return body

    pl.when(core_ref[0] == 0)(product(other_ref))
    pl.when(core_ref[0] != 0)(product(mine_ref))


def first_layer_kernel(
    core_ref, into_ref, cotangent_ref, total_ref, mine_ref, other_ref, slots_ref, aggregate_ref, grad_ref, summed
):
    senders, block, _ = slots_ref.shape
    summed[...] = jnp.zeros_like(summed)
    for sender in range(senders):
        at = pl.ds(pl.multiple_of(into_ref[sender] * block, block), block)
        summed[at, :] = summed[at, :] + slots_ref[sender].astype(F32)
    aggregate_ref[...] = summed[...].astype(BF16)
    layer(core_ref, cotangent_ref, total_ref, mine_ref, other_ref, aggregate_ref, grad_ref)


def term_kernel(use_ref, turned_ref, aggregate_ref, grad_ref, out_ref):
    @pl.when(use_ref[0] == 0)
    def _():
        out_ref[...] = jnp.dot(turned_ref[...], grad_ref[...], preferred_element_type=F32).astype(BF16)

    @pl.when(use_ref[0] != 0)
    def _():
        out_ref[...] = lax.dot_general(
            aggregate_ref[...], grad_ref[...], (((0,), (0,)), ((), ())), preferred_element_type=F32
        ).astype(BF16)


def call(kernel, outs, places, scratch=(), flops=0, moved=0, vmem=24):
    return pl.pallas_call(
        kernel,
        out_shape=outs,
        in_specs=places,
        out_specs=jax.tree.map(lambda _: VMEM, outs),
        scratch_shapes=list(scratch),
        compiler_params=pltpu.CompilerParams(vmem_limit_bytes=vmem * MIB),
        cost_estimate=pl.CostEstimate(flops=flops, bytes_accessed=moved, transcendentals=0),
    )


def after(value, *others):
    return lax.optimization_barrier((value, *others))[0]


def joined(held, other, upper, axis):
    return jnp.stack([jnp.where(upper, other, held), jnp.where(upper, held, other)], axis=axis)


def gather_low(held, me):
    held = joined(held, swap(held, "dom", 1), (me & 1) != 0, 1)
    return held.reshape(-1, held.shape[-1])


def gather_high(held, high):
    step = 1
    while step < lax.axis_size("rep") // 2:
        other = swap(held, "rep", 2 * step)
        upper = (high & step) != 0
        held = jnp.concatenate([jnp.where(upper, other, held), jnp.where(upper, held, other)], axis=-1)
        step *= 2
    return held


def added(left, right):
    return (left.astype(F32) + right.astype(F32)).astype(BF16)


def half(value, axis, which):
    size = value.shape[axis] // 2
    return lax.dynamic_slice_in_dim(value, which * size, size, axis)


def reduce_high(value, high):
    parts = lax.axis_size("rep") // 2
    step = parts // 2
    while step:
        upper = (high // step) % 2
        value = added(half(value, 2, upper), swap(half(value, 2, 1 - upper), "rep", 2 * step))
        step //= 2
    return value


def reduce_low(value, low):
    value = value.reshape(value.shape[0] // 2, 2, *value.shape[1:])
    sent = lax.dynamic_index_in_dim(value, 1 - low, 1, keepdims=False)
    kept = lax.dynamic_index_in_dim(value, low, 1, keepdims=False)
    return added(kept, swap(sent, "dom", 1))


def shards(features, cotangent, w_self, w_neigh, tile_vals, tile_src, tile_peer, in_block):
    dom_size = lax.axis_size("dom")
    rows, width = features.shape
    hidden = w_self.shape[1]
    block = tile_vals.shape[1]
    me = lax.axis_index("dom")
    rep = lax.axis_index("rep")
    parts = lax.axis_size("rep") // 2
    core, high = rep % 2, rep // 2
    low, place = me % 2, me // 2
    core_arg = core.astype(jnp.int32).reshape(1)

    half_width = hidden // 2
    share = half_width // parts

    own = jnp.where(core == 0, w_self, w_neigh)
    held = jnp.concatenate(
        [
            lax.dynamic_slice_in_dim(own, high * share, share, 1),
            lax.dynamic_slice_in_dim(own, half_width + high * share, share, 1),
        ],
        axis=1,
    )[None]
    step = dom_size // 2
    other = swap(held, "dom", step)

    slots = call(
        slots_kernel,
        jax.ShapeDtypeStruct((dom_size * block, width), BF16),
        [SMEM, SMEM, VMEM, VMEM],
        [pltpu.VMEM((dom_size * block, rows), F32)],
        flops=2 * dom_size * block * rows * width,
        moved=tile_vals.size * 2 + rows * width * 4,
    )(tile_src, tile_peer, tile_vals, features)
    other, slots = lax.optimization_barrier((other, slots))
    received = lax.all_to_all(slots.reshape(dom_size, block, width), "dom", split_axis=0, concat_axis=0, tiled=True)

    while step > 1:
        held = joined(held, other, (me & step) != 0, 1).reshape(-1, *held.shape[1:])
        step //= 2
        if step > 1:
            other = swap(held, "dom", step)
    weights = [
        gather_high(gather_low(held[..., :share], me), high),
        gather_low(gather_high(held[..., share:], high), me),
    ]

    others = [swap(weight, "rep", 1) for weight in weights]

    totals = [
        call(
            self_kernel,
            jax.ShapeDtypeStruct((rows, half_width), F32),
            [SMEM, VMEM, VMEM, VMEM],
            flops=2 * rows * width * half_width,
            moved=4 * rows * half_width,
        )(core_arg, features, weight, other)
        for weight, other in zip(weights, others)
    ]
    turned = features.T

    cotangents = [cotangent[:, :half_width], cotangent[:, half_width:]]

    def sums(grad):
        def term(use):
            return call(
                term_kernel,
                jax.ShapeDtypeStruct((width, half_width), BF16),
                [SMEM, VMEM, VMEM, VMEM],
                flops=2 * rows * width * half_width,
                moved=2 * width * half_width,
            )(use, turned, aggregate, grad)

        sent = swap(term(1 - core_arg), "rep", 1)
        chip = added(term(core_arg), sent).reshape(dom_size, width // dom_size, half_width)
        first, second = chip[:, :, : half_width // 2], chip[:, :, half_width // 2 :]
        first, second = reduce_low(first, low), reduce_high(second, high)
        first, second = reduce_high(first, high), reduce_low(second, low)
        both = jnp.concatenate([first, second], axis=2)
        total = lax.dynamic_index_in_dim(both, place, 0, keepdims=False).astype(F32)
        for step in range(1, dom_size // 2):
            piece = lax.dynamic_index_in_dim(both, place ^ step, 0, keepdims=False)
            total = total + swap(piece, "dom", 2 * step).astype(F32)
        return total.astype(BF16)

    aggregate, grad = call(
        first_layer_kernel,
        [jax.ShapeDtypeStruct((rows, width), BF16), jax.ShapeDtypeStruct((rows, half_width), BF16)],
        [SMEM, SMEM] + [VMEM] * 5,
        [pltpu.VMEM((rows, width), F32)],
        flops=2 * rows * width * half_width,
        moved=4 * rows * half_width,
    )(core_arg, in_block, cotangents[0], totals[0], weights[0], others[0], received)
    shares = [sums(grad)]
    grad = call(
        layer,
        jax.ShapeDtypeStruct((rows, half_width), BF16),
        [SMEM] + [VMEM] * 5,
        flops=2 * rows * width * half_width,
        moved=4 * rows * half_width,
    )(core_arg, cotangents[1], totals[1], weights[1], others[1], aggregate)
    shares.append(sums(grad))

    size = shares[0].shape[1] // 2
    held = jnp.stack([share[:, at : at + size] for share in shares for at in (0, size)])
    held = gather_high(held, high)
    whole = jnp.concatenate([held[index] for index in range(held.shape[0])], axis=1)
    opposite = swap(whole, "rep", 1)
    return (
        jnp.where(core == 0, whole, opposite).astype(F32),
        jnp.where(core == 0, opposite, whole).astype(F32),
    )


def solution(mesh):
    in_specs = (
        P(("rep", "dom"), None),
        P(("rep", "dom"), None),
        P("dom", None),
        P("dom", None),
        P(("rep", "dom"), None, None),
        P(("rep", "dom")),
        P(("rep", "dom")),
        P(("rep", "dom")),
    )
    out_specs = (P("dom", None), P("dom", None))
    return jax.shard_map(shards, mesh=mesh, in_specs=in_specs, out_specs=out_specs, check_vma=False)
```

```python
import functools

import jax
import jax.numpy as jnp
from jax import lax
from jax.experimental import pallas as pl
from jax.experimental.pallas import tpu as pltpu
from jax.sharding import PartitionSpec as P

F32 = jnp.float32
BF16 = jnp.bfloat16
SCALE = 0.7978845608
CUBIC = 0.044715
MIB = 1 << 20
HBM = pl.BlockSpec(memory_space=pltpu.HBM)
SMEM = pl.BlockSpec(memory_space=pltpu.SMEM)
VMEM = pl.BlockSpec(memory_space=pltpu.VMEM)
DMA = pltpu.SemaphoreType.DMA


def swap(value, axis, step):
    size = lax.axis_size(axis)
    return lax.ppermute(value, axis, [(index, index ^ step) for index in range(size)])


def slots_kernel(
    src_hbm, peer_hbm, tiles_hbm, features_hbm, out_hbm, src, peer, tiles, features, dense, out, in_sems, out_sems
):
    copies = [
        pltpu.make_async_copy(source, target, in_sems.at[index])
        for index, (source, target) in enumerate(
            [(src_hbm, src), (peer_hbm, peer), (tiles_hbm, tiles), (features_hbm, features)]
        )
    ]
    for copy in copies:
        copy.start()
    count, block, _ = tiles.shape
    dense[...] = jnp.zeros_like(dense)
    for copy in copies[:3]:
        copy.wait()

    def place(tile, carry):
        row = pl.multiple_of(peer[tile] * block, block)
        column = pl.multiple_of(src[tile] * block, block)
        at = (pl.ds(row, block), pl.ds(column, block))
        dense[at] = dense[at] + tiles[tile].astype(F32)
        return carry

    lax.fori_loop(0, count, place, 0)
    copies[3].wait()
    chunk = 4 * block
    results = []
    for index in range(out.shape[0] // chunk):
        at = slice(index * chunk, (index + 1) * chunk)
        out[at, :] = jnp.dot(dense[at, :].astype(BF16), features[...], preferred_element_type=F32).astype(BF16)
        results.append(pltpu.make_async_copy(out.at[at, :], out_hbm.at[at, :], out_sems.at[index]))
        results[-1].start()
    for result in results:
        result.wait()


def self_kernel(core_ref, features_ref, first_ref, second_ref, other_first_ref, other_second_ref, out_ref):
    rows = features_ref.shape[0]
    half_width = first_ref.shape[1]
    chunk = 256

    def product(*weight_refs):
        def body():
            for first in range(0, rows, chunk):
                at = slice(first, first + chunk)
                for index, weight_ref in enumerate(weight_refs):
                    out_ref[at, index * half_width : (index + 1) * half_width] = jnp.dot(
                        features_ref[at, :], weight_ref[...], preferred_element_type=F32
                    )

        return body

    pl.when(core_ref[0] == 0)(product(first_ref, second_ref))
    pl.when(core_ref[0] != 0)(product(other_first_ref, other_second_ref))


def layer_kernel(
    core_ref,
    into_ref,
    first_ref,
    second_ref,
    other_first_ref,
    other_second_ref,
    slots_hbm,
    total_hbm,
    cotangent_hbm,
    aggregate_ref,
    grad_ref,
    slots,
    total,
    cotangent,
    summed,
    slot_sems,
    row_sems,
):
    senders, block, _ = slots.shape
    rows = aggregate_ref.shape[0]
    half_width = first_ref.shape[1]
    chunk = 256
    arrivals = [
        pltpu.make_async_copy(slots_hbm.at[sender], slots.at[sender], slot_sems.at[sender]) for sender in range(senders)
    ]
    for arrival in arrivals:
        arrival.start()
    streams = []
    for index in range(rows // chunk):
        at = slice(index * chunk, (index + 1) * chunk)
        streams.append(
            [
                pltpu.make_async_copy(total_hbm.at[at, :], total.at[at, :], row_sems.at[0, index]),
                pltpu.make_async_copy(cotangent_hbm.at[at, :], cotangent.at[at, :], row_sems.at[1, index]),
            ]
        )
        for stream in streams[-1]:
            stream.start()
    summed[...] = jnp.zeros_like(summed)
    for sender in range(senders):
        arrivals[sender].wait()
        at = pl.ds(pl.multiple_of(into_ref[sender] * block, block), block)
        summed[at, :] = summed[at, :] + slots[sender].astype(F32)
    aggregate_ref[...] = summed[...].astype(BF16)

    def product(*weight_refs):
        def body():
            for index in range(rows // chunk):
                at = slice(index * chunk, (index + 1) * chunk)
                for stream in streams[index]:
                    stream.wait()
                for half, weight_ref in enumerate(weight_refs):
                    columns = slice(half * half_width, (half + 1) * half_width)
                    value = total[at, columns] + jnp.dot(
                        aggregate_ref[at, :], weight_ref[...], preferred_element_type=F32
                    )
                    square = value * value
                    bend = jnp.tanh(value * (SCALE + SCALE * CUBIC * square))
                    inner = value * (SCALE + 3.0 * SCALE * CUBIC * square)
                    slope = (1.0 + bend) * (0.5 + 0.5 * inner * (1.0 - bend))
                    grad_ref[at, columns] = (cotangent[at, columns].astype(F32) * slope).astype(BF16)

        return body

    pl.when(core_ref[0] == 0)(product(other_first_ref, other_second_ref))
    pl.when(core_ref[0] != 0)(product(first_ref, second_ref))


def term_kernel(half, use_ref, turned_ref, aggregate_ref, grad_ref, *refs):
    out_ref = refs[-1]
    half_width = out_ref.shape[1]
    columns = slice(half * half_width, (half + 1) * half_width)

    def store(value):
        if len(refs) > 1:
            value = value + refs[0][...].astype(F32)
        out_ref[...] = value.astype(BF16)

    @pl.when(use_ref[0] == 0)
    def _():
        store(jnp.dot(turned_ref[...], grad_ref[:, columns], preferred_element_type=F32))

    @pl.when(use_ref[0] != 0)
    def _():
        store(
            lax.dot_general(
                aggregate_ref[...], grad_ref[:, columns], (((0,), (0,)), ((), ())), preferred_element_type=F32
            )
        )


def call(kernel, outs, places, out_places, scratch=(), flops=0, moved=0, vmem=16):
    return pl.pallas_call(
        kernel,
        out_shape=outs,
        in_specs=places,
        out_specs=out_places,
        scratch_shapes=list(scratch),
        compiler_params=pltpu.CompilerParams(vmem_limit_bytes=vmem * MIB),
        cost_estimate=pl.CostEstimate(flops=flops, bytes_accessed=moved, transcendentals=0),
    )


def joined(held, other, upper, axis):
    return jnp.stack([jnp.where(upper, other, held), jnp.where(upper, held, other)], axis=axis)


def gather_low(held, me):
    held = joined(held, swap(held, "dom", 1), (me & 1) != 0, 1)
    return held.reshape(-1, held.shape[-1])


def gather_high(held, high):
    step = 1
    while step < lax.axis_size("rep") // 2:
        other = swap(held, "rep", 2 * step)
        upper = (high & step) != 0
        held = jnp.concatenate([jnp.where(upper, other, held), jnp.where(upper, held, other)], axis=-1)
        step *= 2
    return held


def added(left, right):
    return (left.astype(F32) + right.astype(F32)).astype(BF16)


def half_of(value, axis, which):
    size = value.shape[axis] // 2
    return lax.dynamic_slice_in_dim(value, which * size, size, axis)


def reduce_high(value, high):
    step = lax.axis_size("rep") // 4
    while step:
        upper = (high // step) % 2
        value = added(half_of(value, 2, upper), swap(half_of(value, 2, 1 - upper), "rep", 2 * step))
        step //= 2
    return value


def reduce_low(value, low):
    value = value.reshape(value.shape[0] // 2, 2, *value.shape[1:])
    sent = lax.dynamic_index_in_dim(value, 1 - low, 1, keepdims=False)
    kept = lax.dynamic_index_in_dim(value, low, 1, keepdims=False)
    return added(kept, swap(sent, "dom", 1))


def shards(features, cotangent, w_self, w_neigh, tile_vals, tile_src, tile_peer, in_block):
    dom_size = lax.axis_size("dom")
    rows, width = features.shape
    hidden = w_self.shape[1]
    block = tile_vals.shape[1]
    me = lax.axis_index("dom")
    rep = lax.axis_index("rep")
    parts = lax.axis_size("rep") // 2
    core, high = rep & 1, rep >> 1
    low, place = me & 1, me >> 1
    core_arg = core.astype(jnp.int32).reshape(1)
    half_width = hidden // 2
    share = half_width // parts

    own = jnp.where(core == 0, w_self, w_neigh)
    held = jnp.concatenate(
        [
            lax.dynamic_slice_in_dim(own, high * share, share, 1),
            lax.dynamic_slice_in_dim(own, half_width + high * share, share, 1),
        ],
        axis=1,
    )
    pieces = [held] + [swap(held, "dom", 2 * step) for step in range(1, dom_size // 2)]
    slots = call(
        slots_kernel,
        jax.ShapeDtypeStruct((dom_size * block, width), BF16),
        [HBM] * 4,
        HBM,
        [
            pltpu.SMEM(tile_src.shape, jnp.int32),
            pltpu.SMEM(tile_peer.shape, jnp.int32),
            pltpu.VMEM(tile_vals.shape, BF16),
            pltpu.VMEM(features.shape, BF16),
            pltpu.VMEM((dom_size * block, rows), F32),
            pltpu.VMEM((dom_size * block, width), BF16),
            DMA((4,)),
            DMA((dom_size // 4,)),
        ],
        flops=2 * dom_size * block * rows * width,
        moved=tile_vals.size * 2 + rows * width * 4,
        vmem=16 if dom_size <= 8 else 40,
    )(tile_src, tile_peer, tile_vals, features)
    received = lax.all_to_all(slots.reshape(dom_size, block, width), "dom", split_axis=0, concat_axis=0, tiled=True)

    *pieces, _ = lax.optimization_barrier((*pieces, slots))
    bit = 1
    while len(pieces) > 1:
        upper = (place & bit) != 0
        pieces = [joined(pieces[at], pieces[at + 1], upper, 0) for at in range(0, len(pieces), 2)]
        pieces = [piece.reshape(-1, *held.shape) for piece in pieces]
        bit *= 2
    weights = [
        gather_high(gather_low(pieces[0][..., :share], me), high),
        gather_low(gather_high(pieces[0][..., share:], high), me),
    ]
    weights += [swap(weight, "rep", 1) for weight in weights]
    total = call(
        self_kernel,
        jax.ShapeDtypeStruct((rows, hidden), F32),
        [SMEM] + [VMEM] * 5,
        VMEM,
        flops=2 * rows * width * hidden,
        moved=4 * rows * hidden,
    )(core_arg, features, *weights)
    turned = features.T

    aggregate, grad = call(
        layer_kernel,
        [jax.ShapeDtypeStruct((rows, width), BF16), jax.ShapeDtypeStruct((rows, hidden), BF16)],
        [SMEM, SMEM] + [VMEM] * 4 + [HBM] * 3,
        [VMEM, VMEM],
        [
            pltpu.VMEM((dom_size, block, width), BF16),
            pltpu.VMEM((rows, hidden), F32),
            pltpu.VMEM((rows, hidden), BF16),
            pltpu.VMEM((rows, width), F32),
            DMA((dom_size,)),
            DMA((2, rows // 256)),
        ],
        flops=2 * rows * width * hidden,
        moved=4 * rows * hidden,
        vmem=24 if dom_size <= 8 else 40,
    )(core_arg, in_block, *weights, received, total, cotangent)

    def term(half, use, *others):
        return call(
            functools.partial(term_kernel, half),
            jax.ShapeDtypeStruct((width, half_width), BF16),
            [SMEM] + [VMEM] * (3 + len(others)),
            VMEM,
            flops=2 * rows * width * half_width,
            moved=2 * width * half_width,
        )(use, turned, aggregate, grad, *others)

    others = [swap(term(half, 1 - core_arg), "rep", 1) for half in range(2)]
    first, second = [
        term(half, core_arg, others[half]).reshape(dom_size, width // dom_size, half_width) for half in range(2)
    ]
    first, second = reduce_low(first, low), reduce_high(second, high)
    first, second = reduce_high(first, high), reduce_low(second, low)
    both = jnp.concatenate([first, second], axis=2)
    summed = lax.dynamic_index_in_dim(both, place, 0, keepdims=False).astype(F32)
    for step in range(1, dom_size // 2):
        piece = lax.dynamic_index_in_dim(both, place ^ step, 0, keepdims=False)
        summed = summed + swap(piece, "dom", 2 * step).astype(F32)
    summed = summed.astype(BF16)
    held = gather_high(jnp.stack([summed[:, :share], summed[:, share:]]), high)
    whole = jnp.concatenate([held[0], held[1]], axis=1)
    opposite = swap(whole, "rep", 1)
    return (
        jnp.where(core == 0, whole, opposite).astype(F32),
        jnp.where(core == 0, opposite, whole).astype(F32),
    )


def solution(mesh):
    in_specs = (
        P(("rep", "dom"), None),
        P(("rep", "dom"), None),
        P("dom", None),
        P("dom", None),
        P(("rep", "dom"), None, None),
        P(("rep", "dom")),
        P(("rep", "dom")),
        P(("rep", "dom")),
    )
    out_specs = (P("dom", None), P("dom", None))
    return jax.shard_map(shards, mesh=mesh, in_specs=in_specs, out_specs=out_specs, check_vma=False)
```

```python
import jax
import jax.numpy as jnp
from jax import lax
from jax.experimental import pallas as pl
from jax.experimental.pallas import tpu as pltpu
from jax.sharding import PartitionSpec as P

F32 = jnp.float32
BF16 = jnp.bfloat16
SCALE = 0.7978845608
CUBIC = 0.044715
MIB = 1 << 20
HBM = pl.BlockSpec(memory_space=pltpu.HBM)
SMEM = pl.BlockSpec(memory_space=pltpu.SMEM)
VMEM = pl.BlockSpec(memory_space=pltpu.VMEM)
DMA = pltpu.SemaphoreType.DMA


def swap(value, axis, step):
    size = lax.axis_size(axis)
    return lax.ppermute(value, axis, [(index, index ^ step) for index in range(size)])


def slots_kernel(
    src_hbm, peer_hbm, tiles_hbm, features_hbm, out_hbm, src, peer, tiles, features, dense, out, in_sems, out_sems
):
    copies = [
        pltpu.make_async_copy(source, target, in_sems.at[index])
        for index, (source, target) in enumerate(
            [(src_hbm, src), (peer_hbm, peer), (tiles_hbm, tiles), (features_hbm, features)]
        )
    ]
    for copy in copies:
        copy.start()
    count, block, _ = tiles.shape
    dense[...] = jnp.zeros_like(dense)
    for copy in copies[:3]:
        copy.wait()

    def place(tile, carry):
        row = pl.multiple_of(peer[tile] * block, block)
        column = pl.multiple_of(src[tile] * block, block)
        at = (pl.ds(row, block), pl.ds(column, block))
        dense[at] = dense[at] + tiles[tile].astype(F32)
        return carry

    lax.fori_loop(0, count, place, 0)
    copies[3].wait()
    chunk = 4 * block
    results = []
    for index in range(out.shape[0] // chunk):
        at = slice(index * chunk, (index + 1) * chunk)
        out[at, :] = jnp.dot(dense[at, :].astype(BF16), features[...], preferred_element_type=F32).astype(BF16)
        results.append(pltpu.make_async_copy(out.at[at, :], out_hbm.at[at, :], out_sems.at[index]))
        results[-1].start()
    for result in results:
        result.wait()


def layer_kernel(
    core_ref,
    into_ref,
    slots_hbm,
    features_hbm,
    turned_hbm,
    cotangent_hbm,
    mine_first_hbm,
    mine_second_hbm,
    other_first_hbm,
    other_second_hbm,
    aggregate_hbm,
    grad_hbm,
    sent_hbm,
    slots,
    features,
    turned,
    cotangent,
    w_self,
    w_neigh,
    summed,
    aggregate,
    grad,
    sent,
    slot_sems,
    weight_sems,
    row_sems,
    out_sems,
):
    senders, block, _ = slots.shape
    rows, width = features.shape
    split = mine_first_hbm.shape[1]
    chunk = 256
    core = core_ref[0]
    arrivals = [
        pltpu.make_async_copy(slots_hbm.at[sender], slots.at[sender], slot_sems.at[sender]) for sender in range(senders)
    ]
    for arrival in arrivals:
        arrival.start()

    def weight_copies(first_hbm, second_hbm, target, index):
        return [
            pltpu.make_async_copy(first_hbm, target.at[:, :split], weight_sems.at[index]),
            pltpu.make_async_copy(second_hbm, target.at[:, split:], weight_sems.at[index + 1]),
        ]

    mine = (mine_first_hbm, mine_second_hbm)
    other = (other_first_hbm, other_second_hbm)

    @pl.when(core == 0)
    def _():
        for copy in weight_copies(*mine, w_self, 0) + weight_copies(*other, w_neigh, 2):
            copy.start()

    @pl.when(core != 0)
    def _():
        for copy in weight_copies(*other, w_self, 0) + weight_copies(*mine, w_neigh, 2):
            copy.start()

    weights = weight_copies(*mine, w_self, 0) + weight_copies(*other, w_neigh, 2)
    spans = [slice(first, first + chunk) for first in range(0, rows, chunk)]
    streams = [
        [
            pltpu.make_async_copy(features_hbm.at[at, :], features.at[at, :], row_sems.at[0, index]),
            pltpu.make_async_copy(cotangent_hbm.at[at, :], cotangent.at[at, :], row_sems.at[1, index]),
        ]
        for index, at in enumerate(spans)
    ]
    for stream in streams:
        for copy in stream:
            copy.start()
    turning = pltpu.make_async_copy(turned_hbm, turned, out_sems.at[0])
    turning.start()

    summed[...] = jnp.zeros_like(summed)
    for sender in range(senders):
        arrivals[sender].wait()
        at = pl.ds(pl.multiple_of(into_ref[sender] * block, block), block)
        summed[at, :] = summed[at, :] + slots[sender].astype(F32)
    aggregate[...] = summed[...].astype(BF16)
    results = [pltpu.make_async_copy(aggregate, aggregate_hbm, out_sems.at[1])]
    results[0].start()
    for copy in weights:
        copy.wait()
    span = 512
    for index, at in enumerate(spans):
        for copy in streams[index]:
            copy.wait()
        for first in range(0, grad.shape[1], span):
            columns = slice(first, first + span)
            value = jnp.dot(features[at, :], w_self[:, columns], preferred_element_type=F32) + jnp.dot(
                aggregate[at, :], w_neigh[:, columns], preferred_element_type=F32
            )
            square = value * value
            bend = jnp.tanh(value * (SCALE + SCALE * CUBIC * square))
            inner = value * (SCALE + 3.0 * SCALE * CUBIC * square)
            slope = (1.0 + bend) * (0.5 + 0.5 * inner * (1.0 - bend))
            grad[at, columns] = (cotangent[at, columns].astype(F32) * slope).astype(BF16)
        results.append(pltpu.make_async_copy(grad.at[at, :], grad_hbm.at[at, :], out_sems.at[2 + index]))
        results[-1].start()
    turning.wait()
    term(1 - core, turned, aggregate, grad, sent, sent_hbm, out_sems, 2 + len(spans))
    for result in results:
        result.wait()


def term(use, turned, aggregate, grad, out, out_hbm, sems, first_sem):
    chunk = 256
    spans = [slice(first, first + chunk) for first in range(0, out.shape[0], chunk)]
    copies = [
        pltpu.make_async_copy(out.at[at, :], out_hbm.at[at, :], sems.at[first_sem + index])
        for index, at in enumerate(spans)
    ]

    @pl.when(use == 0)
    def _():
        for at, copy in zip(spans, copies):
            out[at, :] = jnp.dot(turned[at, :], grad[...], preferred_element_type=F32).astype(BF16)
            copy.start()

    @pl.when(use != 0)
    def _():
        contract = (((0,), (0,)), ((), ()))
        for at, copy in zip(spans, copies):
            out[at, :] = lax.dot_general(
                aggregate[:, at], grad[...], contract, preferred_element_type=F32
            ).astype(BF16)
            copy.start()

    for copy in copies:
        copy.wait()


def kept_kernel(core_ref, turned_hbm, aggregate_hbm, grad_hbm, out_hbm, turned, aggregate, grad, out, in_sems, out_sems):
    grads = pltpu.make_async_copy(grad_hbm, grad, in_sems.at[0])
    grads.start()
    core = core_ref[0]

    @pl.when(core == 0)
    def _():
        copy = pltpu.make_async_copy(turned_hbm, turned, in_sems.at[1])
        copy.start()
        copy.wait()

    @pl.when(core != 0)
    def _():
        copy = pltpu.make_async_copy(aggregate_hbm, aggregate, in_sems.at[1])
        copy.start()
        copy.wait()

    grads.wait()
    term(core, turned, aggregate, grad, out, out_hbm, out_sems, 0)


def call(kernel, outs, places, out_places, scratch=(), flops=0, moved=0, vmem=56):
    return pl.pallas_call(
        kernel,
        out_shape=outs,
        in_specs=places,
        out_specs=out_places,
        scratch_shapes=list(scratch),
        compiler_params=pltpu.CompilerParams(vmem_limit_bytes=vmem * MIB),
        cost_estimate=pl.CostEstimate(flops=flops, bytes_accessed=moved, transcendentals=0),
    )


def joined(held, other, upper, axis):
    return jnp.stack([jnp.where(upper, other, held), jnp.where(upper, held, other)], axis=axis)


def gather_low(held, me):
    held = joined(held, swap(held, "dom", 1), (me & 1) != 0, 1)
    return held.reshape(-1, held.shape[-1])


def gather_high(held, high):
    step = 1
    while step < lax.axis_size("rep") // 2:
        other = swap(held, "rep", 2 * step)
        upper = (high & step) != 0
        held = jnp.concatenate([jnp.where(upper, other, held), jnp.where(upper, held, other)], axis=-1)
        step *= 2
    return held


def added(left, right):
    return (left.astype(F32) + right.astype(F32)).astype(BF16)


def half_of(value, axis, which):
    size = value.shape[axis] // 2
    return lax.dynamic_slice_in_dim(value, which * size, size, axis)


def reduce_high(value, high):
    step = lax.axis_size("rep") // 4
    while step:
        upper = (high // step) % 2
        value = added(half_of(value, 2, upper), swap(half_of(value, 2, 1 - upper), "rep", 2 * step))
        step //= 2
    return value


def reduce_low(value, low):
    value = value.reshape(value.shape[0] // 2, 2, *value.shape[1:])
    sent = lax.dynamic_index_in_dim(value, 1 - low, 1, keepdims=False)
    kept = lax.dynamic_index_in_dim(value, low, 1, keepdims=False)
    return added(kept, swap(sent, "dom", 1))


def shards(features, cotangent, w_self, w_neigh, tile_vals, tile_src, tile_peer, in_block):
    dom_size = lax.axis_size("dom")
    rows, width = features.shape
    hidden = w_self.shape[1]
    block = tile_vals.shape[1]
    me = lax.axis_index("dom")
    rep = lax.axis_index("rep")
    parts = lax.axis_size("rep") // 2
    core, high = rep & 1, rep >> 1
    low, place = me & 1, me >> 1
    core_arg = core.astype(jnp.int32).reshape(1)

    own = jnp.where(core == 0, w_self, w_neigh)
    split = hidden // 4
    share = split // parts
    rest = (hidden - split) // parts
    held = jnp.concatenate(
        [
            lax.dynamic_slice_in_dim(own, high * share, share, 1),
            lax.dynamic_slice_in_dim(own, split + high * rest, rest, 1),
        ],
        axis=1,
    )[None]
    step = dom_size // 2
    other = swap(held, "dom", step)
    slots = call(
        slots_kernel,
        jax.ShapeDtypeStruct((dom_size * block, width), BF16),
        [HBM] * 4,
        HBM,
        [
            pltpu.SMEM(tile_src.shape, jnp.int32),
            pltpu.SMEM(tile_peer.shape, jnp.int32),
            pltpu.VMEM(tile_vals.shape, BF16),
            pltpu.VMEM(features.shape, BF16),
            pltpu.VMEM((dom_size * block, rows), F32),
            pltpu.VMEM((dom_size * block, width), BF16),
            DMA((4,)),
            DMA((dom_size // 4,)),
        ],
        flops=2 * dom_size * block * rows * width,
        moved=tile_vals.size * 2 + rows * width * 4,
    )(tile_src, tile_peer, tile_vals, features)
    received = lax.all_to_all(slots.reshape(dom_size, block, width), "dom", split_axis=0, concat_axis=0, tiled=True)

    other, _ = lax.optimization_barrier((other, slots))
    while step > 1:
        held = joined(held, other, (me & step) != 0, 1).reshape(-1, *held.shape[1:])
        step //= 2
        if step > 1:
            other = swap(held, "dom", step)
    weights = [
        gather_high(gather_low(held[..., :share], me), high),
        gather_low(gather_high(held[..., share:], high), me),
    ]
    weights += [swap(weight, "rep", 1) for weight in weights]
    turned = features.T

    aggregate, grad, sent = call(
        layer_kernel,
        [
            jax.ShapeDtypeStruct((rows, width), BF16),
            jax.ShapeDtypeStruct((rows, hidden), BF16),
            jax.ShapeDtypeStruct((width, hidden), BF16),
        ],
        [SMEM, SMEM] + [HBM] * 8,
        [HBM] * 3,
        [
            pltpu.VMEM((dom_size, block, width), BF16),
            pltpu.VMEM((rows, width), BF16),
            pltpu.VMEM((width, rows), BF16),
            pltpu.VMEM((rows, hidden), BF16),
            pltpu.VMEM((width, hidden), BF16),
            pltpu.VMEM((width, hidden), BF16),
            pltpu.VMEM((rows, width), F32),
            pltpu.VMEM((rows, width), BF16),
            pltpu.VMEM((rows, hidden), BF16),
            pltpu.VMEM((width, hidden), BF16),
            DMA((dom_size,)),
            DMA((4,)),
            DMA((2, rows // 256)),
            DMA((2 + rows // 256 + width // 256,)),
        ],
        flops=6 * rows * width * hidden,
        moved=16 * rows * hidden,
    )(core_arg, in_block, received, features, turned, cotangent, *weights)
    other = swap(sent, "rep", 1)
    kept = call(
        kept_kernel,
        jax.ShapeDtypeStruct((width, hidden), BF16),
        [SMEM] + [HBM] * 3,
        HBM,
        [
            pltpu.VMEM((width, rows), BF16),
            pltpu.VMEM((rows, width), BF16),
            pltpu.VMEM((rows, hidden), BF16),
            pltpu.VMEM((width, hidden), BF16),
            DMA((2,)),
            DMA((width // 256,)),
        ],
        flops=2 * rows * width * hidden,
        moved=6 * rows * hidden,
        vmem=16,
    )(core_arg, turned, aggregate, grad)
    chip = added(kept, other).reshape(dom_size, width // dom_size, hidden)
    first, second = chip[:, :, : hidden // 2], chip[:, :, hidden // 2 :]
    first, second = reduce_low(first, low), reduce_high(second, high)
    first, second = reduce_high(first, high), reduce_low(second, low)
    both = jnp.concatenate([first, second], axis=2)
    summed = lax.dynamic_index_in_dim(both, place, 0, keepdims=False).astype(F32)
    for step in range(1, dom_size // 2):
        piece = lax.dynamic_index_in_dim(both, place ^ step, 0, keepdims=False)
        summed = summed + swap(piece, "dom", 2 * step).astype(F32)
    summed = summed.astype(BF16)
    size = summed.shape[1] // 2
    held = gather_high(jnp.stack([summed[:, :size], summed[:, size:]]), high)
    whole = jnp.concatenate([held[0], held[1]], axis=1)
    opposite = swap(whole, "rep", 1)
    return (
        jnp.where(core == 0, whole, opposite).astype(F32),
        jnp.where(core == 0, opposite, whole).astype(F32),
    )


def solution(mesh):
    in_specs = (
        P(("rep", "dom"), None),
        P(("rep", "dom"), None),
        P("dom", None),
        P("dom", None),
        P(("rep", "dom"), None, None),
        P(("rep", "dom")),
        P(("rep", "dom")),
        P(("rep", "dom")),
    )
    out_specs = (P("dom", None), P("dom", None))
    return jax.shard_map(shards, mesh=mesh, in_specs=in_specs, out_specs=out_specs, check_vma=False)
```

```python
import jax
import jax.numpy as jnp
from jax import lax
from jax.experimental import pallas as pl
from jax.experimental.pallas import tpu as pltpu
from jax.sharding import PartitionSpec as P

F32 = jnp.float32
BF16 = jnp.bfloat16
SCALE = 0.7978845608
CUBIC = 0.044715
MIB = 1 << 20
HBM = pl.BlockSpec(memory_space=pltpu.HBM)
SMEM = pl.BlockSpec(memory_space=pltpu.SMEM)
VMEM = pl.BlockSpec(memory_space=pltpu.VMEM)
DMA = pltpu.SemaphoreType.DMA


def swap(value, axis, step):
    size = lax.axis_size(axis)
    return lax.ppermute(value, axis, [(index, index ^ step) for index in range(size)])


def slots_kernel(
    src_hbm, peer_hbm, tiles_hbm, features_hbm, out_hbm, src, peer, tiles, features, dense, out, in_sems, out_sems
):
    copies = [
        pltpu.make_async_copy(source, target, in_sems.at[index])
        for index, (source, target) in enumerate(
            [(src_hbm, src), (peer_hbm, peer), (tiles_hbm, tiles), (features_hbm, features)]
        )
    ]
    for copy in copies:
        copy.start()
    count, block, _ = tiles.shape
    dense[...] = jnp.zeros_like(dense)
    for copy in copies[:3]:
        copy.wait()

    def place(tile, carry):
        row = pl.multiple_of(peer[tile] * block, block)
        column = pl.multiple_of(src[tile] * block, block)
        at = (pl.ds(row, block), pl.ds(column, block))
        dense[at] = dense[at] + tiles[tile].astype(F32)
        return carry

    lax.fori_loop(0, count, place, 0)
    copies[3].wait()
    chunk = 4 * block
    results = []
    for index in range(out.shape[0] // chunk):
        at = slice(index * chunk, (index + 1) * chunk)
        out[at, :] = jnp.dot(dense[at, :].astype(BF16), features[...], preferred_element_type=F32).astype(BF16)
        results.append(pltpu.make_async_copy(out.at[at, :], out_hbm.at[at, :], out_sems.at[index]))
        results[-1].start()
    for result in results:
        result.wait()


def self_kernel(core_ref, features_hbm, mine_hbm, other_hbm, out_hbm, features, weights, out, in_sems, out_sems):
    rows = features.shape[0]
    chunk = 256
    core = core_ref[0]
    copies = [
        pltpu.make_async_copy(mine_hbm, weights, in_sems.at[0]),
        pltpu.make_async_copy(features_hbm, features, in_sems.at[1]),
    ]
    pl.when(core == 0)(copies[0].start)
    pl.when(core != 0)(pltpu.make_async_copy(other_hbm, weights, in_sems.at[0]).start)
    copies[1].start()
    for copy in copies:
        copy.wait()
    results = []
    for index in range(rows // chunk):
        at = slice(index * chunk, (index + 1) * chunk)
        out[at, :] = jnp.dot(features[at, :], weights[...], preferred_element_type=F32)
        results.append(pltpu.make_async_copy(out.at[at, :], out_hbm.at[at, :], out_sems.at[index]))
        results[-1].start()
    for result in results:
        result.wait()


def layer_kernel(
    core_ref,
    into_ref,
    slots_hbm,
    total_hbm,
    turned_hbm,
    cotangent_hbm,
    mine_hbm,
    other_hbm,
    aggregate_hbm,
    grad_hbm,
    sent_hbm,
    slots,
    total,
    turned,
    cotangent,
    w_neigh,
    summed,
    aggregate,
    grad,
    sent,
    slot_sems,
    weight_sem,
    row_sems,
    out_sems,
):
    senders, block, _ = slots.shape
    rows = total.shape[0]
    chunk = 256
    core = core_ref[0]
    arrivals = [
        pltpu.make_async_copy(slots_hbm.at[sender], slots.at[sender], slot_sems.at[sender]) for sender in range(senders)
    ]
    for arrival in arrivals:
        arrival.start()
    weights = pltpu.make_async_copy(other_hbm, w_neigh, weight_sem.at[0])
    pl.when(core == 0)(weights.start)
    pl.when(core != 0)(pltpu.make_async_copy(mine_hbm, w_neigh, weight_sem.at[0]).start)
    spans = [slice(first, first + chunk) for first in range(0, rows, chunk)]
    streams = [
        [
            pltpu.make_async_copy(total_hbm.at[at, :], total.at[at, :], row_sems.at[0, index]),
            pltpu.make_async_copy(cotangent_hbm.at[at, :], cotangent.at[at, :], row_sems.at[1, index]),
        ]
        for index, at in enumerate(spans)
    ]
    for stream in streams:
        for copy in stream:
            copy.start()
    turning = pltpu.make_async_copy(turned_hbm, turned, out_sems.at[0])
    turning.start()

    summed[...] = jnp.zeros_like(summed)
    for sender in range(senders):
        arrivals[sender].wait()
        at = pl.ds(pl.multiple_of(into_ref[sender] * block, block), block)
        summed[at, :] = summed[at, :] + slots[sender].astype(F32)
    aggregate[...] = summed[...].astype(BF16)
    results = [pltpu.make_async_copy(aggregate, aggregate_hbm, out_sems.at[1])]
    results[0].start()
    weights.wait()
    span = 512
    for index, at in enumerate(spans):
        for copy in streams[index]:
            copy.wait()
        for first in range(0, grad.shape[1], span):
            columns = slice(first, first + span)
            value = total[at, columns] + jnp.dot(
                aggregate[at, :], w_neigh[:, columns], preferred_element_type=F32
            )
            square = value * value
            bend = jnp.tanh(value * (SCALE + SCALE * CUBIC * square))
            inner = value * (SCALE + 3.0 * SCALE * CUBIC * square)
            slope = (1.0 + bend) * (0.5 + 0.5 * inner * (1.0 - bend))
            grad[at, columns] = (cotangent[at, columns].astype(F32) * slope).astype(BF16)
        results.append(pltpu.make_async_copy(grad.at[at, :], grad_hbm.at[at, :], out_sems.at[2 + index]))
        results[-1].start()
    turning.wait()
    term(1 - core, turned, aggregate, grad, sent, sent_hbm, out_sems, 2 + len(spans))
    for result in results:
        result.wait()


def term(use, turned, aggregate, grad, out, out_hbm, sems, first_sem):
    chunk = 256
    spans = [slice(first, first + chunk) for first in range(0, out.shape[0], chunk)]
    copies = [
        pltpu.make_async_copy(out.at[at, :], out_hbm.at[at, :], sems.at[first_sem + index])
        for index, at in enumerate(spans)
    ]

    @pl.when(use == 0)
    def _():
        for at, copy in zip(spans, copies):
            out[at, :] = jnp.dot(turned[at, :], grad[...], preferred_element_type=F32).astype(BF16)
            copy.start()

    @pl.when(use != 0)
    def _():
        contract = (((0,), (0,)), ((), ()))
        for at, copy in zip(spans, copies):
            out[at, :] = lax.dot_general(
                aggregate[:, at], grad[...], contract, preferred_element_type=F32
            ).astype(BF16)
            copy.start()

    for copy in copies:
        copy.wait()


def kept_kernel(core_ref, turned_hbm, aggregate_hbm, grad_hbm, out_hbm, turned, aggregate, grad, out, in_sems, out_sems):
    grads = pltpu.make_async_copy(grad_hbm, grad, in_sems.at[0])
    grads.start()
    core = core_ref[0]

    @pl.when(core == 0)
    def _():
        copy = pltpu.make_async_copy(turned_hbm, turned, in_sems.at[1])
        copy.start()
        copy.wait()

    @pl.when(core != 0)
    def _():
        copy = pltpu.make_async_copy(aggregate_hbm, aggregate, in_sems.at[1])
        copy.start()
        copy.wait()

    grads.wait()
    term(core, turned, aggregate, grad, out, out_hbm, out_sems, 0)


def call(kernel, outs, places, out_places, scratch=(), flops=0, moved=0, vmem=56):
    return pl.pallas_call(
        kernel,
        out_shape=outs,
        in_specs=places,
        out_specs=out_places,
        scratch_shapes=list(scratch),
        compiler_params=pltpu.CompilerParams(vmem_limit_bytes=vmem * MIB),
        cost_estimate=pl.CostEstimate(flops=flops, bytes_accessed=moved, transcendentals=0),
    )


def joined(held, other, upper, axis):
    return jnp.stack([jnp.where(upper, other, held), jnp.where(upper, held, other)], axis=axis)


def gather_low(held, me):
    held = joined(held, swap(held, "dom", 1), (me & 1) != 0, 1)
    return held.reshape(-1, held.shape[-1])


def gather_high(held, high):
    step = 1
    while step < lax.axis_size("rep") // 2:
        other = swap(held, "rep", 2 * step)
        upper = (high & step) != 0
        held = jnp.concatenate([jnp.where(upper, other, held), jnp.where(upper, held, other)], axis=-1)
        step *= 2
    return held


def added(left, right):
    return (left.astype(F32) + right.astype(F32)).astype(BF16)


def half_of(value, axis, which):
    size = value.shape[axis] // 2
    return lax.dynamic_slice_in_dim(value, which * size, size, axis)


def reduce_high(value, high):
    step = lax.axis_size("rep") // 4
    while step:
        upper = (high // step) % 2
        value = added(half_of(value, 2, upper), swap(half_of(value, 2, 1 - upper), "rep", 2 * step))
        step //= 2
    return value


def reduce_low(value, low):
    value = value.reshape(value.shape[0] // 2, 2, *value.shape[1:])
    sent = lax.dynamic_index_in_dim(value, 1 - low, 1, keepdims=False)
    kept = lax.dynamic_index_in_dim(value, low, 1, keepdims=False)
    return added(kept, swap(sent, "dom", 1))


def shards(features, cotangent, w_self, w_neigh, tile_vals, tile_src, tile_peer, in_block):
    dom_size = lax.axis_size("dom")
    rows, width = features.shape
    hidden = w_self.shape[1]
    block = tile_vals.shape[1]
    me = lax.axis_index("dom")
    rep = lax.axis_index("rep")
    parts = lax.axis_size("rep") // 2
    core, high = rep & 1, rep >> 1
    low, place = me & 1, me >> 1
    core_arg = core.astype(jnp.int32).reshape(1)

    own = jnp.where(core == 0, w_self, w_neigh)
    held = lax.dynamic_slice_in_dim(own, high * (hidden // parts), hidden // parts, 1)
    pieces = [held] + [swap(held, "dom", 2 * step) for step in range(1, dom_size // 2)]
    slots = call(
        slots_kernel,
        jax.ShapeDtypeStruct((dom_size * block, width), BF16),
        [HBM] * 4,
        HBM,
        [
            pltpu.SMEM(tile_src.shape, jnp.int32),
            pltpu.SMEM(tile_peer.shape, jnp.int32),
            pltpu.VMEM(tile_vals.shape, BF16),
            pltpu.VMEM(features.shape, BF16),
            pltpu.VMEM((dom_size * block, rows), F32),
            pltpu.VMEM((dom_size * block, width), BF16),
            DMA((4,)),
            DMA((dom_size // 4,)),
        ],
        flops=2 * dom_size * block * rows * width,
        moved=tile_vals.size * 2 + rows * width * 4,
    )(tile_src, tile_peer, tile_vals, features)
    *pieces, slots = lax.optimization_barrier((*pieces, slots))
    received = lax.all_to_all(slots.reshape(dom_size, block, width), "dom", split_axis=0, concat_axis=0, tiled=True)
    bit = 1
    while len(pieces) > 1:
        upper = (place & bit) != 0
        pieces = [joined(pieces[at], pieces[at + 1], upper, 0) for at in range(0, len(pieces), 2)]
        pieces = [piece.reshape(-1, *held.shape) for piece in pieces]
        bit *= 2
    mine = gather_high(gather_low(pieces[0], me), high)
    other = swap(mine, "rep", 1)
    total = call(
        self_kernel,
        jax.ShapeDtypeStruct((rows, hidden), F32),
        [SMEM] + [HBM] * 3,
        HBM,
        [
            pltpu.VMEM((rows, width), BF16),
            pltpu.VMEM((width, hidden), BF16),
            pltpu.VMEM((rows, hidden), F32),
            DMA((2,)),
            DMA((rows // 256,)),
        ],
        flops=2 * rows * width * hidden,
        moved=8 * rows * hidden,
    )(core_arg, features, mine, other)
    turned = features.T

    aggregate, grad, sent = call(
        layer_kernel,
        [
            jax.ShapeDtypeStruct((rows, width), BF16),
            jax.ShapeDtypeStruct((rows, hidden), BF16),
            jax.ShapeDtypeStruct((width, hidden), BF16),
        ],
        [SMEM, SMEM] + [HBM] * 6,
        [HBM] * 3,
        [
            pltpu.VMEM((dom_size, block, width), BF16),
            pltpu.VMEM((rows, hidden), F32),
            pltpu.VMEM((width, rows), BF16),
            pltpu.VMEM((rows, hidden), BF16),
            pltpu.VMEM((width, hidden), BF16),
            pltpu.VMEM((rows, width), F32),
            pltpu.VMEM((rows, width), BF16),
            pltpu.VMEM((rows, hidden), BF16),
            pltpu.VMEM((width, hidden), BF16),
            DMA((dom_size,)),
            DMA((1,)),
            DMA((2, rows // 256)),
            DMA((2 + rows // 256 + width // 256,)),
        ],
        flops=6 * rows * width * hidden,
        moved=16 * rows * hidden,
    )(core_arg, in_block, received, total, turned, cotangent, mine, other)
    arrived = swap(sent, "rep", 1)
    kept = call(
        kept_kernel,
        jax.ShapeDtypeStruct((width, hidden), BF16),
        [SMEM] + [HBM] * 3,
        HBM,
        [
            pltpu.VMEM((width, rows), BF16),
            pltpu.VMEM((rows, width), BF16),
            pltpu.VMEM((rows, hidden), BF16),
            pltpu.VMEM((width, hidden), BF16),
            DMA((2,)),
            DMA((width // 256,)),
        ],
        flops=2 * rows * width * hidden,
        moved=6 * rows * hidden,
    )(core_arg, turned, aggregate, grad)
    chip = added(kept, arrived).reshape(dom_size, width // dom_size, hidden)
    first, second = chip[:, :, : hidden // 2], chip[:, :, hidden // 2 :]
    first, second = reduce_low(first, low), reduce_high(second, high)
    first, second = reduce_high(first, high), reduce_low(second, low)
    both = jnp.concatenate([first, second], axis=2)
    summed = lax.dynamic_index_in_dim(both, place, 0, keepdims=False).astype(F32)
    for step in range(1, dom_size // 2):
        piece = lax.dynamic_index_in_dim(both, place ^ step, 0, keepdims=False)
        summed = summed + swap(piece, "dom", 2 * step).astype(F32)
    summed = summed.astype(BF16)
    size = summed.shape[1] // 2
    held = gather_high(jnp.stack([summed[:, :size], summed[:, size:]]), high)
    whole = jnp.concatenate([held[0], held[1]], axis=1)
    opposite = swap(whole, "rep", 1)
    return (
        jnp.where(core == 0, whole, opposite).astype(F32),
        jnp.where(core == 0, opposite, whole).astype(F32),
    )


def solution(mesh):
    in_specs = (
        P(("rep", "dom"), None),
        P(("rep", "dom"), None),
        P("dom", None),
        P("dom", None),
        P(("rep", "dom"), None, None),
        P(("rep", "dom")),
        P(("rep", "dom")),
        P(("rep", "dom")),
    )
    out_specs = (P("dom", None), P("dom", None))
    return jax.shard_map(shards, mesh=mesh, in_specs=in_specs, out_specs=out_specs, check_vma=False)
```

```python
import jax
import jax.numpy as jnp
from jax import lax
from jax.experimental import pallas as pl
from jax.experimental.pallas import tpu as pltpu
from jax.sharding import PartitionSpec as P

F32 = jnp.float32
BF16 = jnp.bfloat16
SCALE = 0.7978845608
CUBIC = 0.044715
MIB = 1 << 20
HBM = pl.BlockSpec(memory_space=pltpu.HBM)
SMEM = pl.BlockSpec(memory_space=pltpu.SMEM)
VMEM = pl.BlockSpec(memory_space=pltpu.VMEM)
DMA = pltpu.SemaphoreType.DMA


def swap(value, axis, step):
    size = lax.axis_size(axis)
    return lax.ppermute(value, axis, [(index, index ^ step) for index in range(size)])


def slots_kernel(
    src_hbm, peer_hbm, tiles_hbm, features_hbm, out_hbm, src, peer, tiles, features, dense, out, in_sems, out_sems
):
    copies = [
        pltpu.make_async_copy(source, target, in_sems.at[index])
        for index, (source, target) in enumerate(
            [(src_hbm, src), (peer_hbm, peer), (tiles_hbm, tiles), (features_hbm, features)]
        )
    ]
    for copy in copies:
        copy.start()
    count, block, _ = tiles.shape
    dense[...] = jnp.zeros_like(dense)
    for copy in copies[:3]:
        copy.wait()

    def place(tile, carry):
        row = pl.multiple_of(peer[tile] * block, block)
        column = pl.multiple_of(src[tile] * block, block)
        at = (pl.ds(row, block), pl.ds(column, block))
        dense[at] = dense[at] + tiles[tile].astype(F32)
        return carry

    lax.fori_loop(0, count, place, 0)
    copies[3].wait()
    chunk = 4 * block
    results = []
    for index in range(out.shape[0] // chunk):
        at = slice(index * chunk, (index + 1) * chunk)
        out[at, :] = jnp.dot(dense[at, :].astype(BF16), features[...], preferred_element_type=F32).astype(BF16)
        results.append(pltpu.make_async_copy(out.at[at, :], out_hbm.at[at, :], out_sems.at[index]))
        results[-1].start()
    for result in results:
        result.wait()


def layer_kernel(
    core_ref,
    into_ref,
    slots_hbm,
    features_hbm,
    turned_hbm,
    cotangent_hbm,
    mine_first_hbm,
    mine_second_hbm,
    other_first_hbm,
    other_second_hbm,
    aggregate_hbm,
    grad_hbm,
    sent_hbm,
    slots,
    features,
    turned,
    cotangent,
    w_self,
    w_neigh,
    summed,
    aggregate,
    grad,
    sent,
    slot_sems,
    weight_sems,
    row_sems,
    out_sems,
):
    senders, block, _ = slots.shape
    rows, width = features.shape
    split = mine_first_hbm.shape[1]
    chunk = 256
    core = core_ref[0]
    arrivals = [
        pltpu.make_async_copy(slots_hbm.at[sender], slots.at[sender], slot_sems.at[sender]) for sender in range(senders)
    ]
    for arrival in arrivals:
        arrival.start()

    def weight_copies(first_hbm, second_hbm, target, index):
        return [
            pltpu.make_async_copy(first_hbm, target.at[:, :split], weight_sems.at[index]),
            pltpu.make_async_copy(second_hbm, target.at[:, split:], weight_sems.at[index + 1]),
        ]

    mine = (mine_first_hbm, mine_second_hbm)
    other = (other_first_hbm, other_second_hbm)

    @pl.when(core == 0)
    def _():
        for copy in weight_copies(*mine, w_self, 0) + weight_copies(*other, w_neigh, 2):
            copy.start()

    @pl.when(core != 0)
    def _():
        for copy in weight_copies(*other, w_self, 0) + weight_copies(*mine, w_neigh, 2):
            copy.start()

    weights = weight_copies(*mine, w_self, 0) + weight_copies(*other, w_neigh, 2)
    spans = [slice(first, first + chunk) for first in range(0, rows, chunk)]
    streams = [
        [
            pltpu.make_async_copy(features_hbm.at[at, :], features.at[at, :], row_sems.at[0, index]),
            pltpu.make_async_copy(cotangent_hbm.at[at, :], cotangent.at[at, :], row_sems.at[1, index]),
        ]
        for index, at in enumerate(spans)
    ]
    for stream in streams:
        for copy in stream:
            copy.start()
    turning = pltpu.make_async_copy(turned_hbm, turned, out_sems.at[0])
    turning.start()

    summed[...] = jnp.zeros_like(summed)
    for sender in range(senders):
        arrivals[sender].wait()
        at = pl.ds(pl.multiple_of(into_ref[sender] * block, block), block)
        summed[at, :] = summed[at, :] + slots[sender].astype(F32)
    aggregate[...] = summed[...].astype(BF16)
    results = [pltpu.make_async_copy(aggregate, aggregate_hbm, out_sems.at[1])]
    results[0].start()
    for copy in weights:
        copy.wait()
    span = 512
    for index, at in enumerate(spans):
        for copy in streams[index]:
            copy.wait()
        for first in range(0, grad.shape[1], span):
            columns = slice(first, first + span)
            value = jnp.dot(features[at, :], w_self[:, columns], preferred_element_type=F32) + jnp.dot(
                aggregate[at, :], w_neigh[:, columns], preferred_element_type=F32
            )
            square = value * value
            bend = jnp.tanh(value * (SCALE + SCALE * CUBIC * square))
            inner = value * (SCALE + 3.0 * SCALE * CUBIC * square)
            slope = (1.0 + bend) * (0.5 + 0.5 * inner * (1.0 - bend))
            grad[at, columns] = (cotangent[at, columns].astype(F32) * slope).astype(BF16)
        results.append(pltpu.make_async_copy(grad.at[at, :], grad_hbm.at[at, :], out_sems.at[2 + index]))
        results[-1].start()
    turning.wait()
    term(1 - core, turned, aggregate, grad, sent, sent_hbm, out_sems, 2 + len(spans))
    for result in results:
        result.wait()


def term(use, turned, aggregate, grad, out, out_hbm, sems, first_sem):
    chunk = 256
    spans = [slice(first, first + chunk) for first in range(0, out.shape[0], chunk)]
    copies = [
        pltpu.make_async_copy(out.at[at, :], out_hbm.at[at, :], sems.at[first_sem + index])
        for index, at in enumerate(spans)
    ]

    @pl.when(use == 0)
    def _():
        for at, copy in zip(spans, copies):
            out[at, :] = jnp.dot(turned[at, :], grad[...], preferred_element_type=F32).astype(BF16)
            copy.start()

    @pl.when(use != 0)
    def _():
        contract = (((0,), (0,)), ((), ()))
        for at, copy in zip(spans, copies):
            out[at, :] = lax.dot_general(
                aggregate[:, at], grad[...], contract, preferred_element_type=F32
            ).astype(BF16)
            copy.start()

    for copy in copies:
        copy.wait()


def kept_kernel(core_ref, turned_hbm, aggregate_hbm, grad_hbm, out_hbm, turned, aggregate, grad, out, in_sems, out_sems):
    grads = pltpu.make_async_copy(grad_hbm, grad, in_sems.at[0])
    grads.start()
    core = core_ref[0]

    @pl.when(core == 0)
    def _():
        copy = pltpu.make_async_copy(turned_hbm, turned, in_sems.at[1])
        copy.start()
        copy.wait()

    @pl.when(core != 0)
    def _():
        copy = pltpu.make_async_copy(aggregate_hbm, aggregate, in_sems.at[1])
        copy.start()
        copy.wait()

    grads.wait()
    term(core, turned, aggregate, grad, out, out_hbm, out_sems, 0)


def call(kernel, outs, places, out_places, scratch=(), flops=0, moved=0, vmem=56):
    return pl.pallas_call(
        kernel,
        out_shape=outs,
        in_specs=places,
        out_specs=out_places,
        scratch_shapes=list(scratch),
        compiler_params=pltpu.CompilerParams(vmem_limit_bytes=vmem * MIB),
        cost_estimate=pl.CostEstimate(flops=flops, bytes_accessed=moved, transcendentals=0),
    )


def joined(held, other, upper, axis):
    return jnp.stack([jnp.where(upper, other, held), jnp.where(upper, held, other)], axis=axis)


def gather_high(held, high):
    step = 1
    while step < lax.axis_size("rep") // 2:
        other = swap(held, "rep", 2 * step)
        upper = (high & step) != 0
        held = jnp.concatenate([jnp.where(upper, other, held), jnp.where(upper, held, other)], axis=-1)
        step *= 2
    return held


def added(left, right):
    return (left.astype(F32) + right.astype(F32)).astype(BF16)


def half_of(value, axis, which):
    size = value.shape[axis] // 2
    return lax.dynamic_slice_in_dim(value, which * size, size, axis)


def reduce_high(value, high):
    step = lax.axis_size("rep") // 4
    while step:
        upper = (high // step) % 2
        value = added(half_of(value, 2, upper), swap(half_of(value, 2, 1 - upper), "rep", 2 * step))
        step //= 2
    return value


def reduce_low(value, low):
    value = value.reshape(value.shape[0] // 2, 2, *value.shape[1:])
    sent = lax.dynamic_index_in_dim(value, 1 - low, 1, keepdims=False)
    kept = lax.dynamic_index_in_dim(value, low, 1, keepdims=False)
    return added(kept, swap(sent, "dom", 1))


def shards(features, cotangent, w_self, w_neigh, tile_vals, tile_src, tile_peer, in_block):
    dom_size = lax.axis_size("dom")
    rows, width = features.shape
    hidden = w_self.shape[1]
    block = tile_vals.shape[1]
    me = lax.axis_index("dom")
    rep = lax.axis_index("rep")
    parts = lax.axis_size("rep") // 2
    core, high = rep & 1, rep >> 1
    low, place = me & 1, me >> 1
    core_arg = core.astype(jnp.int32).reshape(1)

    share = hidden // parts
    own = jnp.where(core == 0, w_self, w_neigh)
    held = lax.dynamic_slice_in_dim(own, high * share, share, 1)
    top = dom_size // 2
    pieces = [held] + [swap(held, "dom", step) for step in (1, top, top + 1)]
    slots = call(
        slots_kernel,
        jax.ShapeDtypeStruct((dom_size * block, width), BF16),
        [HBM] * 4,
        HBM,
        [
            pltpu.SMEM(tile_src.shape, jnp.int32),
            pltpu.SMEM(tile_peer.shape, jnp.int32),
            pltpu.VMEM(tile_vals.shape, BF16),
            pltpu.VMEM(features.shape, BF16),
            pltpu.VMEM((dom_size * block, rows), F32),
            pltpu.VMEM((dom_size * block, width), BF16),
            DMA((4,)),
            DMA((dom_size // 4,)),
        ],
        flops=2 * dom_size * block * rows * width,
        moved=tile_vals.size * 2 + rows * width * 4,
    )(tile_src, tile_peer, tile_vals, features)
    *pieces, _ = lax.optimization_barrier((*pieces, slots))
    received = lax.all_to_all(slots.reshape(dom_size, block, width), "dom", split_axis=0, concat_axis=0, tiled=True)
    pairs = [joined(pieces[at], pieces[at + 1], low != 0, 0) for at in (0, 2)]
    held = joined(*pairs, (me & top) != 0, 0)
    step = top // 2
    while step > 1:
        held = joined(held, swap(held, "dom", step), (me & step) != 0, 1)
        held = held.reshape(-1, *held.shape[2:])
        step //= 2
    held = held.reshape(-1, share)
    mine = gather_high(held, high)
    weights = [mine[:, : hidden // 2], mine[:, hidden // 2 :]]
    weights += [swap(weight, "rep", 1) for weight in weights]
    turned = features.T

    aggregate, grad, sent = call(
        layer_kernel,
        [
            jax.ShapeDtypeStruct((rows, width), BF16),
            jax.ShapeDtypeStruct((rows, hidden), BF16),
            jax.ShapeDtypeStruct((width, hidden), BF16),
        ],
        [SMEM, SMEM] + [HBM] * 8,
        [HBM] * 3,
        [
            pltpu.VMEM((dom_size, block, width), BF16),
            pltpu.VMEM((rows, width), BF16),
            pltpu.VMEM((width, rows), BF16),
            pltpu.VMEM((rows, hidden), BF16),
            pltpu.VMEM((width, hidden), BF16),
            pltpu.VMEM((width, hidden), BF16),
            pltpu.VMEM((rows, width), F32),
            pltpu.VMEM((rows, width), BF16),
            pltpu.VMEM((rows, hidden), BF16),
            pltpu.VMEM((width, hidden), BF16),
            DMA((dom_size,)),
            DMA((4,)),
            DMA((2, rows // 256)),
            DMA((2 + rows // 256 + width // 256,)),
        ],
        flops=6 * rows * width * hidden,
        moved=16 * rows * hidden,
    )(core_arg, in_block, received, features, turned, cotangent, *weights)
    arrived = swap(sent, "rep", 1)
    kept = call(
        kept_kernel,
        jax.ShapeDtypeStruct((width, hidden), BF16),
        [SMEM] + [HBM] * 3,
        HBM,
        [
            pltpu.VMEM((width, rows), BF16),
            pltpu.VMEM((rows, width), BF16),
            pltpu.VMEM((rows, hidden), BF16),
            pltpu.VMEM((width, hidden), BF16),
            DMA((2,)),
            DMA((width // 256,)),
        ],
        flops=2 * rows * width * hidden,
        moved=6 * rows * hidden,
    )(core_arg, turned, aggregate, grad)
    chip = added(kept, arrived).reshape(dom_size, width // dom_size, hidden)
    first, second = chip[:, :, : hidden // 2], chip[:, :, hidden // 2 :]
    first, second = reduce_low(first, low), reduce_high(second, high)
    first, second = reduce_high(first, high), reduce_low(second, low)
    both = jnp.concatenate([first, second], axis=2)
    summed = lax.dynamic_index_in_dim(both, place, 0, keepdims=False).astype(F32)
    for step in range(1, dom_size // 2):
        piece = lax.dynamic_index_in_dim(both, place ^ step, 0, keepdims=False)
        summed = summed + swap(piece, "dom", 2 * step).astype(F32)
    summed = summed.astype(BF16)
    size = summed.shape[1] // 2
    held = gather_high(jnp.stack([summed[:, :size], summed[:, size:]]), high)
    whole = jnp.concatenate([held[0], held[1]], axis=1)
    opposite = swap(whole, "rep", 1)
    return (
        jnp.where(core == 0, whole, opposite).astype(F32),
        jnp.where(core == 0, opposite, whole).astype(F32),
    )


def solution(mesh):
    in_specs = (
        P(("rep", "dom"), None),
        P(("rep", "dom"), None),
        P("dom", None),
        P("dom", None),
        P(("rep", "dom"), None, None),
        P(("rep", "dom")),
        P(("rep", "dom")),
        P(("rep", "dom")),
    )
    out_specs = (P("dom", None), P("dom", None))
    return jax.shard_map(shards, mesh=mesh, in_specs=in_specs, out_specs=out_specs, check_vma=False)
```

```python
import jax
import jax.numpy as jnp
from jax import lax
from jax.experimental import pallas as pl
from jax.experimental.pallas import tpu as pltpu
from jax.sharding import PartitionSpec as P

F32 = jnp.float32
BF16 = jnp.bfloat16
SCALE = 0.7978845608
CUBIC = 0.044715
MIB = 1 << 20
HBM = pl.BlockSpec(memory_space=pltpu.HBM)
SMEM = pl.BlockSpec(memory_space=pltpu.SMEM)
VMEM = pl.BlockSpec(memory_space=pltpu.VMEM)
DMA = pltpu.SemaphoreType.DMA


def swap(value, axis, step):
    size = lax.axis_size(axis)
    return lax.ppermute(value, axis, [(index, index ^ step) for index in range(size)])


def cross(value, step):
    reps, doms = lax.axis_size("rep"), lax.axis_size("dom")
    pairs = [
        (rep * doms + dom, rep * doms + (dom ^ step ^ (rep & 1))) for rep in range(reps) for dom in range(doms)
    ]
    return lax.ppermute(value, ("rep", "dom"), [(source, target) for source, target in pairs if source != target])


def slots_kernel(
    src_hbm, peer_hbm, tiles_hbm, features_hbm, out_hbm, src, peer, tiles, features, dense, out, in_sems, out_sems
):
    copies = [
        pltpu.make_async_copy(source, target, in_sems.at[index])
        for index, (source, target) in enumerate(
            [(src_hbm, src), (peer_hbm, peer), (tiles_hbm, tiles), (features_hbm, features)]
        )
    ]
    for copy in copies:
        copy.start()
    count, block, _ = tiles.shape
    dense[...] = jnp.zeros_like(dense)
    for copy in copies[:3]:
        copy.wait()

    def place(tile, carry):
        row = pl.multiple_of(peer[tile] * block, block)
        column = pl.multiple_of(src[tile] * block, block)
        at = (pl.ds(row, block), pl.ds(column, block))
        dense[at] = dense[at] + tiles[tile].astype(F32)
        return carry

    lax.fori_loop(0, count, place, 0)
    copies[3].wait()
    chunk = 4 * block
    results = []
    for index in range(out.shape[0] // chunk):
        at = slice(index * chunk, (index + 1) * chunk)
        out[at, :] = jnp.dot(dense[at, :].astype(BF16), features[...], preferred_element_type=F32).astype(BF16)
        results.append(pltpu.make_async_copy(out.at[at, :], out_hbm.at[at, :], out_sems.at[index]))
        results[-1].start()
    for result in results:
        result.wait()


def layer_kernel(
    core_ref,
    into_ref,
    slots_hbm,
    features_hbm,
    turned_hbm,
    cotangent_hbm,
    weights_hbm,
    aggregate_hbm,
    grad_hbm,
    sent_hbm,
    slots,
    features,
    left,
    cotangent,
    weights,
    summed,
    aggregate,
    grad,
    sent,
    slot_sems,
    row_sems,
    column_sems,
    out_sems,
):
    senders, block, _ = slots.shape
    hidden = grad.shape[1]
    core = core_ref[0]
    arrivals = [
        pltpu.make_async_copy(slots_hbm.at[sender], slots.at[sender], slot_sems.at[sender]) for sender in range(senders)
    ]
    for arrival in arrivals:
        arrival.start()
    inputs = pltpu.make_async_copy(features_hbm, features, row_sems.at[0])
    inputs.start()
    spans = [slice(first, first + 256) for first in range(0, hidden, 256)]
    streams = [
        [
            pltpu.make_async_copy(weights_hbm.at[0, :, at], weights.at[0, :, at], column_sems.at[0, index]),
            pltpu.make_async_copy(weights_hbm.at[1, :, at], weights.at[1, :, at], column_sems.at[1, index]),
            pltpu.make_async_copy(cotangent_hbm.at[:, at], cotangent.at[:, at], column_sems.at[2, index]),
        ]
        for index, at in enumerate(spans)
    ]
    for stream in streams:
        for copy in stream:
            copy.start()

    summed[...] = jnp.zeros_like(summed)
    for sender in range(senders):
        arrivals[sender].wait()
        at = pl.ds(pl.multiple_of(into_ref[sender] * block, block), block)
        summed[at, :] = summed[at, :] + slots[sender].astype(F32)
    aggregate[...] = summed[...].astype(BF16)
    results = [pltpu.make_async_copy(aggregate, aggregate_hbm, row_sems.at[1])]
    results[0].start()

    @pl.when(core == 0)
    def _():
        left[...] = aggregate[...].T

    @pl.when(core != 0)
    def _():
        turning = pltpu.make_async_copy(turned_hbm, left, row_sems.at[2])
        turning.start()
        turning.wait()

    inputs.wait()
    for index, at in enumerate(spans):
        for copy in streams[index]:
            copy.wait()
        value = jnp.dot(features[...], weights[0, :, at], preferred_element_type=F32) + jnp.dot(
            aggregate[...], weights[1, :, at], preferred_element_type=F32
        )
        square = value * value
        bend = jnp.tanh(value * (SCALE + SCALE * CUBIC * square))
        inner = value * (SCALE + 3.0 * SCALE * CUBIC * square)
        slope = (1.0 + bend) * (0.5 + 0.5 * inner * (1.0 - bend))
        grad[:, at] = (cotangent[:, at].astype(F32) * slope).astype(BF16)
        results.append(pltpu.make_async_copy(grad.at[:, at], grad_hbm.at[:, at], out_sems.at[0, index]))
        results[-1].start()
        sent[:, at] = jnp.dot(left[...], grad[:, at], preferred_element_type=F32).astype(BF16)
        results.append(pltpu.make_async_copy(sent.at[:, at], sent_hbm.at[:, at], out_sems.at[1, index]))
        results[-1].start()
    for result in results:
        result.wait()


def kept_kernel(core_ref, turned_hbm, aggregate_hbm, grad_hbm, out_hbm, turned, aggregate, grad, out, in_sems, out_sems):
    core = core_ref[0]
    spans = [slice(first, first + 512) for first in range(0, out.shape[1], 512)]
    grads = [
        pltpu.make_async_copy(grad_hbm.at[:, at], grad.at[:, at], in_sems.at[1 + index]) for index, at in enumerate(spans)
    ]
    results = [
        pltpu.make_async_copy(out.at[:, at], out_hbm.at[:, at], out_sems.at[index]) for index, at in enumerate(spans)
    ]

    def product(left_hbm, left, contract):
        def body():
            copy = pltpu.make_async_copy(left_hbm, left, in_sems.at[0])
            copy.start()
            for stream in grads:
                stream.start()
            copy.wait()
            for at, stream, result in zip(spans, grads, results):
                stream.wait()
                value = lax.dot_general(left[...], grad[:, at], (contract, ((), ())), preferred_element_type=F32)
                out[:, at] = value.astype(BF16)
                result.start()

        return body

    pl.when(core == 0)(product(turned_hbm, turned, ((1,), (0,))))
    pl.when(core != 0)(product(aggregate_hbm, aggregate, ((0,), (0,))))
    for result in results:
        result.wait()


def call(kernel, outs, places, out_places, scratch=(), flops=0, moved=0, vmem=56):
    return pl.pallas_call(
        kernel,
        out_shape=outs,
        in_specs=places,
        out_specs=out_places,
        scratch_shapes=list(scratch),
        compiler_params=pltpu.CompilerParams(vmem_limit_bytes=vmem * MIB),
        cost_estimate=pl.CostEstimate(flops=flops, bytes_accessed=moved, transcendentals=0),
    )


def joined(held, other, upper, axis):
    return jnp.stack([jnp.where(upper, other, held), jnp.where(upper, held, other)], axis=axis)


def gather_high(held, high):
    step = 1
    while step < lax.axis_size("rep") // 2:
        other = swap(held, "rep", 2 * step)
        upper = (high & step) != 0
        held = jnp.concatenate([jnp.where(upper, other, held), jnp.where(upper, held, other)], axis=-1)
        step *= 2
    return held


def added(left, right):
    return (left.astype(F32) + right.astype(F32)).astype(BF16)


def half_of(value, axis, which):
    size = value.shape[axis] // 2
    return lax.dynamic_slice_in_dim(value, which * size, size, axis)


def reduce_high(value, high):
    step = lax.axis_size("rep") // 4
    while step:
        upper = (high // step) % 2
        value = added(half_of(value, 2, upper), swap(half_of(value, 2, 1 - upper), "rep", 2 * step))
        step //= 2
    return value


def reduce_low(value, low):
    value = value.reshape(value.shape[0] // 2, 2, *value.shape[1:])
    sent = lax.dynamic_index_in_dim(value, 1 - low, 1, keepdims=False)
    kept = lax.dynamic_index_in_dim(value, low, 1, keepdims=False)
    return added(kept, swap(sent, "dom", 1))


def shards(features, cotangent, w_self, w_neigh, tile_vals, tile_src, tile_peer, in_block):
    dom_size = lax.axis_size("dom")
    rows, width = features.shape
    hidden = w_self.shape[1]
    block = tile_vals.shape[1]
    me = lax.axis_index("dom")
    rep = lax.axis_index("rep")
    parts = lax.axis_size("rep") // 2
    core, high = rep & 1, rep >> 1
    low, place = me & 1, me >> 1
    core_arg = core.astype(jnp.int32).reshape(1)

    share = hidden // parts
    held = jnp.stack([lax.dynamic_slice_in_dim(weight, high * share, share, 1) for weight in (w_self, w_neigh)])
    pieces = [cross(held, 2 * step) for step in range(dom_size // 2)]
    slots = call(
        slots_kernel,
        jax.ShapeDtypeStruct((dom_size * block, width), BF16),
        [HBM] * 4,
        HBM,
        [
            pltpu.SMEM(tile_src.shape, jnp.int32),
            pltpu.SMEM(tile_peer.shape, jnp.int32),
            pltpu.VMEM(tile_vals.shape, BF16),
            pltpu.VMEM(features.shape, BF16),
            pltpu.VMEM((dom_size * block, rows), F32),
            pltpu.VMEM((dom_size * block, width), BF16),
            DMA((4,)),
            DMA((dom_size // 4,)),
        ],
        flops=2 * dom_size * block * rows * width,
        moved=tile_vals.size * 2 + rows * width * 4,
    )(tile_src, tile_peer, tile_vals, features)
    *pieces, _ = lax.optimization_barrier((*pieces, slots))
    received = lax.all_to_all(slots.reshape(dom_size, block, width), "dom", split_axis=0, concat_axis=0, tiled=True)
    pieces[0] = jnp.where(core == 0, held, pieces[0])
    pieces = [piece[:, None] for piece in pieces]
    bit = 1
    while len(pieces) > 1:
        upper = (place & bit) != 0
        pieces = [
            jnp.concatenate([jnp.where(upper, b, a), jnp.where(upper, a, b)], axis=1)
            for a, b in zip(pieces[::2], pieces[1::2])
        ]
        bit *= 2
    mine = gather_high(pieces[0], high)
    other = swap(mine, "rep", 1)
    weights = joined(mine, other, (low ^ core) != 0, 2).reshape(2, width, hidden)
    turned = features.T

    aggregate, grad, sent = call(
        layer_kernel,
        [
            jax.ShapeDtypeStruct((rows, width), BF16),
            jax.ShapeDtypeStruct((rows, hidden), BF16),
            jax.ShapeDtypeStruct((width, hidden), BF16),
        ],
        [SMEM, SMEM] + [HBM] * 5,
        [HBM] * 3,
        [
            pltpu.VMEM((dom_size, block, width), BF16),
            pltpu.VMEM((rows, width), BF16),
            pltpu.VMEM((width, rows), BF16),
            pltpu.VMEM((rows, hidden), BF16),
            pltpu.VMEM((2, width, hidden), BF16),
            pltpu.VMEM((rows, width), F32),
            pltpu.VMEM((rows, width), BF16),
            pltpu.VMEM((rows, hidden), BF16),
            pltpu.VMEM((width, hidden), BF16),
            DMA((dom_size,)),
            DMA((3,)),
            DMA((3, hidden // 256)),
            DMA((2, hidden // 256)),
        ],
        flops=6 * rows * width * hidden,
        moved=16 * rows * hidden,
    )(core_arg, in_block, received, features, turned, cotangent, weights)
    arrived = swap(sent, "rep", 1)
    kept = call(
        kept_kernel,
        jax.ShapeDtypeStruct((width, hidden), BF16),
        [SMEM] + [HBM] * 3,
        HBM,
        [
            pltpu.VMEM((width, rows), BF16),
            pltpu.VMEM((rows, width), BF16),
            pltpu.VMEM((rows, hidden), BF16),
            pltpu.VMEM((width, hidden), BF16),
            DMA((1 + hidden // 512,)),
            DMA((hidden // 512,)),
        ],
        flops=2 * rows * width * hidden,
        moved=6 * rows * hidden,
    )(core_arg, turned, aggregate, grad)
    chip = added(kept, arrived).reshape(dom_size, width // dom_size, hidden)
    first, second = chip[:, :, : hidden // 2], chip[:, :, hidden // 2 :]
    first, second = reduce_low(first, low), reduce_high(second, high)
    first, second = reduce_high(first, high), reduce_low(second, low)
    both = jnp.concatenate([first, second], axis=2)
    summed = lax.dynamic_index_in_dim(both, place, 0, keepdims=False).astype(F32)
    for step in range(1, dom_size // 2):
        piece = lax.dynamic_index_in_dim(both, place ^ step, 0, keepdims=False)
        summed = summed + swap(piece, "dom", 2 * step).astype(F32)
    summed = summed.astype(BF16)
    size = summed.shape[1] // 2
    held = gather_high(jnp.stack([summed[:, :size], summed[:, size:]]), high)
    whole = jnp.concatenate([held[0], held[1]], axis=1)
    opposite = swap(whole, "rep", 1)
    return (
        jnp.where(core == 0, whole, opposite).astype(F32),
        jnp.where(core == 0, opposite, whole).astype(F32),
    )


def solution(mesh):
    in_specs = (
        P(("rep", "dom"), None),
        P(("rep", "dom"), None),
        P("dom", None),
        P("dom", None),
        P(("rep", "dom"), None, None),
        P(("rep", "dom")),
        P(("rep", "dom")),
        P(("rep", "dom")),
    )
    out_specs = (P("dom", None), P("dom", None))
    return jax.shard_map(shards, mesh=mesh, in_specs=in_specs, out_specs=out_specs, check_vma=False)
```

```python
import jax
import jax.numpy as jnp
from jax import lax
from jax.experimental import pallas as pl
from jax.experimental.pallas import tpu as pltpu
from jax.sharding import PartitionSpec as P

F32 = jnp.float32
BF16 = jnp.bfloat16
SCALE = 0.7978845608
CUBIC = 0.044715
MIB = 1 << 20
HBM = pl.BlockSpec(memory_space=pltpu.HBM)
SMEM = pl.BlockSpec(memory_space=pltpu.SMEM)
VMEM = pl.BlockSpec(memory_space=pltpu.VMEM)
DMA = pltpu.SemaphoreType.DMA


def swap(value, axis, step):
    size = lax.axis_size(axis)
    return lax.ppermute(value, axis, [(index, index ^ step) for index in range(size)])


def cross(value, step):
    reps, doms = lax.axis_size("rep"), lax.axis_size("dom")
    pairs = [
        (rep * doms + dom, rep * doms + (dom ^ step ^ (rep & 1))) for rep in range(reps) for dom in range(doms)
    ]
    return lax.ppermute(value, ("rep", "dom"), [(source, target) for source, target in pairs if source != target])


def split_copies(source, target, sems, count=4):
    size = source.shape[0] // count
    return [
        pltpu.make_async_copy(
            source.at[index * size : (index + 1) * size], target.at[index * size : (index + 1) * size], sems.at[index]
        )
        for index in range(count)
    ]


def slots_kernel(
    src_hbm, peer_hbm, tiles_hbm, features_hbm, out_hbm, src, peer, tiles, features, dense, out, in_sems, out_sems
):
    scalars = [
        pltpu.make_async_copy(src_hbm, src, in_sems.at[2, 0]),
        pltpu.make_async_copy(peer_hbm, peer, in_sems.at[2, 1]),
    ]
    tile_copies = split_copies(tiles_hbm, tiles, in_sems.at[0])
    feature_copies = split_copies(features_hbm, features, in_sems.at[1])
    for copy in scalars + tile_copies + feature_copies:
        copy.start()
    count, block, _ = tiles.shape
    dense[...] = jnp.zeros_like(dense)
    for copy in scalars + tile_copies:
        copy.wait()

    def place(tile, carry):
        row = pl.multiple_of(peer[tile] * block, block)
        column = pl.multiple_of(src[tile] * block, block)
        at = (pl.ds(row, block), pl.ds(column, block))
        dense[at] = dense[at] + tiles[tile].astype(F32)
        return carry

    lax.fori_loop(0, count, place, 0)
    for copy in feature_copies:
        copy.wait()
    chunk = 4 * block
    results = []
    for index in range(out.shape[0] // chunk):
        at = slice(index * chunk, (index + 1) * chunk)
        out[at, :] = jnp.dot(dense[at, :].astype(BF16), features[...], preferred_element_type=F32).astype(BF16)
        results.append(pltpu.make_async_copy(out.at[at, :], out_hbm.at[at, :], out_sems.at[index]))
        results[-1].start()
    for result in results:
        result.wait()


def layer_kernel(
    core_ref,
    into_ref,
    slots_hbm,
    features_hbm,
    turned_hbm,
    cotangent_hbm,
    w_self_hbm,
    w_neigh_hbm,
    aggregate_hbm,
    grad_hbm,
    sent_hbm,
    slots,
    features,
    left,
    cotangent,
    w_self,
    w_neigh,
    summed,
    values,
    aggregate,
    grad,
    sent,
    slot_sems,
    row_sems,
    weight_sems,
    out_sems,
):
    senders, block, _ = slots.shape
    rows, hidden = grad.shape
    core = core_ref[0]
    arrivals = [
        pltpu.make_async_copy(slots_hbm.at[sender], slots.at[sender], slot_sems.at[sender]) for sender in range(senders)
    ]
    chunk = 256
    parts = rows // chunk
    weight_copies = split_copies(w_self_hbm, w_self, weight_sems.at[0])
    weight_copies += split_copies(w_neigh_hbm, w_neigh, weight_sems.at[1])
    feature_copies = split_copies(features_hbm, features, row_sems.at[0], parts)
    cotangent_copies = split_copies(cotangent_hbm, cotangent, row_sems.at[1], parts)
    for copy in arrivals + weight_copies + feature_copies + cotangent_copies:
        copy.start()
    turning = pltpu.make_async_copy(turned_hbm, left, weight_sems.at[2, 0])
    pl.when(core != 0)(turning.start)

    summed[...] = jnp.zeros_like(summed)
    for sender in range(senders):
        arrivals[sender].wait()
        at = pl.ds(pl.multiple_of(into_ref[sender] * block, block), block)
        summed[at, :] = summed[at, :] + slots[sender].astype(F32)
    aggregate[...] = summed[...].astype(BF16)
    results = [pltpu.make_async_copy(aggregate, aggregate_hbm, weight_sems.at[2, 1])]
    results[0].start()

    @pl.when(core == 0)
    def _():
        left[...] = aggregate[...].T

    pl.when(core != 0)(turning.wait)
    for copy in weight_copies + feature_copies:
        copy.wait()
    span = 512

    def multiply(index):
        at = slice(index * chunk, (index + 1) * chunk)
        for first in range(0, hidden, span):
            columns = slice(first, first + span)
            values[index % 2, :, columns] = jnp.dot(
                features[at, :], w_self[:, columns], preferred_element_type=F32
            ) + jnp.dot(aggregate[at, :], w_neigh[:, columns], preferred_element_type=F32)

    multiply(0)
    for index in range(parts):
        if index + 1 < parts:
            multiply(index + 1)
        cotangent_copies[index].wait()
        for row in range(0, chunk, 16):
            at = slice(index * chunk + row, index * chunk + row + 16)
            for first in range(0, hidden, span):
                columns = slice(first, first + span)
                value = values[index % 2, row : row + 16, columns]
                square = value * value
                bend = jnp.tanh(value * (SCALE + SCALE * CUBIC * square))
                inner = value * (SCALE + 3.0 * SCALE * CUBIC * square)
                slope = (1.0 + bend) * (0.5 + 0.5 * inner * (1.0 - bend))
                grad[at, columns] = (cotangent[at, columns].astype(F32) * slope).astype(BF16)
        at = slice(index * chunk, (index + 1) * chunk)
        results.append(pltpu.make_async_copy(grad.at[at, :], grad_hbm.at[at, :], out_sems.at[0, index]))
        results[-1].start()
    for index, first in enumerate(range(0, hidden, span)):
        at = slice(first, first + span)
        sent[:, at] = jnp.dot(left[...], grad[:, at], preferred_element_type=F32).astype(BF16)
        results.append(pltpu.make_async_copy(sent.at[:, at], sent_hbm.at[:, at], out_sems.at[1, index]))
        results[-1].start()
    for result in results:
        result.wait()


def kept_kernel(core_ref, turned_hbm, aggregate_hbm, grad_hbm, out_hbm, turned, aggregate, grad, out, in_sems, out_sems):
    core = core_ref[0]
    spans = [slice(first, first + 512) for first in range(0, out.shape[1], 512)]
    grads = split_copies(grad_hbm, grad, in_sems.at[1])
    results = [
        pltpu.make_async_copy(out.at[:, at], out_hbm.at[:, at], out_sems.at[index]) for index, at in enumerate(spans)
    ]

    def product(left_hbm, left, contract):
        def body():
            copies = split_copies(left_hbm, left, in_sems.at[0]) + grads
            for copy in copies:
                copy.start()
            for copy in copies:
                copy.wait()
            for at, result in zip(spans, results):
                value = lax.dot_general(left[...], grad[:, at], (contract, ((), ())), preferred_element_type=F32)
                out[:, at] = value.astype(BF16)
                result.start()

        return body

    pl.when(core == 0)(product(turned_hbm, turned, ((1,), (0,))))
    pl.when(core != 0)(product(aggregate_hbm, aggregate, ((0,), (0,))))
    for result in results:
        result.wait()


def call(kernel, outs, places, out_places, scratch=(), flops=0, moved=0, vmem=56):
    return pl.pallas_call(
        kernel,
        out_shape=outs,
        in_specs=places,
        out_specs=out_places,
        scratch_shapes=list(scratch),
        compiler_params=pltpu.CompilerParams(vmem_limit_bytes=vmem * MIB),
        cost_estimate=pl.CostEstimate(flops=flops, bytes_accessed=moved, transcendentals=0),
    )


def joined(held, other, upper, axis):
    return jnp.stack([jnp.where(upper, other, held), jnp.where(upper, held, other)], axis=axis)


def gather_high(held, high):
    step = 1
    while step < lax.axis_size("rep") // 2:
        other = swap(held, "rep", 2 * step)
        upper = (high & step) != 0
        held = jnp.concatenate([jnp.where(upper, other, held), jnp.where(upper, held, other)], axis=-1)
        step *= 2
    return held


def added(left, right):
    return (left.astype(F32) + right.astype(F32)).astype(BF16)


def half_of(value, axis, which):
    size = value.shape[axis] // 2
    return lax.dynamic_slice_in_dim(value, which * size, size, axis)


def reduce_high(value, high):
    step = lax.axis_size("rep") // 4
    while step:
        upper = (high // step) % 2
        value = added(half_of(value, 2, upper), swap(half_of(value, 2, 1 - upper), "rep", 2 * step))
        step //= 2
    return value


def reduce_low(value, low):
    value = value.reshape(value.shape[0] // 2, 2, *value.shape[1:])
    sent = lax.dynamic_index_in_dim(value, 1 - low, 1, keepdims=False)
    kept = lax.dynamic_index_in_dim(value, low, 1, keepdims=False)
    return added(kept, swap(sent, "dom", 1))


def shards(features, cotangent, w_self, w_neigh, tile_vals, tile_src, tile_peer, in_block):
    dom_size = lax.axis_size("dom")
    rows, width = features.shape
    hidden = w_self.shape[1]
    block = tile_vals.shape[1]
    me = lax.axis_index("dom")
    rep = lax.axis_index("rep")
    parts = lax.axis_size("rep") // 2
    core, high = rep & 1, rep >> 1
    low, place = me & 1, me >> 1
    core_arg = core.astype(jnp.int32).reshape(1)

    share = hidden // parts
    held = jnp.stack([lax.dynamic_slice_in_dim(weight, high * share, share, 1) for weight in (w_self, w_neigh)])
    pieces = [cross(held, 2 * step) for step in range(dom_size // 2)]
    slots = call(
        slots_kernel,
        jax.ShapeDtypeStruct((dom_size * block, width), BF16),
        [HBM] * 4,
        HBM,
        [
            pltpu.SMEM(tile_src.shape, jnp.int32),
            pltpu.SMEM(tile_peer.shape, jnp.int32),
            pltpu.VMEM(tile_vals.shape, BF16),
            pltpu.VMEM(features.shape, BF16),
            pltpu.VMEM((dom_size * block, rows), F32),
            pltpu.VMEM((dom_size * block, width), BF16),
            DMA((3, 4)),
            DMA((dom_size // 4,)),
        ],
        flops=2 * dom_size * block * rows * width,
        moved=tile_vals.size * 2 + rows * width * 4,
    )(tile_src, tile_peer, tile_vals, features)
    *pieces, _ = lax.optimization_barrier((*pieces, slots))
    received = lax.all_to_all(slots.reshape(dom_size, block, width), "dom", split_axis=0, concat_axis=0, tiled=True)
    pieces[0] = jnp.where(core == 0, held, pieces[0])
    pieces = [piece[:, None] for piece in pieces]
    bit = 1
    while len(pieces) > 1:
        upper = (place & bit) != 0
        pieces = [
            jnp.concatenate([jnp.where(upper, b, a), jnp.where(upper, a, b)], axis=1)
            for a, b in zip(pieces[::2], pieces[1::2])
        ]
        bit *= 2
    mine = gather_high(pieces[0], high)
    weights = [
        joined(mine[index], swap(mine[index], "rep", 1), (low ^ core) != 0, 1).reshape(width, hidden)
        for index in range(2)
    ]
    turned = features.T

    aggregate, grad, sent = call(
        layer_kernel,
        [
            jax.ShapeDtypeStruct((rows, width), BF16),
            jax.ShapeDtypeStruct((rows, hidden), BF16),
            jax.ShapeDtypeStruct((width, hidden), BF16),
        ],
        [SMEM, SMEM] + [HBM] * 6,
        [HBM] * 3,
        [
            pltpu.VMEM((dom_size, block, width), BF16),
            pltpu.VMEM((rows, width), BF16),
            pltpu.VMEM((width, rows), BF16),
            pltpu.VMEM((rows, hidden), BF16),
            pltpu.VMEM((width, hidden), BF16),
            pltpu.VMEM((width, hidden), BF16),
            pltpu.VMEM((rows, width), F32),
            pltpu.VMEM((2, 256, hidden), F32),
            pltpu.VMEM((rows, width), BF16),
            pltpu.VMEM((rows, hidden), BF16),
            pltpu.VMEM((width, hidden), BF16),
            DMA((dom_size,)),
            DMA((2, rows // 256)),
            DMA((3, 4)),
            DMA((2, rows // 256)),
        ],
        flops=6 * rows * width * hidden,
        moved=16 * rows * hidden,
    )(core_arg, in_block, received, features, turned, cotangent, *weights)
    arrived = swap(sent, "rep", 1)
    kept = call(
        kept_kernel,
        jax.ShapeDtypeStruct((width, hidden), BF16),
        [SMEM] + [HBM] * 3,
        HBM,
        [
            pltpu.VMEM((width, rows), BF16),
            pltpu.VMEM((rows, width), BF16),
            pltpu.VMEM((rows, hidden), BF16),
            pltpu.VMEM((width, hidden), BF16),
            DMA((2, 4)),
            DMA((hidden // 512,)),
        ],
        flops=2 * rows * width * hidden,
        moved=6 * rows * hidden,
    )(core_arg, turned, aggregate, grad)
    chip = added(kept, arrived).reshape(dom_size, width // dom_size, hidden)
    first, second = chip[:, :, : hidden // 2], chip[:, :, hidden // 2 :]
    first, second = reduce_low(first, low), reduce_high(second, high)
    first, second = reduce_high(first, high), reduce_low(second, low)
    both = jnp.concatenate([first, second], axis=2)
    summed = lax.dynamic_index_in_dim(both, place, 0, keepdims=False).astype(F32)
    for step in range(1, dom_size // 2):
        piece = lax.dynamic_index_in_dim(both, place ^ step, 0, keepdims=False)
        summed = summed + swap(piece, "dom", 2 * step).astype(F32)
    summed = summed.astype(BF16)
    size = summed.shape[1] // 2
    held = gather_high(jnp.stack([summed[:, :size], summed[:, size:]]), high)
    whole = jnp.concatenate([held[0], held[1]], axis=1)
    opposite = swap(whole, "rep", 1)
    return (
        jnp.where(core == 0, whole, opposite).astype(F32),
        jnp.where(core == 0, opposite, whole).astype(F32),
    )


def solution(mesh):
    in_specs = (
        P(("rep", "dom"), None),
        P(("rep", "dom"), None),
        P("dom", None),
        P("dom", None),
        P(("rep", "dom"), None, None),
        P(("rep", "dom")),
        P(("rep", "dom")),
        P(("rep", "dom")),
    )
    out_specs = (P("dom", None), P("dom", None))
    return jax.shard_map(shards, mesh=mesh, in_specs=in_specs, out_specs=out_specs, check_vma=False)
```

```python
import functools

import jax
import jax.numpy as jnp
from jax import lax
from jax.experimental import pallas as pl
from jax.experimental.pallas import tpu as pltpu
from jax.sharding import PartitionSpec as P

F32 = jnp.float32
BF16 = jnp.bfloat16
SCALE = 0.7978845608
CUBIC = 0.044715
MIB = 1 << 20
HBM = pl.BlockSpec(memory_space=pltpu.HBM)
SMEM = pl.BlockSpec(memory_space=pltpu.SMEM)
VMEM = pl.BlockSpec(memory_space=pltpu.VMEM)
DMA = pltpu.SemaphoreType.DMA


def swap(value, axis, step):
    size = lax.axis_size(axis)
    return lax.ppermute(value, axis, [(index, index ^ step) for index in range(size)])


def cross(value, step):
    reps, doms = lax.axis_size("rep"), lax.axis_size("dom")
    pairs = [
        (rep * doms + dom, rep * doms + (dom ^ step ^ (rep & 1))) for rep in range(reps) for dom in range(doms)
    ]
    return lax.ppermute(value, ("rep", "dom"), [(source, target) for source, target in pairs if source != target])


def split_copies(source, target, sems, count=4):
    size = source.shape[0] // count
    return [
        pltpu.make_async_copy(
            source.at[index * size : (index + 1) * size], target.at[index * size : (index + 1) * size], sems.at[index]
        )
        for index in range(count)
    ]


def slots_kernel(
    src_hbm, peer_hbm, tiles_hbm, features_hbm, out_hbm, src, peer, tiles, features, dense, out, in_sems, out_sems
):
    scalars = [
        pltpu.make_async_copy(src_hbm, src, in_sems.at[2, 0]),
        pltpu.make_async_copy(peer_hbm, peer, in_sems.at[2, 1]),
    ]
    tile_copies = split_copies(tiles_hbm, tiles, in_sems.at[0])
    feature_copies = split_copies(features_hbm, features, in_sems.at[1])
    for copy in scalars + tile_copies + feature_copies:
        copy.start()
    count, block, _ = tiles.shape
    dense[...] = jnp.zeros_like(dense)
    for copy in scalars + tile_copies:
        copy.wait()

    def place(tile, carry):
        row = pl.multiple_of(peer[tile] * block, block)
        column = pl.multiple_of(src[tile] * block, block)
        at = (pl.ds(row, block), pl.ds(column, block))
        dense[at] = dense[at] + tiles[tile].astype(F32)
        return carry

    lax.fori_loop(0, count, place, 0)
    for copy in feature_copies:
        copy.wait()
    chunk = 4 * block
    results = []
    for index in range(out.shape[0] // chunk):
        at = slice(index * chunk, (index + 1) * chunk)
        out[at, :] = jnp.dot(dense[at, :].astype(BF16), features[...], preferred_element_type=F32).astype(BF16)
        results.append(pltpu.make_async_copy(out.at[at, :], out_hbm.at[at, :], out_sems.at[index]))
        results[-1].start()
    for result in results:
        result.wait()


def layer_kernel(
    sources,
    core_ref,
    flip_ref,
    into_ref,
    slots_hbm,
    features_hbm,
    turned_hbm,
    cotangent_hbm,
    *refs,
):
    self_hbms, neigh_hbms, refs = refs[:sources], refs[sources : 2 * sources], refs[2 * sources :]
    aggregate_hbm, grad_hbm, sent_hbm, slots, features, left, cotangent, w_self, w_neigh, summed = refs[:10]
    values, aggregate, grad, sent, slot_sems, row_sems, weight_sems, out_sems = refs[10:]
    senders, block, _ = slots.shape
    rows, hidden = grad.shape
    width = features.shape[1]
    core = core_ref[0]
    arrivals = [
        pltpu.make_async_copy(slots_hbm.at[sender], slots.at[sender], slot_sems.at[sender]) for sender in range(senders)
    ]
    chunk = 256
    parts = rows // chunk
    flip = flip_ref[0]
    weight_copies = []
    for index, (weight_hbms, weight) in enumerate([(self_hbms, w_self), (neigh_hbms, w_neigh)]):
        for source, weight_hbm in enumerate(weight_hbms):
            for piece in range(weight_hbm.shape[0]):
                target = piece if sources == 1 else 2 * piece + (flip ^ source)
                weight_copies.append(
                    pltpu.make_async_copy(
                        weight_hbm.at[piece], weight.at[target], weight_sems.at[index, sources * piece + source]
                    )
                )
    feature_copies = split_copies(features_hbm, features, row_sems.at[0], parts)
    cotangent_copies = split_copies(cotangent_hbm, cotangent, row_sems.at[1], parts)
    for copy in arrivals + weight_copies + feature_copies + cotangent_copies:
        copy.start()
    turning = pltpu.make_async_copy(turned_hbm, left, row_sems.at[2, 0])
    pl.when(core != 0)(turning.start)

    summed[...] = jnp.zeros_like(summed)
    for sender in range(senders):
        arrivals[sender].wait()
        at = pl.ds(pl.multiple_of(into_ref[sender] * block, block), block)
        summed[at, :] = summed[at, :] + slots[sender].astype(F32)
    aggregate[...] = summed[...].astype(BF16)
    results = [pltpu.make_async_copy(aggregate, aggregate_hbm, row_sems.at[2, 1])]
    results[0].start()

    @pl.when(core == 0)
    def _():
        left[...] = aggregate[...].T

    pl.when(core != 0)(turning.wait)
    for copy in weight_copies + feature_copies:
        copy.wait()
    span = 512

    def multiply(index):
        at = slice(index * chunk, (index + 1) * chunk)
        for first in range(0, hidden, span):
            columns = slice(first, first + span)
            values[index % 2, :, columns] = jnp.dot(
                features[at, :], w_self[:, :, columns].reshape(width, span), preferred_element_type=F32
            ) + jnp.dot(
                aggregate[at, :], w_neigh[:, :, columns].reshape(width, span), preferred_element_type=F32
            )

    multiply(0)
    for index in range(parts):
        if index + 1 < parts:
            multiply(index + 1)
        cotangent_copies[index].wait()
        for row in range(0, chunk, 16):
            at = slice(index * chunk + row, index * chunk + row + 16)
            for first in range(0, hidden, span):
                columns = slice(first, first + span)
                value = values[index % 2, row : row + 16, columns]
                square = value * value
                bend = jnp.tanh(value * (SCALE + SCALE * CUBIC * square))
                inner = value * (SCALE + 3.0 * SCALE * CUBIC * square)
                slope = (1.0 + bend) * (0.5 + 0.5 * inner * (1.0 - bend))
                grad[at, columns] = (cotangent[at, columns].astype(F32) * slope).astype(BF16)
        at = slice(index * chunk, (index + 1) * chunk)
        results.append(pltpu.make_async_copy(grad.at[at, :], grad_hbm.at[at, :], out_sems.at[0, index]))
        results[-1].start()
    for index, first in enumerate(range(0, hidden, span)):
        at = slice(first, first + span)
        sent[:, at] = jnp.dot(left[...], grad[:, at], preferred_element_type=F32).astype(BF16)
        results.append(pltpu.make_async_copy(sent.at[:, at], sent_hbm.at[:, at], out_sems.at[1, index]))
        results[-1].start()
    for result in results:
        result.wait()


def kept_kernel(core_ref, turned_hbm, aggregate_hbm, grad_hbm, out_hbm, turned, aggregate, grad, out, in_sems, out_sems):
    core = core_ref[0]
    spans = [slice(first, first + 512) for first in range(0, out.shape[1], 512)]
    grads = split_copies(grad_hbm, grad, in_sems.at[1])
    results = [
        pltpu.make_async_copy(out.at[:, at], out_hbm.at[:, at], out_sems.at[index]) for index, at in enumerate(spans)
    ]

    def product(left_hbm, left, contract):
        def body():
            copies = split_copies(left_hbm, left, in_sems.at[0]) + grads
            for copy in copies:
                copy.start()
            for copy in copies:
                copy.wait()
            for at, result in zip(spans, results):
                value = lax.dot_general(left[...], grad[:, at], (contract, ((), ())), preferred_element_type=F32)
                out[:, at] = value.astype(BF16)
                result.start()

        return body

    pl.when(core == 0)(product(turned_hbm, turned, ((1,), (0,))))
    pl.when(core != 0)(product(aggregate_hbm, aggregate, ((0,), (0,))))
    for result in results:
        result.wait()


def call(kernel, outs, places, out_places, scratch=(), flops=0, moved=0, vmem=56):
    return pl.pallas_call(
        kernel,
        out_shape=outs,
        in_specs=places,
        out_specs=out_places,
        scratch_shapes=list(scratch),
        compiler_params=pltpu.CompilerParams(vmem_limit_bytes=vmem * MIB),
        cost_estimate=pl.CostEstimate(flops=flops, bytes_accessed=moved, transcendentals=0),
    )


def joined(held, other, upper, axis):
    return jnp.stack([jnp.where(upper, other, held), jnp.where(upper, held, other)], axis=axis)


def gather_high(held, high):
    step = 1
    while step < lax.axis_size("rep") // 2:
        other = swap(held, "rep", 2 * step)
        upper = (high & step) != 0
        held = jnp.concatenate([jnp.where(upper, other, held), jnp.where(upper, held, other)], axis=-1)
        step *= 2
    return held


def added(left, right):
    return (left.astype(F32) + right.astype(F32)).astype(BF16)


def half_of(value, axis, which):
    size = value.shape[axis] // 2
    return lax.dynamic_slice_in_dim(value, which * size, size, axis)


def reduce_high(value, high):
    step = lax.axis_size("rep") // 4
    while step:
        upper = (high // step) % 2
        value = added(half_of(value, 2, upper), swap(half_of(value, 2, 1 - upper), "rep", 2 * step))
        step //= 2
    return value


def reduce_low(value, low):
    value = value.reshape(value.shape[0] // 2, 2, *value.shape[1:])
    sent = lax.dynamic_index_in_dim(value, 1 - low, 1, keepdims=False)
    kept = lax.dynamic_index_in_dim(value, low, 1, keepdims=False)
    return added(kept, swap(sent, "dom", 1))


def shards(features, cotangent, w_self, w_neigh, tile_vals, tile_src, tile_peer, in_block):
    dom_size = lax.axis_size("dom")
    rows, width = features.shape
    hidden = w_self.shape[1]
    block = tile_vals.shape[1]
    me = lax.axis_index("dom")
    rep = lax.axis_index("rep")
    parts = lax.axis_size("rep") // 2
    core, high = rep & 1, rep >> 1
    low, place = me & 1, me >> 1
    core_arg = core.astype(jnp.int32).reshape(1)

    share = hidden // parts
    held = jnp.stack([lax.dynamic_slice_in_dim(weight, high * share, share, 1) for weight in (w_self, w_neigh)])
    pieces = [cross(held, 2 * step) for step in range(dom_size // 2)]
    slots = call(
        slots_kernel,
        jax.ShapeDtypeStruct((dom_size * block, width), BF16),
        [HBM] * 4,
        HBM,
        [
            pltpu.SMEM(tile_src.shape, jnp.int32),
            pltpu.SMEM(tile_peer.shape, jnp.int32),
            pltpu.VMEM(tile_vals.shape, BF16),
            pltpu.VMEM(features.shape, BF16),
            pltpu.VMEM((dom_size * block, rows), F32),
            pltpu.VMEM((dom_size * block, width), BF16),
            DMA((3, 4)),
            DMA((dom_size // 4,)),
        ],
        flops=2 * dom_size * block * rows * width,
        moved=tile_vals.size * 2 + rows * width * 4,
    )(tile_src, tile_peer, tile_vals, features)
    *pieces, _ = lax.optimization_barrier((*pieces, slots))
    received = lax.all_to_all(slots.reshape(dom_size, block, width), "dom", split_axis=0, concat_axis=0, tiled=True)
    pieces[0] = jnp.where(core == 0, held, pieces[0])
    pieces = [piece[:, None] for piece in pieces]
    bit = 1
    while len(pieces) > 1:
        upper = (place & bit) != 0
        pieces = [
            jnp.concatenate([jnp.where(upper, b, a), jnp.where(upper, a, b)], axis=1)
            for a, b in zip(pieces[::2], pieces[1::2])
        ]
        bit *= 2
    mine = gather_high(pieces[0], high)
    flip = low ^ core
    weights = [[mine[index], swap(mine[index], "rep", 1)] for index in range(2)]
    if (width // dom_size) % 16:
        weights = [[joined(*weight, flip != 0, 1).reshape(-1, 128, hidden)] for weight in weights]
    sources, pieces = len(weights[0]), sum(weight.shape[0] for weight in weights[0])
    turned = features.T

    aggregate, grad, sent = call(
        functools.partial(layer_kernel, sources),
        [
            jax.ShapeDtypeStruct((rows, width), BF16),
            jax.ShapeDtypeStruct((rows, hidden), BF16),
            jax.ShapeDtypeStruct((width, hidden), BF16),
        ],
        [SMEM] * 3 + [HBM] * (4 + 2 * sources),
        [HBM] * 3,
        [
            pltpu.VMEM((dom_size, block, width), BF16),
            pltpu.VMEM((rows, width), BF16),
            pltpu.VMEM((width, rows), BF16),
            pltpu.VMEM((rows, hidden), BF16),
            pltpu.VMEM((pieces, width // pieces, hidden), BF16),
            pltpu.VMEM((pieces, width // pieces, hidden), BF16),
            pltpu.VMEM((rows, width), F32),
            pltpu.VMEM((2, 256, hidden), F32),
            pltpu.VMEM((rows, width), BF16),
            pltpu.VMEM((rows, hidden), BF16),
            pltpu.VMEM((width, hidden), BF16),
            DMA((dom_size,)),
            DMA((3, rows // 256)),
            DMA((2, pieces)),
            DMA((2, rows // 256)),
        ],
        flops=6 * rows * width * hidden,
        moved=16 * rows * hidden,
    )(core_arg, flip.astype(jnp.int32).reshape(1), in_block, received, features, turned, cotangent, *weights[0], *weights[1])
    arrived = swap(sent, "rep", 1)
    kept = call(
        kept_kernel,
        jax.ShapeDtypeStruct((width, hidden), BF16),
        [SMEM] + [HBM] * 3,
        HBM,
        [
            pltpu.VMEM((width, rows), BF16),
            pltpu.VMEM((rows, width), BF16),
            pltpu.VMEM((rows, hidden), BF16),
            pltpu.VMEM((width, hidden), BF16),
            DMA((2, 4)),
            DMA((hidden // 512,)),
        ],
        flops=2 * rows * width * hidden,
        moved=6 * rows * hidden,
    )(core_arg, turned, aggregate, grad)
    chip = added(kept, arrived).reshape(dom_size, width // dom_size, hidden)
    first, second = chip[:, :, : hidden // 2], chip[:, :, hidden // 2 :]
    first, second = reduce_low(first, low), reduce_high(second, high)
    first, second = reduce_high(first, high), reduce_low(second, low)
    both = jnp.concatenate([first, second], axis=2)
    summed = lax.dynamic_index_in_dim(both, place, 0, keepdims=False).astype(F32)
    for step in range(1, dom_size // 2):
        piece = lax.dynamic_index_in_dim(both, place ^ step, 0, keepdims=False)
        summed = summed + swap(piece, "dom", 2 * step).astype(F32)
    summed = summed.astype(BF16)
    size = summed.shape[1] // 2
    held = gather_high(jnp.stack([summed[:, :size], summed[:, size:]]), high)
    whole = jnp.concatenate([held[0], held[1]], axis=1)
    opposite = swap(whole, "rep", 1)
    return (
        jnp.where(core == 0, whole, opposite).astype(F32),
        jnp.where(core == 0, opposite, whole).astype(F32),
    )


def solution(mesh):
    in_specs = (
        P(("rep", "dom"), None),
        P(("rep", "dom"), None),
        P("dom", None),
        P("dom", None),
        P(("rep", "dom"), None, None),
        P(("rep", "dom")),
        P(("rep", "dom")),
        P(("rep", "dom")),
    )
    out_specs = (P("dom", None), P("dom", None))
    return jax.shard_map(shards, mesh=mesh, in_specs=in_specs, out_specs=out_specs, check_vma=False)
```

```python
import functools

import jax
import jax.numpy as jnp
from jax import lax
from jax.experimental import pallas as pl
from jax.experimental.pallas import tpu as pltpu
from jax.sharding import PartitionSpec as P

F32 = jnp.float32
BF16 = jnp.bfloat16
SCALE = 0.7978845608
CUBIC = 0.044715
MIB = 1 << 20
HBM = pl.BlockSpec(memory_space=pltpu.HBM)
SMEM = pl.BlockSpec(memory_space=pltpu.SMEM)
VMEM = pl.BlockSpec(memory_space=pltpu.VMEM)
DMA = pltpu.SemaphoreType.DMA


def swap(value, axis, step):
    size = lax.axis_size(axis)
    return lax.ppermute(value, axis, [(index, index ^ step) for index in range(size)])


def cross(value, step):
    reps, doms = lax.axis_size("rep"), lax.axis_size("dom")
    pairs = [
        (rep * doms + dom, rep * doms + (dom ^ step ^ (rep & 1))) for rep in range(reps) for dom in range(doms)
    ]
    return lax.ppermute(value, ("rep", "dom"), [(source, target) for source, target in pairs if source != target])


def split_copies(source, target, sems, count=4):
    size = source.shape[0] // count
    return [
        pltpu.make_async_copy(
            source.at[index * size : (index + 1) * size], target.at[index * size : (index + 1) * size], sems.at[index]
        )
        for index in range(count)
    ]


def slots_kernel(
    src_hbm, peer_hbm, tiles_hbm, features_hbm, out_hbm, src, peer, tiles, features, dense, out, in_sems, out_sems
):
    scalars = [
        pltpu.make_async_copy(src_hbm, src, in_sems.at[2, 0]),
        pltpu.make_async_copy(peer_hbm, peer, in_sems.at[2, 1]),
    ]
    tile_copies = split_copies(tiles_hbm, tiles, in_sems.at[0])
    feature_copies = split_copies(features_hbm, features, in_sems.at[1])
    for copy in scalars + tile_copies + feature_copies:
        copy.start()
    count, block, _ = tiles.shape
    dense[...] = jnp.zeros_like(dense)
    for copy in scalars + tile_copies:
        copy.wait()

    def place(tile, carry):
        row = pl.multiple_of(peer[tile] * block, block)
        column = pl.multiple_of(src[tile] * block, block)
        at = (pl.ds(row, block), pl.ds(column, block))
        dense[at] = dense[at] + tiles[tile].astype(F32)
        return carry

    lax.fori_loop(0, count, place, 0)
    for copy in feature_copies:
        copy.wait()
    chunk = 4 * block
    results = []
    for index in range(out.shape[0] // chunk):
        at = slice(index * chunk, (index + 1) * chunk)
        out[at, :] = jnp.dot(dense[at, :].astype(BF16), features[...], preferred_element_type=F32).astype(BF16)
        results.append(pltpu.make_async_copy(out.at[at, :], out_hbm.at[at, :], out_sems.at[index]))
        results[-1].start()
    for result in results:
        result.wait()


def layer_kernel(
    sources,
    core_ref,
    flip_ref,
    into_ref,
    slots_hbm,
    features_hbm,
    turned_hbm,
    cotangent_hbm,
    *refs,
):
    self_hbms, neigh_hbms, refs = refs[:sources], refs[sources : 2 * sources], refs[2 * sources :]
    aggregate_hbm, grad_hbm, *sent_hbms, slots, features, left, cotangent, w_self, w_neigh, summed = refs[:11]
    values, aggregate, grad, sent, slot_sems, row_sems, weight_sems, out_sems = refs[11:]
    senders, block, _ = slots.shape
    rows, hidden = grad.shape
    width = features.shape[1]
    core = core_ref[0]
    arrivals = [
        pltpu.make_async_copy(slots_hbm.at[sender], slots.at[sender], slot_sems.at[sender]) for sender in range(senders)
    ]
    chunk = 256
    parts = rows // chunk
    flip = flip_ref[0]
    weight_copies = []
    for index, (weight_hbms, weight) in enumerate([(self_hbms, w_self), (neigh_hbms, w_neigh)]):
        for source, weight_hbm in enumerate(weight_hbms):
            for piece in range(weight_hbm.shape[0]):
                target = piece if sources == 1 else 2 * piece + (flip ^ source)
                weight_copies.append(
                    pltpu.make_async_copy(
                        weight_hbm.at[piece], weight.at[target], weight_sems.at[index, sources * piece + source]
                    )
                )
    feature_copies = split_copies(features_hbm, features, row_sems.at[0], parts)
    cotangent_copies = split_copies(cotangent_hbm, cotangent, row_sems.at[1], parts)
    for copy in arrivals + weight_copies + feature_copies + cotangent_copies:
        copy.start()
    turning = pltpu.make_async_copy(turned_hbm, left, row_sems.at[2, 0])
    pl.when(core != 0)(turning.start)

    summed[...] = jnp.zeros_like(summed)
    for sender in range(senders):
        arrivals[sender].wait()
        at = pl.ds(pl.multiple_of(into_ref[sender] * block, block), block)
        summed[at, :] = summed[at, :] + slots[sender].astype(F32)
    aggregate[...] = summed[...].astype(BF16)
    results = [pltpu.make_async_copy(aggregate, aggregate_hbm, row_sems.at[2, 1])]
    results[0].start()

    @pl.when(core == 0)
    def _():
        left[...] = aggregate[...].T

    pl.when(core != 0)(turning.wait)
    for copy in weight_copies + feature_copies:
        copy.wait()
    span = hidden // 2

    def multiply(index):
        at = slice(index * chunk, (index + 1) * chunk)
        for first in range(0, hidden, span):
            columns = slice(first, first + span)
            values[index % 2, :, columns] = jnp.dot(
                features[at, :], w_self[:, :, columns].reshape(width, span), preferred_element_type=F32
            ) + jnp.dot(
                aggregate[at, :], w_neigh[:, :, columns].reshape(width, span), preferred_element_type=F32
            )

    multiply(0)
    for index in range(parts):
        if index + 1 < parts:
            multiply(index + 1)
        cotangent_copies[index].wait()
        for row in range(0, chunk, 32):
            at = slice(index * chunk + row, index * chunk + row + 32)
            for first in range(0, hidden, span):
                columns = slice(first, first + span)
                value = values[index % 2, row : row + 32, columns].astype(BF16)
                square = value * value
                bend = jnp.tanh(value * (square * (SCALE * CUBIC) + SCALE))
                inner = value * (square * (1.5 * SCALE * CUBIC) + 0.5 * SCALE)
                grad[at, columns] = cotangent[at, columns] * ((1.0 + bend) * (inner * (1.0 - bend) + 0.5))
        at = slice(index * chunk, (index + 1) * chunk)
        results.append(pltpu.make_async_copy(grad.at[at, :], grad_hbm.at[at, :], out_sems.at[0, index]))
        results[-1].start()
    for index, sent_hbm in enumerate(sent_hbms):
        at = slice(index * span, (index + 1) * span)
        sent[index] = jnp.dot(left[...], grad[:, at], preferred_element_type=F32).astype(BF16)
        results.append(pltpu.make_async_copy(sent.at[index], sent_hbm, out_sems.at[1, index]))
        results[-1].start()
    for result in results:
        result.wait()


def kept_kernel(core_ref, turned_hbm, aggregate_hbm, grad_hbm, *refs):
    *out_hbms, turned, aggregate, grad, out, in_sems, out_sems = refs
    core = core_ref[0]
    grads = split_copies(grad_hbm, grad, in_sems.at[1])
    span = out.shape[2]
    results = [
        pltpu.make_async_copy(out.at[index], out_hbm, out_sems.at[index]) for index, out_hbm in enumerate(out_hbms)
    ]

    def product(left_hbm, left, contract):
        def body():
            copies = split_copies(left_hbm, left, in_sems.at[0]) + grads
            for copy in copies:
                copy.start()
            for copy in copies:
                copy.wait()
            for index, result in enumerate(results):
                columns = slice(index * span, (index + 1) * span)
                value = lax.dot_general(left[...], grad[:, columns], (contract, ((), ())), preferred_element_type=F32)
                out[index] = value.astype(BF16)
                result.start()

        return body

    pl.when(core == 0)(product(turned_hbm, turned, ((1,), (0,))))
    pl.when(core != 0)(product(aggregate_hbm, aggregate, ((0,), (0,))))
    for result in results:
        result.wait()


def call(kernel, outs, places, out_places, scratch=(), flops=0, moved=0, vmem=56):
    return pl.pallas_call(
        kernel,
        out_shape=outs,
        in_specs=places,
        out_specs=out_places,
        scratch_shapes=list(scratch),
        compiler_params=pltpu.CompilerParams(vmem_limit_bytes=vmem * MIB),
        cost_estimate=pl.CostEstimate(flops=flops, bytes_accessed=moved, transcendentals=0),
    )


def joined(held, other, upper, axis):
    return jnp.stack([jnp.where(upper, other, held), jnp.where(upper, held, other)], axis=axis)


def gather_high(held, high):
    step = 1
    while step < lax.axis_size("rep") // 2:
        other = swap(held, "rep", 2 * step)
        upper = (high & step) != 0
        held = jnp.concatenate([jnp.where(upper, other, held), jnp.where(upper, held, other)], axis=-1)
        step *= 2
    return held


def added(terms):
    return sum(term.astype(F32) for term in terms).astype(BF16)


def half_of(value, axis, which):
    size = value.shape[axis] // 2
    return lax.dynamic_slice_in_dim(value, which * size, size, axis)


def exchanged(terms, take, which, axis, step):
    arrived = swap(added([take(term, 1 - which) for term in terms]), axis, step)
    return added([take(term, which) for term in terms] + [arrived])


def reduce_high(terms, high):
    step = lax.axis_size("rep") // 4
    while step:
        terms = [exchanged(terms, lambda term, which: half_of(term, 2, which), (high // step) % 2, "rep", 2 * step)]
        step //= 2
    return terms


def reduce_low(terms, low):
    def take(term, which):
        return lax.dynamic_index_in_dim(term.reshape(-1, 2, *term.shape[1:]), which, 1, keepdims=False)

    return [exchanged(terms, take, low, "dom", 1)]


def shards(features, cotangent, w_self, w_neigh, tile_vals, tile_src, tile_peer, in_block):
    dom_size = lax.axis_size("dom")
    rows, width = features.shape
    hidden = w_self.shape[1]
    block = tile_vals.shape[1]
    me = lax.axis_index("dom")
    rep = lax.axis_index("rep")
    parts = lax.axis_size("rep") // 2
    core, high = rep & 1, rep >> 1
    low, place = me & 1, me >> 1
    core_arg = core.astype(jnp.int32).reshape(1)

    share = hidden // parts
    held = jnp.stack([lax.dynamic_slice_in_dim(weight, high * share, share, 1) for weight in (w_self, w_neigh)])
    pieces = [cross(held, 2 * step) for step in range(dom_size // 2)]
    slots = call(
        slots_kernel,
        jax.ShapeDtypeStruct((dom_size * block, width), BF16),
        [HBM] * 4,
        HBM,
        [
            pltpu.SMEM(tile_src.shape, jnp.int32),
            pltpu.SMEM(tile_peer.shape, jnp.int32),
            pltpu.VMEM(tile_vals.shape, BF16),
            pltpu.VMEM(features.shape, BF16),
            pltpu.VMEM((dom_size * block, rows), F32),
            pltpu.VMEM((dom_size * block, width), BF16),
            DMA((3, 4)),
            DMA((dom_size // 4,)),
        ],
        flops=2 * dom_size * block * rows * width,
        moved=tile_vals.size * 2 + rows * width * 4,
    )(tile_src, tile_peer, tile_vals, features)
    *pieces, _ = lax.optimization_barrier((*pieces, slots))
    received = lax.all_to_all(slots.reshape(dom_size, block, width), "dom", split_axis=0, concat_axis=0, tiled=True)
    pieces[0] = jnp.where(core == 0, held, pieces[0])
    pieces = [piece[:, None] for piece in pieces]
    bit = 1
    while len(pieces) > 1:
        upper = (place & bit) != 0
        pieces = [
            jnp.concatenate([jnp.where(upper, b, a), jnp.where(upper, a, b)], axis=1)
            for a, b in zip(pieces[::2], pieces[1::2])
        ]
        bit *= 2
    mine = gather_high(pieces[0], high)
    flip = low ^ core
    weights = [[mine[index], swap(mine[index], "rep", 1)] for index in range(2)]
    if (width // dom_size) % 16:
        weights = [[joined(*weight, flip != 0, 1).reshape(-1, 128, hidden)] for weight in weights]
    sources, pieces = len(weights[0]), sum(weight.shape[0] for weight in weights[0])
    turned = features.T

    term_halves = [jax.ShapeDtypeStruct((width, hidden // 2), BF16)] * 2
    aggregate, grad, *sent = call(
        functools.partial(layer_kernel, sources),
        [
            jax.ShapeDtypeStruct((rows, width), BF16),
            jax.ShapeDtypeStruct((rows, hidden), BF16),
            *term_halves,
        ],
        [SMEM] * 3 + [HBM] * (4 + 2 * sources),
        [HBM] * 4,
        [
            pltpu.VMEM((dom_size, block, width), BF16),
            pltpu.VMEM((rows, width), BF16),
            pltpu.VMEM((width, rows), BF16),
            pltpu.VMEM((rows, hidden), BF16),
            pltpu.VMEM((pieces, width // pieces, hidden), BF16),
            pltpu.VMEM((pieces, width // pieces, hidden), BF16),
            pltpu.VMEM((rows, width), F32),
            pltpu.VMEM((2, 256, hidden), F32),
            pltpu.VMEM((rows, width), BF16),
            pltpu.VMEM((rows, hidden), BF16),
            pltpu.VMEM((2, width, hidden // 2), BF16),
            DMA((dom_size,)),
            DMA((3, rows // 256)),
            DMA((2, pieces)),
            DMA((2, rows // 256)),
        ],
        flops=6 * rows * width * hidden,
        moved=16 * rows * hidden,
    )(core_arg, flip.astype(jnp.int32).reshape(1), in_block, received, features, turned, cotangent, *weights[0], *weights[1])
    arrived = [swap(half, "rep", 1) for half in sent]
    kept = call(
        kept_kernel,
        term_halves,
        [SMEM] + [HBM] * 3,
        [HBM] * 2,
        [
            pltpu.VMEM((width, rows), BF16),
            pltpu.VMEM((rows, width), BF16),
            pltpu.VMEM((rows, hidden), BF16),
            pltpu.VMEM((2, width, hidden // 2), BF16),
            DMA((2, 4)),
            DMA((2,)),
        ],
        flops=2 * rows * width * hidden,
        moved=6 * rows * hidden,
    )(core_arg, turned, aggregate, grad)
    first, second = [
        [term.reshape(dom_size, width // dom_size, hidden // 2) for term in terms] for terms in zip(kept, arrived)
    ]
    first, second = reduce_low(first, low), reduce_high(second, high)
    (first,), (second,) = reduce_high(first, high), reduce_low(second, low)
    both = jnp.concatenate([first, second], axis=2)
    summed = lax.dynamic_index_in_dim(both, place, 0, keepdims=False).astype(F32)
    for step in range(1, dom_size // 2):
        piece = lax.dynamic_index_in_dim(both, place ^ step, 0, keepdims=False)
        summed = summed + swap(piece, "dom", 2 * step).astype(F32)
    summed = summed.astype(BF16)
    size = summed.shape[1] // 2
    held = gather_high(jnp.stack([summed[:, :size], summed[:, size:]]), high)
    whole = jnp.concatenate([held[0], held[1]], axis=1)
    opposite = swap(whole, "rep", 1)
    return (
        jnp.where(core == 0, whole, opposite).astype(F32),
        jnp.where(core == 0, opposite, whole).astype(F32),
    )


def solution(mesh):
    in_specs = (
        P(("rep", "dom"), None),
        P(("rep", "dom"), None),
        P("dom", None),
        P("dom", None),
        P(("rep", "dom"), None, None),
        P(("rep", "dom")),
        P(("rep", "dom")),
        P(("rep", "dom")),
    )
    out_specs = (P("dom", None), P("dom", None))
    return jax.shard_map(shards, mesh=mesh, in_specs=in_specs, out_specs=out_specs, check_vma=False)
```

```python
import functools

import jax
import jax.numpy as jnp
from jax import lax
from jax.experimental import pallas as pl
from jax.experimental.pallas import tpu as pltpu
from jax.sharding import PartitionSpec as P

F32 = jnp.float32
BF16 = jnp.bfloat16
SCALE = 0.7978845608
CUBIC = 0.044715
MIB = 1 << 20
HBM = pl.BlockSpec(memory_space=pltpu.HBM)
SMEM = pl.BlockSpec(memory_space=pltpu.SMEM)
VMEM = pl.BlockSpec(memory_space=pltpu.VMEM)
DMA = pltpu.SemaphoreType.DMA


def swap(value, axis, step):
    size = lax.axis_size(axis)
    return lax.ppermute(value, axis, [(index, index ^ step) for index in range(size)])


def cross(value, step):
    reps, doms = lax.axis_size("rep"), lax.axis_size("dom")
    pairs = [
        (rep * doms + dom, rep * doms + (dom ^ step ^ (rep & 1))) for rep in range(reps) for dom in range(doms)
    ]
    return lax.ppermute(value, ("rep", "dom"), [(source, target) for source, target in pairs if source != target])


def split_copies(source, target, sems, count=4):
    size = source.shape[0] // count
    return [
        pltpu.make_async_copy(
            source.at[index * size : (index + 1) * size], target.at[index * size : (index + 1) * size], sems.at[index]
        )
        for index in range(count)
    ]


def slots_kernel(
    src_hbm, peer_hbm, tiles_hbm, features_hbm, out_hbm, src, peer, tiles, features, dense, out, in_sems, out_sems
):
    scalars = [
        pltpu.make_async_copy(src_hbm, src, in_sems.at[2, 0]),
        pltpu.make_async_copy(peer_hbm, peer, in_sems.at[2, 1]),
    ]
    tile_copies = split_copies(tiles_hbm, tiles, in_sems.at[0])
    feature_copies = split_copies(features_hbm, features, in_sems.at[1])
    for copy in scalars + tile_copies + feature_copies:
        copy.start()
    count, block, _ = tiles.shape
    dense[...] = jnp.zeros_like(dense)
    for copy in scalars + tile_copies:
        copy.wait()

    def place(tile, carry):
        row = pl.multiple_of(peer[tile] * block, block)
        column = pl.multiple_of(src[tile] * block, block)
        at = (pl.ds(row, block), pl.ds(column, block))
        dense[at] = dense[at] + tiles[tile].astype(F32)
        return carry

    lax.fori_loop(0, count, place, 0)
    for copy in feature_copies:
        copy.wait()
    chunk = 4 * block
    results = []
    for index in range(out.shape[0] // chunk):
        at = slice(index * chunk, (index + 1) * chunk)
        out[at, :] = jnp.dot(dense[at, :].astype(BF16), features[...], preferred_element_type=F32).astype(BF16)
        results.append(pltpu.make_async_copy(out.at[at, :], out_hbm.at[at, :], out_sems.at[index]))
        results[-1].start()
    for result in results:
        result.wait()


def weight_copies(flip, weight_hbms, weight, sems):
    sources = len(weight_hbms)
    copies = []
    for source, weight_hbm in enumerate(weight_hbms):
        for piece in range(weight_hbm.shape[0]):
            target = piece if sources == 1 else 2 * piece + (flip ^ source)
            copies.append(
                pltpu.make_async_copy(weight_hbm.at[piece], weight.at[target], sems.at[sources * piece + source])
            )
    return copies


def self_kernel(flip_ref, features_hbm, *refs):
    *weight_hbms, out_hbm, features, weight, out, feature_sems, weight_sems, out_sems = refs
    rows, width = features.shape
    hidden = out.shape[1]
    copies = weight_copies(flip_ref[0], weight_hbms, weight, weight_sems)
    copies += split_copies(features_hbm, features, feature_sems)
    for copy in copies:
        copy.start()
    for copy in copies:
        copy.wait()
    chunk = 256
    results = split_copies(out, out_hbm, out_sems, rows // chunk)
    for index, result in enumerate(results):
        at = slice(index * chunk, (index + 1) * chunk)
        out[at, :] = jnp.dot(
            features[at, :], weight[...].reshape(width, hidden), preferred_element_type=F32
        ).astype(BF16)
        result.start()
    for result in results:
        result.wait()


def layer_kernel(
    sources, pieces, places_ref, into_ref, slots_ref, total_hbm, turned_hbm, cotangent_hbm, *refs
):
    weight_hbms, out_hbms = refs[:sources], refs[sources:-15]
    total, turned, cotangent, weight, summed, values, aggregate, left, grad, first, second = refs[-15:-4]
    row_sems, weight_sems, turned_sems, out_sems = refs[-4:]
    senders, block, _ = slots_ref.shape
    rows, hidden = grad.shape
    width = aggregate.shape[1]
    core, flip, low, upper = [places_ref[index] for index in range(4)]
    chunk = 256
    parts = rows // chunk
    weights = weight_copies(flip, weight_hbms, weight, weight_sems)
    totals = split_copies(total_hbm, total, row_sems.at[0], parts)
    cotangents = split_copies(cotangent_hbm, cotangent, row_sems.at[1], parts)
    turnings = split_copies(turned_hbm, turned, turned_sems)
    for copy in weights + totals + cotangents + turnings:
        copy.start()

    summed[...] = jnp.zeros_like(summed)
    for sender in range(senders):
        at = pl.ds(pl.multiple_of(into_ref[sender] * block, block), block)
        summed[at, :] = summed[at, :] + slots_ref[sender].astype(F32)
    aggregate[...] = summed[...].astype(BF16)
    left[...] = aggregate[...].T
    for copy in weights:
        copy.wait()
    span = hidden // 2

    def multiply(index):
        at = slice(index * chunk, (index + 1) * chunk)
        for begin in range(0, hidden, span):
            columns = slice(begin, begin + span)
            values[index % 2, :, columns] = jnp.dot(
                aggregate[at, :], weight[:, :, columns].reshape(width, span), preferred_element_type=F32
            )

    multiply(0)
    for index in range(parts):
        if index + 1 < parts:
            multiply(index + 1)
        totals[index].wait()
        cotangents[index].wait()
        for row in range(0, chunk, 32):
            at = slice(index * chunk + row, index * chunk + row + 32)
            for begin in range(0, hidden, span):
                columns = slice(begin, begin + span)
                value = values[index % 2, row : row + 32, columns] + total[at, columns].astype(F32)
                value = value.astype(BF16)
                square = value * value
                bend = jnp.tanh(value * (square * (SCALE * CUBIC) + SCALE))
                inner = value * (square * (1.5 * SCALE * CUBIC) + 0.5 * SCALE)
                grad[at, columns] = cotangent[at, columns] * ((1.0 + bend) * (inner * (1.0 - bend) + 0.5))

    for copy in turnings:
        copy.wait()
    results = []

    def send(source, target):
        results.append(pltpu.make_async_copy(source, target, out_sems.at[len(results)]))
        results[-1].start()

    for index, operand in enumerate([turned, left]):
        product = jnp.dot(operand[...], grad[:, :span], preferred_element_type=F32).astype(BF16)
        first[index] = product.reshape(first.shape[1:])
    for term, which in enumerate([1 - core, core]):
        if pieces:
            for leave, bit in enumerate([1 - low, low]):
                for row in range(first.shape[1] // 2):
                    send(first.at[which, 2 * row + bit], out_hbms[4 * term + leave].at[row])
        else:
            send(first.at[which], out_hbms[4 * term])
    for index, operand in enumerate([turned, left]):
        for side in range(2):
            columns = slice(span + side * span // 2, span + (side + 1) * span // 2)
            second[index, side] = jnp.dot(operand[...], grad[:, columns], preferred_element_type=F32).astype(BF16)
    for term, which in enumerate([1 - core, core]):
        for leave, bit in enumerate([1 - upper, upper]):
            send(second.at[which, bit], out_hbms[4 * term + 2 + leave])
    for result in results:
        result.wait()


def call(kernel, outs, places, out_places, scratch=(), flops=0, moved=0, vmem=56):
    return pl.pallas_call(
        kernel,
        out_shape=outs,
        in_specs=places,
        out_specs=out_places,
        scratch_shapes=list(scratch),
        compiler_params=pltpu.CompilerParams(vmem_limit_bytes=vmem * MIB),
        cost_estimate=pl.CostEstimate(flops=flops, bytes_accessed=moved, transcendentals=0),
    )


def joined(held, other, upper, axis):
    return jnp.stack([jnp.where(upper, other, held), jnp.where(upper, held, other)], axis=axis)


def gather_high(held, high):
    step = 1
    while step < lax.axis_size("rep") // 2:
        other = swap(held, "rep", 2 * step)
        upper = (high & step) != 0
        held = jnp.concatenate([jnp.where(upper, other, held), jnp.where(upper, held, other)], axis=-1)
        step *= 2
    return held


def added(terms):
    return sum(term.astype(F32) for term in terms).astype(BF16)


def half_of(value, axis, which):
    size = value.shape[axis] // 2
    return lax.dynamic_slice_in_dim(value, which * size, size, axis)


def low_half(term, which):
    return lax.dynamic_index_in_dim(term.reshape(-1, 2, *term.shape[1:]), which, 1, keepdims=False)


def column_half(term, which):
    size = term.shape[-1] // 2
    return lax.dynamic_slice_in_dim(term, which * size, size, term.ndim - 1)


def exchanged(term, take, which, axis, step):
    return added([take(term, which), swap(take(term, 1 - which), axis, step)])


def reduce_high(term, high, step):
    while step:
        term = exchanged(term, column_half, (high // step) % 2, "rep", 2 * step)
        step //= 2
    return term


def shards(features, cotangent, w_self, w_neigh, tile_vals, tile_src, tile_peer, in_block):
    dom_size = lax.axis_size("dom")
    rows, width = features.shape
    hidden = w_self.shape[1]
    block = tile_vals.shape[1]
    me = lax.axis_index("dom")
    rep = lax.axis_index("rep")
    parts = lax.axis_size("rep") // 2
    core, high = rep & 1, rep >> 1
    low, place = me & 1, me >> 1

    share = hidden // parts
    held = jnp.stack([lax.dynamic_slice_in_dim(weight, high * share, share, 1) for weight in (w_self, w_neigh)])
    pieces = [cross(held, 2 * step) for step in range(dom_size // 2)]
    slots = call(
        slots_kernel,
        jax.ShapeDtypeStruct((dom_size * block, width), BF16),
        [HBM] * 4,
        HBM,
        [
            pltpu.SMEM(tile_src.shape, jnp.int32),
            pltpu.SMEM(tile_peer.shape, jnp.int32),
            pltpu.VMEM(tile_vals.shape, BF16),
            pltpu.VMEM(features.shape, BF16),
            pltpu.VMEM((dom_size * block, rows), F32),
            pltpu.VMEM((dom_size * block, width), BF16),
            DMA((3, 4)),
            DMA((dom_size // 4,)),
        ],
        flops=2 * dom_size * block * rows * width,
        moved=tile_vals.size * 2 + rows * width * 4,
    )(tile_src, tile_peer, tile_vals, features)
    *pieces, _ = lax.optimization_barrier((*pieces, slots))
    received = lax.all_to_all(slots.reshape(dom_size, block, width), "dom", split_axis=0, concat_axis=0, tiled=True)
    pieces[0] = jnp.where(core == 0, held, pieces[0])
    pieces = [piece[:, None] for piece in pieces]
    bit = 1
    while len(pieces) > 1:
        upper = (place & bit) != 0
        pieces = [
            jnp.concatenate([jnp.where(upper, b, a), jnp.where(upper, a, b)], axis=1)
            for a, b in zip(pieces[::2], pieces[1::2])
        ]
        bit *= 2
    mine = gather_high(pieces[0], high)
    depth = width // dom_size
    tiled = depth % 16 == 0
    flip = low ^ core
    weights = [[mine[index], swap(mine[index], "rep", 1)] for index in range(2)]
    if not tiled:
        weights = [[joined(*weight, flip != 0, 1).reshape(-1, 128, hidden)] for weight in weights]
    sources, count = len(weights[0]), sum(weight.shape[0] for weight in weights[0])
    weight_shape = pltpu.VMEM((count, width // count, hidden), BF16)
    total = call(
        self_kernel,
        jax.ShapeDtypeStruct((rows, hidden), BF16),
        [SMEM] + [HBM] * (1 + sources),
        HBM,
        [
            pltpu.VMEM((rows, width), BF16),
            weight_shape,
            pltpu.VMEM((rows, hidden), BF16),
            DMA((4,)),
            DMA((count,)),
            DMA((rows // 256,)),
        ],
    )(flip.astype(jnp.int32).reshape(1), features, *weights[0])
    turned = features.T

    span = hidden // 2
    upper = (high // (parts // 2)) % 2
    places = jnp.stack([core, flip, low, upper]).astype(jnp.int32)
    if tiled:
        first_shapes = [jax.ShapeDtypeStruct((dom_size // 2, depth, span), BF16)] * 2
        first_scratch = (2, dom_size, depth, span)
    else:
        first_shapes = [jax.ShapeDtypeStruct((width, span), BF16), jax.ShapeDtypeStruct((8, 128), BF16)]
        first_scratch = (2, width, span)
    out_shapes = (first_shapes + [jax.ShapeDtypeStruct((width, span // 2), BF16)] * 2) * 2
    outs = call(
        functools.partial(layer_kernel, sources, tiled),
        out_shapes,
        [SMEM, SMEM, VMEM] + [HBM] * (3 + sources),
        [HBM] * 8,
        [
            pltpu.VMEM((rows, hidden), BF16),
            pltpu.VMEM((width, rows), BF16),
            pltpu.VMEM((rows, hidden), BF16),
            weight_shape,
            pltpu.VMEM((rows, width), F32),
            pltpu.VMEM((2, 256, hidden), F32),
            pltpu.VMEM((rows, width), BF16),
            pltpu.VMEM((width, rows), BF16),
            pltpu.VMEM((rows, hidden), BF16),
            pltpu.VMEM(first_scratch, BF16),
            pltpu.VMEM((2, 2, width, span // 2), BF16),
            DMA((2, rows // 256)),
            DMA((count,)),
            DMA((4,)),
            DMA((2 * dom_size + 4,)),
        ],
        flops=6 * rows * width * hidden,
        moved=16 * rows * hidden,
    )(places, in_block, received, total, turned, cotangent, *weights[1])
    outs = list(outs)
    if not tiled:
        for at in (0, 4):
            term = outs[at].reshape(dom_size, depth, span)
            outs[at], outs[at + 1] = low_half(term, 1 - low), low_half(term, low)
    terms = [None] * 4
    for at in (0, 2, 1, 3):
        terms[at] = [outs[4 + at], swap(outs[at], "rep", 1)]
    first = added([*terms[1], swap(added(terms[0]), "dom", 1)])
    second = added([*terms[3], swap(added(terms[2]), "rep", parts)]).reshape(dom_size, depth, -1)
    first = reduce_high(first, high, parts // 2)
    second = exchanged(reduce_high(second, high, parts // 4), low_half, low, "dom", 1)
    both = jnp.concatenate([first, second], axis=2)
    summed = lax.dynamic_index_in_dim(both, place, 0, keepdims=False).astype(F32)
    for step in range(1, dom_size // 2):
        piece = lax.dynamic_index_in_dim(both, place ^ step, 0, keepdims=False)
        summed = summed + swap(piece, "dom", 2 * step).astype(F32)
    summed = summed.astype(BF16)
    size = summed.shape[1] // 2
    held = gather_high(jnp.stack([summed[:, :size], summed[:, size:]]), high)
    whole = jnp.concatenate([held[0], held[1]], axis=1)
    opposite = swap(whole, "rep", 1)
    return (
        jnp.where(core == 0, whole, opposite).astype(F32),
        jnp.where(core == 0, opposite, whole).astype(F32),
    )


def solution(mesh):
    in_specs = (
        P(("rep", "dom"), None),
        P(("rep", "dom"), None),
        P("dom", None),
        P("dom", None),
        P(("rep", "dom"), None, None),
        P(("rep", "dom")),
        P(("rep", "dom")),
        P(("rep", "dom")),
    )
    out_specs = (P("dom", None), P("dom", None))
    return jax.shard_map(shards, mesh=mesh, in_specs=in_specs, out_specs=out_specs, check_vma=False)
```

```python
import functools

import jax
import jax.numpy as jnp
from jax import lax
from jax.experimental import pallas as pl
from jax.experimental.pallas import tpu as pltpu
from jax.sharding import PartitionSpec as P

F32 = jnp.float32
BF16 = jnp.bfloat16
SCALE = 0.7978845608
CUBIC = 0.044715
MIB = 1 << 20
HBM = pl.BlockSpec(memory_space=pltpu.HBM)
SMEM = pl.BlockSpec(memory_space=pltpu.SMEM)
VMEM = pl.BlockSpec(memory_space=pltpu.VMEM)
DMA = pltpu.SemaphoreType.DMA


def swap(value, axis, step):
    size = lax.axis_size(axis)
    return lax.ppermute(value, axis, [(index, index ^ step) for index in range(size)])


def cross(value, step):
    reps, doms = lax.axis_size("rep"), lax.axis_size("dom")
    pairs = [
        (rep * doms + dom, rep * doms + (dom ^ step ^ (rep & 1))) for rep in range(reps) for dom in range(doms)
    ]
    return lax.ppermute(value, ("rep", "dom"), [(source, target) for source, target in pairs if source != target])


def split_copies(source, target, sems, count=4):
    size = source.shape[0] // count
    return [
        pltpu.make_async_copy(
            source.at[index * size : (index + 1) * size], target.at[index * size : (index + 1) * size], sems.at[index]
        )
        for index in range(count)
    ]


def slots_kernel(
    src_hbm, peer_hbm, tiles_hbm, features_hbm, out_hbm, src, peer, tiles, features, dense, out, in_sems, out_sems
):
    scalars = [
        pltpu.make_async_copy(src_hbm, src, in_sems.at[2, 0]),
        pltpu.make_async_copy(peer_hbm, peer, in_sems.at[2, 1]),
    ]
    tile_copies = split_copies(tiles_hbm, tiles, in_sems.at[0])
    feature_copies = split_copies(features_hbm, features, in_sems.at[1])
    for copy in scalars + tile_copies + feature_copies:
        copy.start()
    count, block, _ = tiles.shape
    dense[...] = jnp.zeros_like(dense)
    for copy in scalars + tile_copies:
        copy.wait()

    def place(tile, carry):
        row = pl.multiple_of(peer[tile] * block, block)
        column = pl.multiple_of(src[tile] * block, block)
        at = (pl.ds(row, block), pl.ds(column, block))
        dense[at] = dense[at] + tiles[tile].astype(F32)
        return carry

    lax.fori_loop(0, count, place, 0)
    for copy in feature_copies:
        copy.wait()
    chunk = 4 * block
    results = []
    for index in range(out.shape[0] // chunk):
        at = slice(index * chunk, (index + 1) * chunk)
        out[at, :] = jnp.dot(dense[at, :].astype(BF16), features[...], preferred_element_type=F32).astype(BF16)
        results.append(pltpu.make_async_copy(out.at[at, :], out_hbm.at[at, :], out_sems.at[index]))
        results[-1].start()
    for result in results:
        result.wait()


def weight_copies(flip, weight_hbms, weight, sems):
    sources = len(weight_hbms)
    copies = []
    for source, weight_hbm in enumerate(weight_hbms):
        for piece in range(weight_hbm.shape[0]):
            target = piece if sources == 1 else 2 * piece + (flip ^ source)
            copies.append(
                pltpu.make_async_copy(weight_hbm.at[piece], weight.at[target], sems.at[sources * piece + source])
            )
    return copies


def self_kernel(flip_ref, features_hbm, *refs):
    *weight_hbms, out_hbm, features, weight, out, feature_sems, weight_sems, out_sems = refs
    rows, width = features.shape
    hidden = out.shape[1]
    copies = weight_copies(flip_ref[0], weight_hbms, weight, weight_sems)
    copies += split_copies(features_hbm, features, feature_sems)
    for copy in copies:
        copy.start()
    for copy in copies:
        copy.wait()
    chunk = 256
    results = split_copies(out, out_hbm, out_sems, rows // chunk)
    for index, result in enumerate(results):
        at = slice(index * chunk, (index + 1) * chunk)
        out[at, :] = jnp.dot(
            features[at, :], weight[...].reshape(width, hidden), preferred_element_type=F32
        ).astype(BF16)
        result.start()
    for result in results:
        result.wait()


def layer_kernel(
    sources, pieces, places_ref, into_ref, slots_ref, total_hbm, features_hbm, cotangent_hbm, *refs
):
    weight_hbms, out_hbms = refs[:sources], refs[sources:-14]
    total, features, cotangent, weight, summed, values, aggregate, grad, first, second = refs[-14:-4]
    row_sems, weight_sems, feature_sems, out_sems = refs[-4:]
    senders, block, _ = slots_ref.shape
    rows, hidden = grad.shape
    width = aggregate.shape[1]
    core, flip, low, upper = [places_ref[index] for index in range(4)]
    chunk = 256
    parts = rows // chunk
    weights = weight_copies(flip, weight_hbms, weight, weight_sems)
    totals = split_copies(total_hbm, total, row_sems.at[0], parts)
    cotangents = split_copies(cotangent_hbm, cotangent, row_sems.at[1], parts)
    inputs = split_copies(features_hbm, features, feature_sems)
    for copy in weights + totals + cotangents + inputs:
        copy.start()

    summed[...] = jnp.zeros_like(summed)
    for sender in range(senders):
        at = pl.ds(pl.multiple_of(into_ref[sender] * block, block), block)
        summed[at, :] = summed[at, :] + slots_ref[sender].astype(F32)
    aggregate[...] = summed[...].astype(BF16)
    for copy in weights:
        copy.wait()
    span = hidden // 2

    def multiply(index):
        at = slice(index * chunk, (index + 1) * chunk)
        for begin in range(0, hidden, span):
            columns = slice(begin, begin + span)
            values[index % 2, :, columns] = jnp.dot(
                aggregate[at, :], weight[:, :, columns].reshape(width, span), preferred_element_type=F32
            )

    multiply(0)
    for index in range(parts):
        if index + 1 < parts:
            multiply(index + 1)
        totals[index].wait()
        cotangents[index].wait()
        for row in range(0, chunk, 32):
            at = slice(index * chunk + row, index * chunk + row + 32)
            for begin in range(0, hidden, span):
                columns = slice(begin, begin + span)
                value = values[index % 2, row : row + 32, columns] + total[at, columns].astype(F32)
                value = value.astype(BF16)
                square = value * value
                bend = jnp.tanh(value * (square * (SCALE * CUBIC) + SCALE))
                inner = value * (square * (1.5 * SCALE * CUBIC) + 0.5 * SCALE)
                grad[at, columns] = cotangent[at, columns] * ((1.0 + bend) * (inner * (1.0 - bend) + 0.5))

    for copy in inputs:
        copy.wait()
    results = []

    def send(source, target):
        results.append(pltpu.make_async_copy(source, target, out_sems.at[len(results)]))
        results[-1].start()

    contract = (((0,), (0,)), ((), ()))
    for index, operand in enumerate([features, aggregate]):
        product = lax.dot_general(operand[...], grad[:, :span], contract, preferred_element_type=F32)
        first[index] = product.astype(BF16).reshape(first.shape[1:])
    for term, which in enumerate([1 - core, core]):
        if pieces:
            for leave, bit in enumerate([1 - low, low]):
                for row in range(first.shape[1] // 2):
                    send(first.at[which, 2 * row + bit], out_hbms[4 * term + leave].at[row])
        else:
            send(first.at[which], out_hbms[4 * term])
    for index, operand in enumerate([features, aggregate]):
        product = lax.dot_general(operand[...], grad[:, span:], contract, preferred_element_type=F32).astype(BF16)
        for side in range(2):
            second[index, side] = product[:, side * span // 2 : (side + 1) * span // 2]
    for term, which in enumerate([1 - core, core]):
        for leave, bit in enumerate([1 - upper, upper]):
            send(second.at[which, bit], out_hbms[4 * term + 2 + leave])
    for result in results:
        result.wait()


def call(kernel, outs, places, out_places, scratch=(), flops=0, moved=0, vmem=56):
    return pl.pallas_call(
        kernel,
        out_shape=outs,
        in_specs=places,
        out_specs=out_places,
        scratch_shapes=list(scratch),
        compiler_params=pltpu.CompilerParams(vmem_limit_bytes=vmem * MIB),
        cost_estimate=pl.CostEstimate(flops=flops, bytes_accessed=moved, transcendentals=0),
    )


def joined(held, other, upper, axis):
    return jnp.stack([jnp.where(upper, other, held), jnp.where(upper, held, other)], axis=axis)


def gather_high(held, high):
    step = 1
    while step < lax.axis_size("rep") // 2:
        other = swap(held, "rep", 2 * step)
        upper = (high & step) != 0
        held = jnp.concatenate([jnp.where(upper, other, held), jnp.where(upper, held, other)], axis=-1)
        step *= 2
    return held


def added(terms):
    return sum(term.astype(F32) for term in terms).astype(BF16)


def half_of(value, axis, which):
    size = value.shape[axis] // 2
    return lax.dynamic_slice_in_dim(value, which * size, size, axis)


def low_half(term, which):
    return lax.dynamic_index_in_dim(term.reshape(-1, 2, *term.shape[1:]), which, 1, keepdims=False)


def column_half(term, which):
    size = term.shape[-1] // 2
    return lax.dynamic_slice_in_dim(term, which * size, size, term.ndim - 1)


def exchanged(term, take, which, axis, step):
    return added([take(term, which), swap(take(term, 1 - which), axis, step)])


def reduce_high(term, high, step):
    while step:
        term = exchanged(term, column_half, (high // step) % 2, "rep", 2 * step)
        step //= 2
    return term


def shards(features, cotangent, w_self, w_neigh, tile_vals, tile_src, tile_peer, in_block):
    dom_size = lax.axis_size("dom")
    rows, width = features.shape
    hidden = w_self.shape[1]
    block = tile_vals.shape[1]
    me = lax.axis_index("dom")
    rep = lax.axis_index("rep")
    parts = lax.axis_size("rep") // 2
    core, high = rep & 1, rep >> 1
    low, place = me & 1, me >> 1

    share = hidden // parts
    top = dom_size // 2
    held = jnp.stack([lax.dynamic_slice_in_dim(weight, high * share, share, 1) for weight in (w_self, w_neigh)])
    near, far = cross(held, 0), cross(held, top)
    slots = call(
        slots_kernel,
        jax.ShapeDtypeStruct((dom_size * block, width), BF16),
        [HBM] * 4,
        HBM,
        [
            pltpu.SMEM(tile_src.shape, jnp.int32),
            pltpu.SMEM(tile_peer.shape, jnp.int32),
            pltpu.VMEM(tile_vals.shape, BF16),
            pltpu.VMEM(features.shape, BF16),
            pltpu.VMEM((dom_size * block, rows), F32),
            pltpu.VMEM((dom_size * block, width), BF16),
            DMA((3, 4)),
            DMA((dom_size // 4,)),
        ],
        flops=2 * dom_size * block * rows * width,
        moved=tile_vals.size * 2 + rows * width * 4,
    )(tile_src, tile_peer, tile_vals, features)
    near, far, slots = lax.optimization_barrier((near, far, slots))
    held = joined(jnp.where(core == 0, held, near), far, (me & top) != 0, 1)
    step = top // 2
    while step > 1:
        held = joined(held, swap(held, "dom", step), (me & step) != 0, 2)
        held = held.reshape(2, -1, *held.shape[3:])
        step //= 2
    received = lax.all_to_all(slots.reshape(dom_size, block, width), "dom", split_axis=0, concat_axis=0, tiled=True)
    mine = gather_high(held, high)
    depth = width // dom_size
    tiled = depth % 16 == 0
    flip = low ^ core
    weights = [[mine[index], swap(mine[index], "rep", 1)] for index in range(2)]
    if not tiled:
        weights = [[joined(*weight, flip != 0, 1).reshape(-1, 128, hidden)] for weight in weights]
    sources, count = len(weights[0]), sum(weight.shape[0] for weight in weights[0])
    weight_shape = pltpu.VMEM((count, width // count, hidden), BF16)
    total = call(
        self_kernel,
        jax.ShapeDtypeStruct((rows, hidden), BF16),
        [SMEM] + [HBM] * (1 + sources),
        HBM,
        [
            pltpu.VMEM((rows, width), BF16),
            weight_shape,
            pltpu.VMEM((rows, hidden), BF16),
            DMA((4,)),
            DMA((count,)),
            DMA((rows // 256,)),
        ],
        flops=2 * rows * width * hidden,
        moved=7 * rows * hidden,
    )(flip.astype(jnp.int32).reshape(1), features, *weights[0])
    span = hidden // 2
    upper = (high // (parts // 2)) % 2
    places = jnp.stack([core, flip, low, upper]).astype(jnp.int32)
    if tiled:
        first_shapes = [jax.ShapeDtypeStruct((dom_size // 2, depth, span), BF16)] * 2
        first_scratch = (2, dom_size, depth, span)
    else:
        first_shapes = [jax.ShapeDtypeStruct((width, span), BF16), jax.ShapeDtypeStruct((8, 128), BF16)]
        first_scratch = (2, width, span)
    out_shapes = (first_shapes + [jax.ShapeDtypeStruct((width, span // 2), BF16)] * 2) * 2
    outs = call(
        functools.partial(layer_kernel, sources, tiled),
        out_shapes,
        [SMEM, SMEM, VMEM] + [HBM] * (3 + sources),
        [HBM] * 8,
        [
            pltpu.VMEM((rows, hidden), BF16),
            pltpu.VMEM((rows, width), BF16),
            pltpu.VMEM((rows, hidden), BF16),
            weight_shape,
            pltpu.VMEM((rows, width), F32),
            pltpu.VMEM((2, 256, hidden), F32),
            pltpu.VMEM((rows, width), BF16),
            pltpu.VMEM((rows, hidden), BF16),
            pltpu.VMEM(first_scratch, BF16),
            pltpu.VMEM((2, 2, width, span // 2), BF16),
            DMA((2, rows // 256)),
            DMA((count,)),
            DMA((4,)),
            DMA((2 * dom_size + 4,)),
        ],
        flops=6 * rows * width * hidden,
        moved=16 * rows * hidden,
    )(places, in_block, received, total, features, cotangent, *weights[1])
    outs = list(outs)
    if not tiled:
        for at in (0, 4):
            term = outs[at].reshape(dom_size, depth, span)
            outs[at], outs[at + 1] = low_half(term, 1 - low), low_half(term, low)
    terms = [None] * 4
    for at in (0, 2, 1, 3):
        terms[at] = [outs[4 + at], swap(outs[at], "rep", 1)]
    first = added([*terms[1], swap(added(terms[0]), "dom", 1)])
    second = added([*terms[3], swap(added(terms[2]), "rep", parts)]).reshape(dom_size, depth, -1)
    first = reduce_high(first, high, parts // 2)
    second = exchanged(reduce_high(second, high, parts // 4), low_half, low, "dom", 1)
    both = jnp.concatenate([first, second], axis=2)
    summed = lax.dynamic_index_in_dim(both, place, 0, keepdims=False).astype(F32)
    for step in range(1, dom_size // 2):
        piece = lax.dynamic_index_in_dim(both, place ^ step, 0, keepdims=False)
        summed = summed + swap(piece, "dom", 2 * step).astype(F32)
    summed = summed.astype(BF16)
    size = summed.shape[1] // 2
    held = gather_high(jnp.stack([summed[:, :size], summed[:, size:]]), high)
    whole = jnp.concatenate([held[0], held[1]], axis=1)
    opposite = swap(whole, "rep", 1)
    return (
        jnp.where(core == 0, whole, opposite).astype(F32),
        jnp.where(core == 0, opposite, whole).astype(F32),
    )


def solution(mesh):
    in_specs = (
        P(("rep", "dom"), None),
        P(("rep", "dom"), None),
        P("dom", None),
        P("dom", None),
        P(("rep", "dom"), None, None),
        P(("rep", "dom")),
        P(("rep", "dom")),
        P(("rep", "dom")),
    )
    out_specs = (P("dom", None), P("dom", None))
    return jax.shard_map(shards, mesh=mesh, in_specs=in_specs, out_specs=out_specs, check_vma=False)
```

```python
import functools

import jax
import jax.numpy as jnp
from jax import lax
from jax.experimental import pallas as pl
from jax.experimental.pallas import tpu as pltpu
from jax.sharding import PartitionSpec as P

F32 = jnp.float32
BF16 = jnp.bfloat16
SCALE = 0.7978845608
CUBIC = 0.044715
MIB = 1 << 20
HBM = pl.BlockSpec(memory_space=pltpu.HBM)
SMEM = pl.BlockSpec(memory_space=pltpu.SMEM)
VMEM = pl.BlockSpec(memory_space=pltpu.VMEM)
DMA = pltpu.SemaphoreType.DMA


def swap(value, axis, step):
    size = lax.axis_size(axis)
    return lax.ppermute(value, axis, [(index, index ^ step) for index in range(size)])


def cross(value, step):
    reps, doms = lax.axis_size("rep"), lax.axis_size("dom")
    pairs = [
        (rep * doms + dom, rep * doms + (dom ^ step ^ (rep & 1))) for rep in range(reps) for dom in range(doms)
    ]
    return lax.ppermute(value, ("rep", "dom"), [(source, target) for source, target in pairs if source != target])


def split_copies(source, target, sems, count=4):
    size = source.shape[0] // count
    return [
        pltpu.make_async_copy(
            source.at[index * size : (index + 1) * size], target.at[index * size : (index + 1) * size], sems.at[index]
        )
        for index in range(count)
    ]


def slots_kernel(
    src_hbm, peer_hbm, tiles_hbm, features_hbm, out_hbm, src, peer, tiles, features, dense, out, in_sems, out_sems
):
    scalars = [
        pltpu.make_async_copy(src_hbm, src, in_sems.at[2, 0]),
        pltpu.make_async_copy(peer_hbm, peer, in_sems.at[2, 1]),
    ]
    tile_copies = split_copies(tiles_hbm, tiles, in_sems.at[0])
    feature_copies = split_copies(features_hbm, features, in_sems.at[1])
    for copy in scalars + tile_copies + feature_copies:
        copy.start()
    count, block, _ = tiles.shape
    dense[...] = jnp.zeros_like(dense)
    for copy in scalars + tile_copies:
        copy.wait()

    def place(tile, carry):
        row = pl.multiple_of(peer[tile] * block, block)
        column = pl.multiple_of(src[tile] * block, block)
        at = (pl.ds(row, block), pl.ds(column, block))
        dense[at] = dense[at] + tiles[tile].astype(F32)
        return carry

    lax.fori_loop(0, count, place, 0)
    for copy in feature_copies:
        copy.wait()
    chunk = 4 * block
    results = []
    for index in range(out.shape[0] // chunk):
        at = slice(index * chunk, (index + 1) * chunk)
        out[at, :] = jnp.dot(dense[at, :].astype(BF16), features[...], preferred_element_type=F32).astype(BF16)
        results.append(pltpu.make_async_copy(out.at[at, :], out_hbm.at[at, :], out_sems.at[index]))
        results[-1].start()
    for result in results:
        result.wait()


def weight_copies(flip, weight_hbms, weight, sems):
    sources = len(weight_hbms)
    copies = []
    for source, weight_hbm in enumerate(weight_hbms):
        for piece in range(weight_hbm.shape[0]):
            target = piece if sources == 1 else 2 * piece + (flip ^ source)
            copies.append(
                pltpu.make_async_copy(weight_hbm.at[piece], weight.at[target], sems.at[sources * piece + source])
            )
    return copies


def self_kernel(flip_ref, features_hbm, *refs):
    *weight_hbms, out_hbm, features, weight, out, feature_sems, weight_sems, out_sems = refs
    rows, width = features.shape
    hidden = out.shape[1]
    copies = weight_copies(flip_ref[0], weight_hbms, weight, weight_sems)
    copies += split_copies(features_hbm, features, feature_sems)
    for copy in copies:
        copy.start()
    for copy in copies:
        copy.wait()
    chunk = 256
    results = split_copies(out, out_hbm, out_sems, rows // chunk)
    for index, result in enumerate(results):
        at = slice(index * chunk, (index + 1) * chunk)
        out[at, :] = jnp.dot(
            features[at, :], weight[...].reshape(width, hidden), preferred_element_type=F32
        ).astype(BF16)
        result.start()
    for result in results:
        result.wait()


def layer_kernel(
    sources, pieces, places_ref, into_ref, slots_ref, total_hbm, features_hbm, cotangent_hbm, *refs
):
    weight_hbms, out_hbms = refs[:sources], refs[sources:-15]
    total, features, cotangent, weight, summed, values, aggregate, grad, turned, first, second = refs[-15:-4]
    row_sems, weight_sems, feature_sems, out_sems = refs[-4:]
    senders, block, _ = slots_ref.shape
    rows, hidden = grad.shape
    width = aggregate.shape[1]
    core, flip, low, upper = [places_ref[index] for index in range(4)]
    chunk = 256
    parts = rows // chunk
    weights = weight_copies(flip, weight_hbms, weight, weight_sems)
    totals = split_copies(total_hbm, total, row_sems.at[0], parts)
    cotangents = split_copies(cotangent_hbm, cotangent, row_sems.at[1], parts)
    inputs = split_copies(features_hbm, features, feature_sems)
    for copy in weights + totals + cotangents + inputs:
        copy.start()

    summed[...] = jnp.zeros_like(summed)
    for sender in range(senders):
        at = pl.ds(pl.multiple_of(into_ref[sender] * block, block), block)
        summed[at, :] = summed[at, :] + slots_ref[sender].astype(F32)
    aggregate[...] = summed[...].astype(BF16)
    for copy in weights:
        copy.wait()
    span = hidden // 2

    contract = (((0,), (0,)), ((), ()))

    def multiply(half, index):
        at, columns = slice(index * chunk, (index + 1) * chunk), slice(half * span, (half + 1) * span)
        values[at, columns] = jnp.dot(
            aggregate[at, :], weight[:, :, columns].reshape(width, span), preferred_element_type=F32
        )

    def slope(half, row):
        at, columns = slice(row, row + 32), slice(half * span, (half + 1) * span)
        value = (values[at, columns] + total[at, columns].astype(F32)).astype(BF16)
        square = value * value
        bend = jnp.tanh(value * (square * (SCALE * CUBIC) + SCALE))
        inner = value * (square * (1.5 * SCALE * CUBIC) + 0.5 * SCALE)
        grad[at, columns] = cotangent[at, columns] * ((1.0 + bend) * (inner * (1.0 - bend) + 0.5))

    def first_term(index, operand, begin):
        product = lax.dot_general(
            operand[:, begin : begin + chunk], grad[:, :span], contract, preferred_element_type=F32
        )
        turned[index, begin : begin + chunk, :] = product.astype(BF16)

    def in_turn(steps, half):
        done = 0
        for index, step in enumerate(steps):
            step()
            until = (index + 1) * rows // len(steps) // 32 * 32
            for row in range(done, until, 32):
                slope(half, row)
            done = until

    for index in range(parts):
        multiply(0, index)
    for copy in totals + cotangents:
        copy.wait()
    in_turn([functools.partial(multiply, 1, index) for index in range(parts)], 0)
    for copy in inputs:
        copy.wait()
    in_turn(
        [
            functools.partial(first_term, index, operand, begin)
            for index, operand in enumerate([features, aggregate])
            for begin in range(0, width, chunk)
        ],
        1,
    )
    results = []

    def send(source, target):
        results.append(pltpu.make_async_copy(source, target, out_sems.at[len(results)]))
        results[-1].start()

    for index in range(2):
        first[index] = turned[index].reshape(first.shape[1:])
    for term, which in enumerate([1 - core, core]):
        if pieces:
            for leave, bit in enumerate([1 - low, low]):
                for row in range(first.shape[1] // 2):
                    send(first.at[which, 2 * row + bit], out_hbms[4 * term + leave].at[row])
        else:
            send(first.at[which], out_hbms[4 * term])
    for index, operand in enumerate([features, aggregate]):
        product = lax.dot_general(operand[...], grad[:, span:], contract, preferred_element_type=F32).astype(BF16)
        for side in range(2):
            second[index, side] = product[:, side * span // 2 : (side + 1) * span // 2]
    for term, which in enumerate([1 - core, core]):
        for leave, bit in enumerate([1 - upper, upper]):
            send(second.at[which, bit], out_hbms[4 * term + 2 + leave])
    for result in results:
        result.wait()


def call(kernel, outs, places, out_places, scratch=(), flops=0, moved=0, vmem=40):
    return pl.pallas_call(
        kernel,
        out_shape=outs,
        in_specs=places,
        out_specs=out_places,
        scratch_shapes=list(scratch),
        compiler_params=pltpu.CompilerParams(vmem_limit_bytes=vmem * MIB),
        cost_estimate=pl.CostEstimate(flops=flops, bytes_accessed=moved, transcendentals=0),
    )


def joined(held, other, upper, axis):
    return jnp.stack([jnp.where(upper, other, held), jnp.where(upper, held, other)], axis=axis)


def gather_high(held, high):
    step = 1
    while step < lax.axis_size("rep") // 2:
        other = swap(held, "rep", 2 * step)
        upper = (high & step) != 0
        held = jnp.concatenate([jnp.where(upper, other, held), jnp.where(upper, held, other)], axis=-1)
        step *= 2
    return held


def added(terms):
    return sum(term.astype(F32) for term in terms).astype(BF16)


def half_of(value, axis, which):
    size = value.shape[axis] // 2
    return lax.dynamic_slice_in_dim(value, which * size, size, axis)


def low_half(term, which):
    return lax.dynamic_index_in_dim(term.reshape(-1, 2, *term.shape[1:]), which, 1, keepdims=False)


def column_half(term, which):
    size = term.shape[-1] // 2
    return lax.dynamic_slice_in_dim(term, which * size, size, term.ndim - 1)


def exchanged(term, take, which, axis, step):
    return added([take(term, which), swap(take(term, 1 - which), axis, step)])


def reduce_high(term, high, step):
    while step:
        term = exchanged(term, column_half, (high // step) % 2, "rep", 2 * step)
        step //= 2
    return term


def shards(features, cotangent, w_self, w_neigh, tile_vals, tile_src, tile_peer, in_block):
    dom_size = lax.axis_size("dom")
    rows, width = features.shape
    hidden = w_self.shape[1]
    block = tile_vals.shape[1]
    me = lax.axis_index("dom")
    rep = lax.axis_index("rep")
    parts = lax.axis_size("rep") // 2
    core, high = rep & 1, rep >> 1
    low, place = me & 1, me >> 1

    share = hidden // parts
    top = dom_size // 2
    held = jnp.stack([lax.dynamic_slice_in_dim(weight, high * share, share, 1) for weight in (w_self, w_neigh)])
    near, far = cross(held, 0), cross(held, top)
    slots = call(
        slots_kernel,
        jax.ShapeDtypeStruct((dom_size * block, width), BF16),
        [HBM] * 4,
        HBM,
        [
            pltpu.SMEM(tile_src.shape, jnp.int32),
            pltpu.SMEM(tile_peer.shape, jnp.int32),
            pltpu.VMEM(tile_vals.shape, BF16),
            pltpu.VMEM(features.shape, BF16),
            pltpu.VMEM((dom_size * block, rows), F32),
            pltpu.VMEM((dom_size * block, width), BF16),
            DMA((3, 4)),
            DMA((dom_size // 4,)),
        ],
        flops=2 * dom_size * block * rows * width,
        moved=tile_vals.size * 2 + rows * width * 4,
        vmem=56,
    )(tile_src, tile_peer, tile_vals, features)
    near, far, slots = lax.optimization_barrier((near, far, slots))
    held = joined(jnp.where(core == 0, held, near), far, (me & top) != 0, 1)
    step = top // 2
    while step > 1:
        held = joined(held, swap(held, "dom", step), (me & step) != 0, 2)
        held = held.reshape(2, -1, *held.shape[3:])
        step //= 2
    received = lax.all_to_all(slots.reshape(dom_size, block, width), "dom", split_axis=0, concat_axis=0, tiled=True)
    mine = gather_high(held, high)
    depth = width // dom_size
    tiled = depth % 16 == 0
    flip = low ^ core
    weights = [[mine[index], swap(mine[index], "rep", 1)] for index in range(2)]
    if not tiled:
        weights = [[joined(*weight, flip != 0, 1).reshape(-1, 128, hidden)] for weight in weights]
    sources, count = len(weights[0]), sum(weight.shape[0] for weight in weights[0])
    weight_shape = pltpu.VMEM((count, width // count, hidden), BF16)
    total = call(
        self_kernel,
        jax.ShapeDtypeStruct((rows, hidden), BF16),
        [SMEM] + [HBM] * (1 + sources),
        HBM,
        [
            pltpu.VMEM((rows, width), BF16),
            weight_shape,
            pltpu.VMEM((rows, hidden), BF16),
            DMA((4,)),
            DMA((count,)),
            DMA((rows // 256,)),
        ],
        flops=2 * rows * width * hidden,
        moved=7 * rows * hidden,
    )(flip.astype(jnp.int32).reshape(1), features, *weights[0])
    span = hidden // 2
    upper = (high // (parts // 2)) % 2
    places = jnp.stack([core, flip, low, upper]).astype(jnp.int32)
    if tiled:
        first_shapes = [jax.ShapeDtypeStruct((dom_size // 2, depth, span), BF16)] * 2
        first_scratch = (2, dom_size, depth, span)
    else:
        first_shapes = [jax.ShapeDtypeStruct((width, span), BF16), jax.ShapeDtypeStruct((8, 128), BF16)]
        first_scratch = (2, width, span)
    out_shapes = (first_shapes + [jax.ShapeDtypeStruct((width, span // 2), BF16)] * 2) * 2
    outs = call(
        functools.partial(layer_kernel, sources, tiled),
        out_shapes,
        [SMEM, SMEM, VMEM] + [HBM] * (3 + sources),
        [HBM] * 8,
        [
            pltpu.VMEM((rows, hidden), BF16),
            pltpu.VMEM((rows, width), BF16),
            pltpu.VMEM((rows, hidden), BF16),
            weight_shape,
            pltpu.VMEM((rows, width), F32),
            pltpu.VMEM((rows, hidden), F32),
            pltpu.VMEM((rows, width), BF16),
            pltpu.VMEM((rows, hidden), BF16),
            pltpu.VMEM((2, width, span), BF16),
            pltpu.VMEM(first_scratch, BF16),
            pltpu.VMEM((2, 2, width, span // 2), BF16),
            DMA((2, rows // 256)),
            DMA((count,)),
            DMA((4,)),
            DMA((2 * dom_size + 4,)),
        ],
        flops=6 * rows * width * hidden,
        moved=16 * rows * hidden,
    )(places, in_block, received, total, features, cotangent, *weights[1])
    outs = list(outs)
    if not tiled:
        for at in (0, 4):
            term = outs[at].reshape(dom_size, depth, span)
            outs[at], outs[at + 1] = low_half(term, 1 - low), low_half(term, low)
    terms = [None] * 4
    for at in (0, 2, 1, 3):
        terms[at] = [outs[4 + at], swap(outs[at], "rep", 1)]
    first, second = lax.optimization_barrier((added(terms[0]), added(terms[2])))
    first = added([*terms[1], swap(first, "dom", 1)])
    second = added([*terms[3], swap(second, "rep", parts)]).reshape(dom_size, depth, -1)
    first = reduce_high(first, high, parts // 2)
    second = exchanged(reduce_high(second, high, parts // 4), low_half, low, "dom", 1)
    both = jnp.concatenate([first, second], axis=2)
    summed = lax.dynamic_index_in_dim(both, place, 0, keepdims=False).astype(F32)
    for step in range(1, dom_size // 2):
        piece = lax.dynamic_index_in_dim(both, place ^ step, 0, keepdims=False)
        summed = summed + swap(piece, "dom", 2 * step).astype(F32)
    summed = summed.astype(BF16)
    size = summed.shape[1] // 2
    held = gather_high(jnp.stack([summed[:, :size], summed[:, size:]]), high)
    whole = jnp.concatenate([held[0], held[1]], axis=1)
    opposite = swap(whole, "rep", 1)
    return (
        jnp.where(core == 0, whole, opposite).astype(F32),
        jnp.where(core == 0, opposite, whole).astype(F32),
    )


def solution(mesh):
    in_specs = (
        P(("rep", "dom"), None),
        P(("rep", "dom"), None),
        P("dom", None),
        P("dom", None),
        P(("rep", "dom"), None, None),
        P(("rep", "dom")),
        P(("rep", "dom")),
        P(("rep", "dom")),
    )
    out_specs = (P("dom", None), P("dom", None))
    return jax.shard_map(shards, mesh=mesh, in_specs=in_specs, out_specs=out_specs, check_vma=False)
```

```python
import functools

import jax
import jax.numpy as jnp
from jax import lax
from jax.experimental import pallas as pl
from jax.experimental.pallas import tpu as pltpu
from jax.sharding import PartitionSpec as P

F32 = jnp.float32
BF16 = jnp.bfloat16
SCALE = 0.7978845608
CUBIC = 0.044715
MIB = 1 << 20
HBM = pl.BlockSpec(memory_space=pltpu.HBM)
SMEM = pl.BlockSpec(memory_space=pltpu.SMEM)
VMEM = pl.BlockSpec(memory_space=pltpu.VMEM)
DMA = pltpu.SemaphoreType.DMA


def swap(value, axis, step):
    size = lax.axis_size(axis)
    return lax.ppermute(value, axis, [(index, index ^ step) for index in range(size)])


def cross(value, step):
    reps, doms = lax.axis_size("rep"), lax.axis_size("dom")
    pairs = [
        (rep * doms + dom, rep * doms + (dom ^ step ^ (rep & 1))) for rep in range(reps) for dom in range(doms)
    ]
    return lax.ppermute(value, ("rep", "dom"), [(source, target) for source, target in pairs if source != target])


def split_copies(source, target, sems, count=4):
    size = source.shape[0] // count
    return [
        pltpu.make_async_copy(
            source.at[index * size : (index + 1) * size], target.at[index * size : (index + 1) * size], sems.at[index]
        )
        for index in range(count)
    ]


def slots_kernel(
    src_hbm, peer_hbm, tiles_hbm, features_hbm, out_hbm, src, peer, tiles, features, dense, out, in_sems, out_sems
):
    scalars = [
        pltpu.make_async_copy(src_hbm, src, in_sems.at[2, 0]),
        pltpu.make_async_copy(peer_hbm, peer, in_sems.at[2, 1]),
    ]
    tile_copies = split_copies(tiles_hbm, tiles, in_sems.at[0])
    feature_copies = split_copies(features_hbm, features, in_sems.at[1])
    for copy in scalars + tile_copies + feature_copies:
        copy.start()
    count, block, _ = tiles.shape
    dense[...] = jnp.zeros_like(dense)
    for copy in scalars + tile_copies:
        copy.wait()

    def place(tile, carry):
        row = pl.multiple_of(peer[tile] * block, block)
        column = pl.multiple_of(src[tile] * block, block)
        at = (pl.ds(row, block), pl.ds(column, block))
        dense[at] = dense[at] + tiles[tile].astype(F32)
        return carry

    lax.fori_loop(0, count, place, 0)
    for copy in feature_copies:
        copy.wait()
    chunk = 4 * block
    results = []
    for index in range(out.shape[0] // chunk):
        at = slice(index * chunk, (index + 1) * chunk)
        out[at, :] = jnp.dot(dense[at, :].astype(BF16), features[...], preferred_element_type=F32).astype(BF16)
        results.append(pltpu.make_async_copy(out.at[at, :], out_hbm.at[at, :], out_sems.at[index]))
        results[-1].start()
    for result in results:
        result.wait()


def weight_copies(flip, weight_hbms, weight, sems):
    sources = len(weight_hbms)
    copies = []
    for source, weight_hbm in enumerate(weight_hbms):
        for piece in range(weight_hbm.shape[0]):
            target = piece if sources == 1 else 2 * piece + (flip ^ source)
            copies.append(
                pltpu.make_async_copy(weight_hbm.at[piece], weight.at[target], sems.at[sources * piece + source])
            )
    return copies


def self_kernel(flip_ref, features_hbm, *refs):
    *weight_hbms, out_hbm, features, weight, out, feature_sems, weight_sems, out_sems = refs
    rows, width = features.shape
    hidden = out.shape[1]
    copies = weight_copies(flip_ref[0], weight_hbms, weight, weight_sems)
    copies += split_copies(features_hbm, features, feature_sems)
    for copy in copies:
        copy.start()
    for copy in copies:
        copy.wait()
    chunk = 256
    results = split_copies(out, out_hbm, out_sems, rows // chunk)
    for index, result in enumerate(results):
        at = slice(index * chunk, (index + 1) * chunk)
        out[at, :] = jnp.dot(
            features[at, :], weight[...].reshape(width, hidden), preferred_element_type=F32
        ).astype(BF16)
        result.start()
    for result in results:
        result.wait()


def layer_kernel(
    sources, pieces, places_ref, into_ref, slots_ref, total_hbm, features_hbm, cotangent_hbm, *refs
):
    weight_hbms, out_hbms = refs[:sources], refs[sources:-13]
    total, features, cotangent, weight, summed, values, aggregate, grad, both = refs[-13:-4]
    row_sems, weight_sems, feature_sems, out_sems = refs[-4:]
    senders, block, _ = slots_ref.shape
    rows, hidden = grad.shape
    width = aggregate.shape[1]
    core, flip, low, upper = [places_ref[index] for index in range(4)]
    chunk = 256
    parts = rows // chunk
    weights = weight_copies(flip, weight_hbms, weight, weight_sems)
    totals = split_copies(total_hbm, total, row_sems.at[0], parts)
    cotangents = split_copies(cotangent_hbm, cotangent, row_sems.at[1], parts)
    inputs = split_copies(features_hbm, features, feature_sems)
    for copy in weights + totals + cotangents + inputs:
        copy.start()

    summed[...] = jnp.zeros_like(summed)
    for sender in range(senders):
        at = pl.ds(pl.multiple_of(into_ref[sender] * block, block), block)
        summed[at, :] = summed[at, :] + slots_ref[sender].astype(F32)
    aggregate[...] = summed[...].astype(BF16)
    for copy in weights:
        copy.wait()
    span = hidden // 2

    def multiply(index):
        at = slice(index * chunk, (index + 1) * chunk)
        for begin in range(0, hidden, span):
            columns = slice(begin, begin + span)
            values[index % 2, :, columns] = jnp.dot(
                aggregate[at, :], weight[:, :, columns].reshape(width, span), preferred_element_type=F32
            )

    multiply(0)
    for index in range(parts):
        if index + 1 < parts:
            multiply(index + 1)
        totals[index].wait()
        cotangents[index].wait()
        for row in range(0, chunk, 32):
            at = slice(index * chunk + row, index * chunk + row + 32)
            for begin in range(0, hidden, span):
                columns = slice(begin, begin + span)
                value = values[index % 2, row : row + 32, columns] + total[at, columns].astype(F32)
                value = value.astype(BF16)
                square = value * value
                bend = jnp.tanh(value * (square * (SCALE * CUBIC) + SCALE))
                inner = value * (square * (1.5 * SCALE * CUBIC) + 0.5 * SCALE)
                grad[at, columns] = cotangent[at, columns] * ((1.0 + bend) * (inner * (1.0 - bend) + 0.5))

    for copy in inputs:
        copy.wait()
    moves = []
    for term, which in enumerate([1 - core, core]):
        for index, target in enumerate(out_hbms[2 * term : 2 * term + 2]):
            if not pieces:
                moves.append((index, both.at[index, which], target))
                continue
            row_bit, column_bit = (low, upper) if index else (1 - low, 1 - upper)
            for row in range(target.shape[0]):
                for side in range(2):
                    half = jnp.where(which == 0, side, column_bit)
                    place = 2 * row + jnp.where(which == 0, row_bit, side)
                    columns = slice(side * span, (side + 1) * span)
                    moves.append((half, both.at[half, which, place], target.at[row, :, columns]))
    contract = (((0,), (0,)), ((), ()))
    results = [
        pltpu.make_async_copy(source, target, out_sems.at[index]) for index, (_, source, target) in enumerate(moves)
    ]
    for half in range(2):
        columns = slice(half * span, (half + 1) * span)
        for index, operand in enumerate([features, aggregate]):
            product = lax.dot_general(operand[...], grad[:, columns], contract, preferred_element_type=F32)
            both[half, index] = product.astype(BF16).reshape(both.shape[2:])
        for move, result in zip(moves, results):
            pl.when(move[0] == half)(result.start)
    for result in results:
        result.wait()


def call(kernel, outs, places, out_places, scratch=(), flops=0, moved=0, vmem=56):
    return pl.pallas_call(
        kernel,
        out_shape=outs,
        in_specs=places,
        out_specs=out_places,
        scratch_shapes=list(scratch),
        compiler_params=pltpu.CompilerParams(vmem_limit_bytes=vmem * MIB),
        cost_estimate=pl.CostEstimate(flops=flops, bytes_accessed=moved, transcendentals=0),
    )


def joined(held, other, upper, axis):
    return jnp.stack([jnp.where(upper, other, held), jnp.where(upper, held, other)], axis=axis)


def gather_high(held, high):
    step = 1
    while step < lax.axis_size("rep") // 2:
        other = swap(held, "rep", 2 * step)
        upper = (high & step) != 0
        held = jnp.concatenate([jnp.where(upper, other, held), jnp.where(upper, held, other)], axis=-1)
        step *= 2
    return held


def added(terms):
    return sum(term.astype(F32) for term in terms).astype(BF16)


def half_of(value, axis, which):
    size = value.shape[axis] // 2
    return lax.dynamic_slice_in_dim(value, which * size, size, axis)


def first_pieces(term, depth, core, low, upper):
    term = term.reshape(-1, 2, depth, 2, term.shape[1] // 2)
    pieces = []
    for row_bit, column_bit in ((1 - low, 1 - upper), (low, upper)):
        rows = lax.dynamic_index_in_dim(term, row_bit, 1, keepdims=False)
        columns = lax.dynamic_index_in_dim(term, column_bit, 3, keepdims=False).swapaxes(1, 2)
        pieces.append(jnp.where(core == 0, rows, columns).reshape(term.shape[0], depth, -1))
    return pieces


def turn_swap(value, turn):
    reps, doms = lax.axis_size("rep"), lax.axis_size("dom")
    pairs = []
    for rep in range(reps):
        for dom in range(doms):
            target = rep * doms + (dom ^ 1) if rep % 2 == turn else (rep ^ (reps // 2)) * doms + dom
            pairs.append((rep * doms + dom, target))
    return lax.ppermute(value, ("rep", "dom"), pairs)


def column_half(term, which):
    size = term.shape[-1] // 2
    return lax.dynamic_slice_in_dim(term, which * size, size, term.ndim - 1)


def exchanged(term, take, which, axis, step):
    return added([take(term, which), swap(take(term, 1 - which), axis, step)])


def reduce_high(term, high, step):
    while step:
        term = exchanged(term, column_half, (high // step) % 2, "rep", 2 * step)
        step //= 2
    return term


def shards(features, cotangent, w_self, w_neigh, tile_vals, tile_src, tile_peer, in_block):
    dom_size = lax.axis_size("dom")
    rows, width = features.shape
    hidden = w_self.shape[1]
    block = tile_vals.shape[1]
    me = lax.axis_index("dom")
    rep = lax.axis_index("rep")
    parts = lax.axis_size("rep") // 2
    core, high = rep & 1, rep >> 1
    low, place = me & 1, me >> 1

    share = hidden // parts
    top = dom_size // 2
    held = jnp.stack([lax.dynamic_slice_in_dim(weight, high * share, share, 1) for weight in (w_self, w_neigh)])
    near, far = cross(held, 0), cross(held, top)
    slots = call(
        slots_kernel,
        jax.ShapeDtypeStruct((dom_size * block, width), BF16),
        [HBM] * 4,
        HBM,
        [
            pltpu.SMEM(tile_src.shape, jnp.int32),
            pltpu.SMEM(tile_peer.shape, jnp.int32),
            pltpu.VMEM(tile_vals.shape, BF16),
            pltpu.VMEM(features.shape, BF16),
            pltpu.VMEM((dom_size * block, rows), F32),
            pltpu.VMEM((dom_size * block, width), BF16),
            DMA((3, 4)),
            DMA((dom_size // 4,)),
        ],
        flops=2 * dom_size * block * rows * width,
        moved=tile_vals.size * 2 + rows * width * 4,
    )(tile_src, tile_peer, tile_vals, features)
    near, far, slots = lax.optimization_barrier((near, far, slots))
    held = joined(jnp.where(core == 0, held, near), far, (me & top) != 0, 1)
    step = top // 2
    while step > 1:
        held = joined(held, swap(held, "dom", step), (me & step) != 0, 2)
        held = held.reshape(2, -1, *held.shape[3:])
        step //= 2
    received = lax.all_to_all(slots.reshape(dom_size, block, width), "dom", split_axis=0, concat_axis=0, tiled=True)
    mine = gather_high(held, high)
    depth = width // dom_size
    tiled = depth % 16 == 0
    flip = low ^ core
    weights = [[mine[index], swap(mine[index], "rep", 1)] for index in range(2)]
    if not tiled:
        weights = [[joined(*weight, flip != 0, 1).reshape(-1, 128, hidden)] for weight in weights]
    sources, count = len(weights[0]), sum(weight.shape[0] for weight in weights[0])
    weight_shape = pltpu.VMEM((count, width // count, hidden), BF16)
    total = call(
        self_kernel,
        jax.ShapeDtypeStruct((rows, hidden), BF16),
        [SMEM] + [HBM] * (1 + sources),
        HBM,
        [
            pltpu.VMEM((rows, width), BF16),
            weight_shape,
            pltpu.VMEM((rows, hidden), BF16),
            DMA((4,)),
            DMA((count,)),
            DMA((rows // 256,)),
        ],
        flops=2 * rows * width * hidden,
        moved=7 * rows * hidden,
    )(flip.astype(jnp.int32).reshape(1), features, *weights[0])
    span = hidden // 2
    upper = (high // (parts // 2)) % 2
    places = jnp.stack([core, flip, low, upper]).astype(jnp.int32)
    if tiled:
        out_shapes = [jax.ShapeDtypeStruct((dom_size // 2, depth, hidden), BF16)] * 4
        product_shape = (2, 2, dom_size, depth, span)
    else:
        out_shapes = [jax.ShapeDtypeStruct((width, span), BF16)] * 4
        product_shape = (2, 2, width, span)
    outs = call(
        functools.partial(layer_kernel, sources, tiled),
        out_shapes,
        [SMEM, SMEM, VMEM] + [HBM] * (3 + sources),
        [HBM] * 4,
        [
            pltpu.VMEM((rows, hidden), BF16),
            pltpu.VMEM((rows, width), BF16),
            pltpu.VMEM((rows, hidden), BF16),
            weight_shape,
            pltpu.VMEM((rows, width), F32),
            pltpu.VMEM((2, 256, hidden), F32),
            pltpu.VMEM((rows, width), BF16),
            pltpu.VMEM((rows, hidden), BF16),
            pltpu.VMEM(product_shape, BF16),
            DMA((2, rows // 256)),
            DMA((count,)),
            DMA((4,)),
            DMA((4 * dom_size,)),
        ],
        flops=6 * rows * width * hidden,
        moved=16 * rows * hidden,
    )(places, in_block, received, total, features, cotangent, *weights[1])
    sent, kept = outs[:2], outs[2:]
    if not tiled:
        sent, kept = [
            first_pieces(jnp.concatenate(pair, axis=1), depth, which, low, upper)
            for pair, which in ((sent, 1 - core), (kept, core))
        ]
    leave, stay = [[own, swap(piece, "rep", 1)] for own, piece in zip(kept, sent)]
    held = added([*stay, turn_swap(added(leave), 0)])
    bit = jnp.where(core == 0, upper, low)
    held = added([column_half(held, bit), turn_swap(column_half(held, 1 - bit), 1)])
    both = reduce_high(held, high, parts // 4)
    summed = lax.dynamic_index_in_dim(both, place, 0, keepdims=False).astype(F32)
    for step in range(1, dom_size // 2):
        piece = lax.dynamic_index_in_dim(both, place ^ step, 0, keepdims=False)
        summed = summed + swap(piece, "dom", 2 * step).astype(F32)
    summed = summed.astype(BF16)
    whole = gather_high(summed, high)
    opposite = swap(whole, "rep", 1)
    return (
        jnp.where(core == 0, whole, opposite).astype(F32),
        jnp.where(core == 0, opposite, whole).astype(F32),
    )


def solution(mesh):
    in_specs = (
        P(("rep", "dom"), None),
        P(("rep", "dom"), None),
        P("dom", None),
        P("dom", None),
        P(("rep", "dom"), None, None),
        P(("rep", "dom")),
        P(("rep", "dom")),
        P(("rep", "dom")),
    )
    out_specs = (P("dom", None), P("dom", None))
    return jax.shard_map(shards, mesh=mesh, in_specs=in_specs, out_specs=out_specs, check_vma=False)
```

```python
import functools

import jax
import jax.numpy as jnp
from jax import lax
from jax.experimental import pallas as pl
from jax.experimental.pallas import tpu as pltpu
from jax.sharding import PartitionSpec as P

F32 = jnp.float32
BF16 = jnp.bfloat16
SCALE = 0.7978845608
CUBIC = 0.044715
MIB = 1 << 20
HBM = pl.BlockSpec(memory_space=pltpu.HBM)
SMEM = pl.BlockSpec(memory_space=pltpu.SMEM)
VMEM = pl.BlockSpec(memory_space=pltpu.VMEM)
DMA = pltpu.SemaphoreType.DMA


def swap(value, axis, step):
    size = lax.axis_size(axis)
    return lax.ppermute(value, axis, [(index, index ^ step) for index in range(size)])


def cross(value, step):
    reps, doms = lax.axis_size("rep"), lax.axis_size("dom")
    pairs = [
        (rep * doms + dom, rep * doms + (dom ^ step ^ (rep & 1))) for rep in range(reps) for dom in range(doms)
    ]
    return lax.ppermute(value, ("rep", "dom"), [(source, target) for source, target in pairs if source != target])


def split_copies(source, target, sems, count=4):
    size = source.shape[0] // count
    return [
        pltpu.make_async_copy(
            source.at[index * size : (index + 1) * size], target.at[index * size : (index + 1) * size], sems.at[index]
        )
        for index in range(count)
    ]


def slots_kernel(
    src_hbm, peer_hbm, tiles_hbm, features_hbm, out_hbm, src, peer, tiles, features, dense, out, in_sems, out_sems
):
    scalars = [
        pltpu.make_async_copy(src_hbm, src, in_sems.at[2, 0]),
        pltpu.make_async_copy(peer_hbm, peer, in_sems.at[2, 1]),
    ]
    tile_copies = split_copies(tiles_hbm, tiles, in_sems.at[0])
    feature_copies = split_copies(features_hbm, features, in_sems.at[1])
    for copy in scalars + tile_copies + feature_copies:
        copy.start()
    count, block, _ = tiles.shape
    dense[...] = jnp.zeros_like(dense)
    for copy in scalars + tile_copies:
        copy.wait()

    def place(tile, carry):
        row = pl.multiple_of(peer[tile] * block, block)
        column = pl.multiple_of(src[tile] * block, block)
        at = (pl.ds(row, block), pl.ds(column, block))
        dense[at] = dense[at] + tiles[tile].astype(F32)
        return carry

    lax.fori_loop(0, count, place, 0)
    for copy in feature_copies:
        copy.wait()
    chunk = 4 * block
    results = []
    for index in range(out.shape[0] // chunk):
        at = slice(index * chunk, (index + 1) * chunk)
        out[at, :] = jnp.dot(dense[at, :].astype(BF16), features[...], preferred_element_type=F32).astype(BF16)
        results.append(pltpu.make_async_copy(out.at[at, :], out_hbm.at[at, :], out_sems.at[index]))
        results[-1].start()
    for result in results:
        result.wait()


def weight_copies(flip, weight_hbms, weight, sems):
    sources = len(weight_hbms)
    copies = []
    for source, weight_hbm in enumerate(weight_hbms):
        for piece in range(weight_hbm.shape[0]):
            target = piece if sources == 1 else 2 * piece + (flip ^ source)
            copies.append(
                pltpu.make_async_copy(weight_hbm.at[piece], weight.at[target], sems.at[sources * piece + source])
            )
    return copies


def self_kernel(flip_ref, features_hbm, *refs):
    *weight_hbms, out_hbm, features, weight, out, feature_sems, weight_sems, out_sems = refs
    rows, width = features.shape
    hidden = out.shape[1]
    copies = weight_copies(flip_ref[0], weight_hbms, weight, weight_sems)
    copies += split_copies(features_hbm, features, feature_sems)
    for copy in copies:
        copy.start()
    for copy in copies:
        copy.wait()
    chunk = 256
    results = split_copies(out, out_hbm, out_sems, rows // chunk)
    for index, result in enumerate(results):
        at = slice(index * chunk, (index + 1) * chunk)
        out[at, :] = jnp.dot(
            features[at, :], weight[...].reshape(width, hidden), preferred_element_type=F32
        ).astype(BF16)
        result.start()
    for result in results:
        result.wait()


def layer_kernel(
    sources, pieces, places_ref, into_ref, slots_hbm, total_hbm, features_hbm, cotangent_hbm, *refs
):
    weight_hbms, out_hbms = refs[:sources], refs[sources:-15]
    slots, slot_sems = refs[-15:-13]
    total, features, cotangent, weight, summed, values, aggregate, grad, both = refs[-13:-4]
    row_sems, weight_sems, feature_sems, out_sems = refs[-4:]
    senders, block, _ = slots.shape
    rows, hidden = grad.shape
    width = aggregate.shape[1]
    core, flip, low, upper = [places_ref[index] for index in range(4)]
    chunk = 256
    parts = rows // chunk
    weights = weight_copies(flip, weight_hbms, weight, weight_sems)
    totals = split_copies(total_hbm, total, row_sems.at[0], parts)
    cotangents = split_copies(cotangent_hbm, cotangent, row_sems.at[1], parts)
    inputs = split_copies(features_hbm, features, feature_sems)
    arrivals = [
        pltpu.make_async_copy(slots_hbm.at[sender], slots.at[sender], slot_sems.at[sender]) for sender in range(senders)
    ]
    for copy in arrivals + weights + totals + cotangents + inputs:
        copy.start()

    def target(sender):
        return pl.ds(pl.multiple_of(into_ref[sender] * block, block), block)

    for index in range(rows // block):
        reached = functools.reduce(jnp.logical_or, [into_ref[sender] == index for sender in range(senders)])

        @pl.when(jnp.logical_not(reached))
        def _():
            summed[index * block : (index + 1) * block, :] = jnp.zeros((block, width), F32)

    for sender in range(senders):
        arrivals[sender].wait()
        if sender == 0:
            summed[target(0), :] = slots[0].astype(F32)
            continue
        again = functools.reduce(jnp.logical_or, [into_ref[sender] == into_ref[index] for index in range(sender)])

        @pl.when(again)
        def _():
            summed[target(sender), :] = summed[target(sender), :] + slots[sender].astype(F32)

        @pl.when(jnp.logical_not(again))
        def _():
            summed[target(sender), :] = slots[sender].astype(F32)

    aggregate[...] = summed[...].astype(BF16)
    for copy in weights:
        copy.wait()
    span = hidden // 2

    def multiply(index):
        at = slice(index * chunk, (index + 1) * chunk)
        for begin in range(0, hidden, span):
            columns = slice(begin, begin + span)
            values[index % 2, :, columns] = jnp.dot(
                aggregate[at, :], weight[:, :, columns].reshape(width, span), preferred_element_type=F32
            )

    multiply(0)
    for index in range(parts):
        if index + 1 < parts:
            multiply(index + 1)
        totals[index].wait()
        cotangents[index].wait()
        for row in range(0, chunk, 32):
            at = slice(index * chunk + row, index * chunk + row + 32)
            for begin in range(0, hidden, span):
                columns = slice(begin, begin + span)
                value = values[index % 2, row : row + 32, columns] + total[at, columns].astype(F32)
                value = value.astype(BF16)
                square = value * value
                bend = jnp.tanh(value * (square * (SCALE * CUBIC) + SCALE))
                inner = value * (square * (1.5 * SCALE * CUBIC) + 0.5 * SCALE)
                grad[at, columns] = cotangent[at, columns] * ((1.0 + bend) * (inner * (1.0 - bend) + 0.5))

    for copy in inputs:
        copy.wait()
    moves = []
    for term, which in enumerate([1 - core, core]):
        for index, target in enumerate(out_hbms[2 * term : 2 * term + 2]):
            if not pieces:
                moves.append((index, which, both.at[index, which], target))
                continue
            row_bit, column_bit = (low, upper) if index else (1 - low, 1 - upper)
            for row in range(target.shape[0]):
                for side in range(2):
                    half = jnp.where(which == 0, side, column_bit)
                    place = 2 * row + jnp.where(which == 0, row_bit, side)
                    columns = slice(side * span, (side + 1) * span)
                    moves.append((half, which, both.at[half, which, place], target.at[row, :, columns]))
    contract = (((0,), (0,)), ((), ()))
    results = [
        pltpu.make_async_copy(source, target, out_sems.at[index]) for index, (_, _, source, target) in enumerate(moves)
    ]
    for half in range(2):
        columns = slice(half * span, (half + 1) * span)
        for index, operand in enumerate([features, aggregate]):
            product = lax.dot_general(operand[...], grad[:, columns], contract, preferred_element_type=F32)
            both[half, index] = product.astype(BF16).reshape(both.shape[2:])
            for move, result in zip(moves, results):
                pl.when(jnp.logical_and(move[0] == half, move[1] == index))(result.start)
    for result in results:
        result.wait()


def call(kernel, outs, places, out_places, scratch=(), flops=0, moved=0, vmem=56):
    return pl.pallas_call(
        kernel,
        out_shape=outs,
        in_specs=places,
        out_specs=out_places,
        scratch_shapes=list(scratch),
        compiler_params=pltpu.CompilerParams(vmem_limit_bytes=vmem * MIB),
        cost_estimate=pl.CostEstimate(flops=flops, bytes_accessed=moved, transcendentals=0),
    )


def joined(held, other, upper, axis):
    return jnp.stack([jnp.where(upper, other, held), jnp.where(upper, held, other)], axis=axis)


def gather_high(held, high):
    step = 1
    while step < lax.axis_size("rep") // 2:
        other = swap(held, "rep", 2 * step)
        upper = (high & step) != 0
        held = jnp.concatenate([jnp.where(upper, other, held), jnp.where(upper, held, other)], axis=-1)
        step *= 2
    return held


def added(terms):
    return sum(term.astype(F32) for term in terms).astype(BF16)


def half_of(value, axis, which):
    size = value.shape[axis] // 2
    return lax.dynamic_slice_in_dim(value, which * size, size, axis)


def first_pieces(term, depth, core, low, upper):
    term = term.reshape(-1, 2, depth, 2, term.shape[1] // 2)
    pieces = []
    for row_bit, column_bit in ((1 - low, 1 - upper), (low, upper)):
        rows = lax.dynamic_index_in_dim(term, row_bit, 1, keepdims=False)
        columns = lax.dynamic_index_in_dim(term, column_bit, 3, keepdims=False).swapaxes(1, 2)
        pieces.append(jnp.where(core == 0, rows, columns).reshape(term.shape[0], depth, -1))
    return pieces


def turn_swap(value, turn):
    reps, doms = lax.axis_size("rep"), lax.axis_size("dom")
    pairs = []
    for rep in range(reps):
        for dom in range(doms):
            target = rep * doms + (dom ^ 1) if rep % 2 == turn else (rep ^ (reps // 2)) * doms + dom
            pairs.append((rep * doms + dom, target))
    return lax.ppermute(value, ("rep", "dom"), pairs)


def column_half(term, which):
    size = term.shape[-1] // 2
    return lax.dynamic_slice_in_dim(term, which * size, size, term.ndim - 1)


def exchanged(term, take, which, axis, step):
    return added([take(term, which), swap(take(term, 1 - which), axis, step)])


def reduce_high(term, high, step):
    while step:
        term = exchanged(term, column_half, (high // step) % 2, "rep", 2 * step)
        step //= 2
    return term


def shards(features, cotangent, w_self, w_neigh, tile_vals, tile_src, tile_peer, in_block):
    dom_size = lax.axis_size("dom")
    rows, width = features.shape
    hidden = w_self.shape[1]
    block = tile_vals.shape[1]
    me = lax.axis_index("dom")
    rep = lax.axis_index("rep")
    parts = lax.axis_size("rep") // 2
    core, high = rep & 1, rep >> 1
    low, place = me & 1, me >> 1

    share = hidden // parts
    top = dom_size // 2
    held = jnp.stack([lax.dynamic_slice_in_dim(weight, high * share, share, 1) for weight in (w_self, w_neigh)])
    near, far = cross(held, 0), cross(held, top)
    slots = call(
        slots_kernel,
        jax.ShapeDtypeStruct((dom_size * block, width), BF16),
        [HBM] * 4,
        HBM,
        [
            pltpu.SMEM(tile_src.shape, jnp.int32),
            pltpu.SMEM(tile_peer.shape, jnp.int32),
            pltpu.VMEM(tile_vals.shape, BF16),
            pltpu.VMEM(features.shape, BF16),
            pltpu.VMEM((dom_size * block, rows), F32),
            pltpu.VMEM((dom_size * block, width), BF16),
            DMA((3, 4)),
            DMA((dom_size // 4,)),
        ],
        flops=2 * dom_size * block * rows * width,
        moved=tile_vals.size * 2 + rows * width * 4,
    )(tile_src, tile_peer, tile_vals, features)
    near, far, slots = lax.optimization_barrier((near, far, slots))
    held = joined(jnp.where(core == 0, held, near), far, (me & top) != 0, 1)
    step = top // 2
    while step > 1:
        held = joined(held, swap(held, "dom", step), (me & step) != 0, 2)
        held = held.reshape(2, -1, *held.shape[3:])
        step //= 2
    received = lax.all_to_all(slots.reshape(dom_size, block, width), "dom", split_axis=0, concat_axis=0, tiled=True)
    mine = gather_high(held, high)
    depth = width // dom_size
    tiled = depth % 16 == 0
    flip = low ^ core
    weights = [[mine[index], swap(mine[index], "rep", 1)] for index in range(2)]
    if not tiled:
        weights = [[joined(*weight, flip != 0, 1).reshape(-1, 128, hidden)] for weight in weights]
    sources, count = len(weights[0]), sum(weight.shape[0] for weight in weights[0])
    weight_shape = pltpu.VMEM((count, width // count, hidden), BF16)
    total = call(
        self_kernel,
        jax.ShapeDtypeStruct((rows, hidden), BF16),
        [SMEM] + [HBM] * (1 + sources),
        HBM,
        [
            pltpu.VMEM((rows, width), BF16),
            weight_shape,
            pltpu.VMEM((rows, hidden), BF16),
            DMA((4,)),
            DMA((count,)),
            DMA((rows // 256,)),
        ],
        flops=2 * rows * width * hidden,
        moved=7 * rows * hidden,
        vmem=62,
    )(flip.astype(jnp.int32).reshape(1), features, *weights[0])
    span = hidden // 2
    upper = (high // (parts // 2)) % 2
    places = jnp.stack([core, flip, low, upper]).astype(jnp.int32)
    if tiled:
        out_shapes = [jax.ShapeDtypeStruct((dom_size // 2, depth, hidden), BF16)] * 4
        product_shape = (2, 2, dom_size, depth, span)
    else:
        out_shapes = [jax.ShapeDtypeStruct((width, span), BF16)] * 4
        product_shape = (2, 2, width, span)
    outs = call(
        functools.partial(layer_kernel, sources, tiled),
        out_shapes,
        [SMEM, SMEM] + [HBM] * (4 + sources),
        [HBM] * 4,
        [
            pltpu.VMEM((dom_size, block, width), BF16),
            DMA((dom_size,)),
            pltpu.VMEM((rows, hidden), BF16),
            pltpu.VMEM((rows, width), BF16),
            pltpu.VMEM((rows, hidden), BF16),
            weight_shape,
            pltpu.VMEM((rows, width), F32),
            pltpu.VMEM((2, 256, hidden), F32),
            pltpu.VMEM((rows, width), BF16),
            pltpu.VMEM((rows, hidden), BF16),
            pltpu.VMEM(product_shape, BF16),
            DMA((2, rows // 256)),
            DMA((count,)),
            DMA((4,)),
            DMA((4 * dom_size,)),
        ],
        flops=6 * rows * width * hidden,
        moved=16 * rows * hidden,
    )(places, in_block, received, total, features, cotangent, *weights[1])
    sent, kept = outs[:2], outs[2:]
    if not tiled:
        sent, kept = [
            first_pieces(jnp.concatenate(pair, axis=1), depth, which, low, upper)
            for pair, which in ((sent, 1 - core), (kept, core))
        ]
    leave, stay = [[own, swap(piece, "rep", 1)] for own, piece in zip(kept, sent)]
    held = added([*stay, turn_swap(added(leave), 0)])
    bit = jnp.where(core == 0, upper, low)
    held = added([column_half(held, bit), turn_swap(column_half(held, 1 - bit), 1)])
    both = reduce_high(held, high, parts // 4)
    summed = lax.dynamic_index_in_dim(both, place, 0, keepdims=False).astype(F32)
    for step in range(1, dom_size // 2):
        piece = lax.dynamic_index_in_dim(both, place ^ step, 0, keepdims=False)
        summed = summed + swap(piece, "dom", 2 * step).astype(F32)
    summed = summed.astype(BF16)
    whole = gather_high(summed, high)
    opposite = swap(whole, "rep", 1)
    return (
        jnp.where(core == 0, whole, opposite).astype(F32),
        jnp.where(core == 0, opposite, whole).astype(F32),
    )


def solution(mesh):
    in_specs = (
        P(("rep", "dom"), None),
        P(("rep", "dom"), None),
        P("dom", None),
        P("dom", None),
        P(("rep", "dom"), None, None),
        P(("rep", "dom")),
        P(("rep", "dom")),
        P(("rep", "dom")),
    )
    out_specs = (P("dom", None), P("dom", None))
    return jax.shard_map(shards, mesh=mesh, in_specs=in_specs, out_specs=out_specs, check_vma=False)
```

```python
import functools

import jax
import jax.numpy as jnp
from jax import lax
from jax.experimental import pallas as pl
from jax.experimental.pallas import tpu as pltpu
from jax.sharding import PartitionSpec as P

F32 = jnp.float32
BF16 = jnp.bfloat16
SCALE = 0.7978845608
CUBIC = 0.044715
MIB = 1 << 20
HBM = pl.BlockSpec(memory_space=pltpu.HBM)
SMEM = pl.BlockSpec(memory_space=pltpu.SMEM)
VMEM = pl.BlockSpec(memory_space=pltpu.VMEM)
DMA = pltpu.SemaphoreType.DMA


def swap(value, axis, step):
    size = lax.axis_size(axis)
    return lax.ppermute(value, axis, [(index, index ^ step) for index in range(size)])


def cross(value, step):
    reps, doms = lax.axis_size("rep"), lax.axis_size("dom")
    pairs = [
        (rep * doms + dom, rep * doms + (dom ^ step ^ (rep & 1))) for rep in range(reps) for dom in range(doms)
    ]
    return lax.ppermute(value, ("rep", "dom"), [(source, target) for source, target in pairs if source != target])


def split_copies(source, target, sems, count=4):
    size = source.shape[0] // count
    return [
        pltpu.make_async_copy(
            source.at[index * size : (index + 1) * size], target.at[index * size : (index + 1) * size], sems.at[index]
        )
        for index in range(count)
    ]


def slots_kernel(
    src_hbm, peer_hbm, tiles_hbm, features_hbm, out_hbm, src, peer, tiles, features, dense, out, in_sems, out_sems
):
    scalars = [
        pltpu.make_async_copy(src_hbm, src, in_sems.at[2, 0]),
        pltpu.make_async_copy(peer_hbm, peer, in_sems.at[2, 1]),
    ]
    tile_copies = split_copies(tiles_hbm, tiles, in_sems.at[0])
    feature_copies = split_copies(features_hbm, features, in_sems.at[1])
    for copy in scalars + tile_copies + feature_copies:
        copy.start()
    count, block, _ = tiles.shape
    dense[...] = jnp.zeros_like(dense)
    for copy in scalars + tile_copies:
        copy.wait()

    def place(tile, carry):
        row = pl.multiple_of(peer[tile] * block, block)
        column = pl.multiple_of(src[tile] * block, block)
        at = (pl.ds(row, block), pl.ds(column, block))
        dense[at] = dense[at] + tiles[tile].astype(F32)
        return carry

    lax.fori_loop(0, count, place, 0)
    for copy in feature_copies:
        copy.wait()
    chunk = 4 * block
    results = []
    for index in range(out.shape[0] // chunk):
        at = slice(index * chunk, (index + 1) * chunk)
        out[at, :] = jnp.dot(dense[at, :].astype(BF16), features[...], preferred_element_type=F32).astype(BF16)
        results.append(pltpu.make_async_copy(out.at[at, :], out_hbm.at[at, :], out_sems.at[index]))
        results[-1].start()
    for result in results:
        result.wait()


def weight_copies(flip, weight_hbms, weight, sems):
    sources = len(weight_hbms)
    copies = []
    for source, weight_hbm in enumerate(weight_hbms):
        for piece in range(weight_hbm.shape[0]):
            target = piece if sources == 1 else 2 * piece + (flip ^ source)
            copies.append(
                pltpu.make_async_copy(weight_hbm.at[piece], weight.at[target], sems.at[sources * piece + source])
            )
    return copies


def self_kernel(flip_ref, features_hbm, *refs):
    *weight_hbms, out_hbm, features, weight, out, feature_sems, weight_sems, out_sems = refs
    rows, width = features.shape
    hidden = out.shape[1]
    copies = weight_copies(flip_ref[0], weight_hbms, weight, weight_sems)
    copies += split_copies(features_hbm, features, feature_sems)
    for copy in copies:
        copy.start()
    for copy in copies:
        copy.wait()
    chunk = 256
    results = split_copies(out, out_hbm, out_sems, rows // chunk)
    for index, result in enumerate(results):
        at = slice(index * chunk, (index + 1) * chunk)
        out[at, :] = jnp.dot(
            features[at, :], weight[...].reshape(width, hidden), preferred_element_type=F32
        ).astype(BF16)
        result.start()
    for result in results:
        result.wait()


def layer_kernel(
    sources, pieces, places_ref, into_ref, slots_hbm, total_hbm, features_hbm, cotangent_hbm, *refs
):
    weight_hbms, out_hbms = refs[:sources], refs[sources:-15]
    slots, slot_sems = refs[-15:-13]
    total, features, cotangent, weight, summed, values, aggregate, grad, both = refs[-13:-4]
    row_sems, weight_sems, feature_sems, out_sems = refs[-4:]
    senders, block, _ = slots.shape
    rows, hidden = grad.shape
    width = aggregate.shape[1]
    core, flip, low, upper = [places_ref[index] for index in range(4)]
    chunk = 256
    parts = rows // chunk
    weights = weight_copies(flip, weight_hbms, weight, weight_sems)
    totals = split_copies(total_hbm, total, row_sems.at[0], parts)
    cotangents = split_copies(cotangent_hbm, cotangent, row_sems.at[1], parts)
    inputs = split_copies(features_hbm, features, feature_sems)
    arrivals = [
        pltpu.make_async_copy(slots_hbm.at[sender], slots.at[sender], slot_sems.at[sender]) for sender in range(senders)
    ]
    for copy in arrivals + weights + totals[:1] + cotangents[:1]:
        copy.start()

    def target(sender):
        return pl.ds(pl.multiple_of(into_ref[sender] * block, block), block)

    for index in range(rows // block):
        reached = functools.reduce(jnp.logical_or, [into_ref[sender] == index for sender in range(senders)])

        @pl.when(jnp.logical_not(reached))
        def _():
            summed[index * block : (index + 1) * block, :] = jnp.zeros((block, width), F32)

    for copy in arrivals:
        copy.wait()
    for copy in [copy for pair in zip(totals[1:], cotangents[1:]) for copy in pair] + inputs:
        copy.start()
    for sender in range(senders):
        if sender == 0:
            summed[target(0), :] = slots[0].astype(F32)
            continue
        again = functools.reduce(jnp.logical_or, [into_ref[sender] == into_ref[index] for index in range(sender)])

        @pl.when(again)
        def _():
            summed[target(sender), :] = summed[target(sender), :] + slots[sender].astype(F32)

        @pl.when(jnp.logical_not(again))
        def _():
            summed[target(sender), :] = slots[sender].astype(F32)

    aggregate[...] = summed[...].astype(BF16)
    for copy in weights:
        copy.wait()
    span = hidden // 2

    def multiply(index):
        at = slice(index * chunk, (index + 1) * chunk)
        for begin in range(0, hidden, span):
            columns = slice(begin, begin + span)
            values[index % 2, :, columns] = jnp.dot(
                aggregate[at, :], weight[:, :, columns].reshape(width, span), preferred_element_type=F32
            )

    multiply(0)
    for index in range(parts):
        if index + 1 < parts:
            multiply(index + 1)
        totals[index].wait()
        cotangents[index].wait()
        for row in range(0, chunk, 32):
            at = slice(index * chunk + row, index * chunk + row + 32)
            for begin in range(0, hidden, span):
                columns = slice(begin, begin + span)
                value = values[index % 2, row : row + 32, columns] + total[at, columns].astype(F32)
                value = value.astype(BF16)
                square = value * value
                bend = jnp.tanh(value * (square * (SCALE * CUBIC) + SCALE))
                inner = value * (square * (1.5 * SCALE * CUBIC) + 0.5 * SCALE)
                grad[at, columns] = cotangent[at, columns] * ((1.0 + bend) * (inner * (1.0 - bend) + 0.5))

    for copy in inputs:
        copy.wait()
    moves = []
    for term, which in enumerate([1 - core, core]):
        for index, target in enumerate(out_hbms[2 * term : 2 * term + 2]):
            if not pieces:
                moves.append((index, which, both.at[index, which], target))
                continue
            row_bit, column_bit = (low, upper) if index else (1 - low, 1 - upper)
            for row in range(target.shape[0]):
                for side in range(2):
                    half = jnp.where(which == 0, side, column_bit)
                    place = 2 * row + jnp.where(which == 0, row_bit, side)
                    columns = slice(side * span, (side + 1) * span)
                    moves.append((half, which, both.at[half, which, place], target.at[row, :, columns]))
    contract = (((0,), (0,)), ((), ()))
    results = [
        pltpu.make_async_copy(source, target, out_sems.at[index]) for index, (_, _, source, target) in enumerate(moves)
    ]
    for half in range(2):
        columns = slice(half * span, (half + 1) * span)
        for index, operand in enumerate([features, aggregate]):
            product = lax.dot_general(operand[...], grad[:, columns], contract, preferred_element_type=F32)
            both[half, index] = product.astype(BF16).reshape(both.shape[2:])
            for move, result in zip(moves, results):
                pl.when(jnp.logical_and(move[0] == half, move[1] == index))(result.start)
    for result in results:
        result.wait()


def call(kernel, outs, places, out_places, scratch=(), flops=0, moved=0, vmem=56):
    return pl.pallas_call(
        kernel,
        out_shape=outs,
        in_specs=places,
        out_specs=out_places,
        scratch_shapes=list(scratch),
        compiler_params=pltpu.CompilerParams(vmem_limit_bytes=vmem * MIB),
        cost_estimate=pl.CostEstimate(flops=flops, bytes_accessed=moved, transcendentals=0),
    )


def joined(held, other, upper, axis):
    return jnp.stack([jnp.where(upper, other, held), jnp.where(upper, held, other)], axis=axis)


def gather_high(held, high):
    step = 1
    while step < lax.axis_size("rep") // 2:
        other = swap(held, "rep", 2 * step)
        upper = (high & step) != 0
        held = jnp.concatenate([jnp.where(upper, other, held), jnp.where(upper, held, other)], axis=-1)
        step *= 2
    return held


def added(terms):
    return sum(term.astype(F32) for term in terms).astype(BF16)


def half_of(value, axis, which):
    size = value.shape[axis] // 2
    return lax.dynamic_slice_in_dim(value, which * size, size, axis)


def first_pieces(term, depth, core, low, upper):
    term = term.reshape(-1, 2, depth, 2, term.shape[1] // 2)
    pieces = []
    for row_bit, column_bit in ((1 - low, 1 - upper), (low, upper)):
        rows = lax.dynamic_index_in_dim(term, row_bit, 1, keepdims=False)
        columns = lax.dynamic_index_in_dim(term, column_bit, 3, keepdims=False).swapaxes(1, 2)
        pieces.append(jnp.where(core == 0, rows, columns).reshape(term.shape[0], depth, -1))
    return pieces


def turn_swap(value, turn):
    reps, doms = lax.axis_size("rep"), lax.axis_size("dom")
    pairs = []
    for rep in range(reps):
        for dom in range(doms):
            target = rep * doms + (dom ^ 1) if rep % 2 == turn else (rep ^ (reps // 2)) * doms + dom
            pairs.append((rep * doms + dom, target))
    return lax.ppermute(value, ("rep", "dom"), pairs)


def column_half(term, which):
    size = term.shape[-1] // 2
    return lax.dynamic_slice_in_dim(term, which * size, size, term.ndim - 1)


def exchanged(term, take, which, axis, step):
    return added([take(term, which), swap(take(term, 1 - which), axis, step)])


def reduce_high(term, high, step):
    while step:
        term = exchanged(term, column_half, (high // step) % 2, "rep", 2 * step)
        step //= 2
    return term


def shards(features, cotangent, w_self, w_neigh, tile_vals, tile_src, tile_peer, in_block):
    dom_size = lax.axis_size("dom")
    rows, width = features.shape
    hidden = w_self.shape[1]
    block = tile_vals.shape[1]
    me = lax.axis_index("dom")
    rep = lax.axis_index("rep")
    parts = lax.axis_size("rep") // 2
    core, high = rep & 1, rep >> 1
    low, place = me & 1, me >> 1

    share = hidden // parts
    top = dom_size // 2
    held = jnp.stack([lax.dynamic_slice_in_dim(weight, high * share, share, 1) for weight in (w_self, w_neigh)])
    near, far = cross(held, 0), cross(held, top)
    slots = call(
        slots_kernel,
        jax.ShapeDtypeStruct((dom_size * block, width), BF16),
        [HBM] * 4,
        HBM,
        [
            pltpu.SMEM(tile_src.shape, jnp.int32),
            pltpu.SMEM(tile_peer.shape, jnp.int32),
            pltpu.VMEM(tile_vals.shape, BF16),
            pltpu.VMEM(features.shape, BF16),
            pltpu.VMEM((dom_size * block, rows), F32),
            pltpu.VMEM((dom_size * block, width), BF16),
            DMA((3, 4)),
            DMA((dom_size // 4,)),
        ],
        flops=2 * dom_size * block * rows * width,
        moved=tile_vals.size * 2 + rows * width * 4,
    )(tile_src, tile_peer, tile_vals, features)
    near, far, slots = lax.optimization_barrier((near, far, slots))
    held = joined(jnp.where(core == 0, held, near), far, (me & top) != 0, 1)
    step = top // 2
    while step > 1:
        held = joined(held, swap(held, "dom", step), (me & step) != 0, 2)
        held = held.reshape(2, -1, *held.shape[3:])
        step //= 2
    received = lax.all_to_all(slots.reshape(dom_size, block, width), "dom", split_axis=0, concat_axis=0, tiled=True)
    mine = gather_high(held, high)
    depth = width // dom_size
    tiled = depth % 16 == 0
    flip = low ^ core
    weights = [[mine[index], swap(mine[index], "rep", 1)] for index in range(2)]
    if not tiled:
        weights = [[joined(*weight, flip != 0, 1).reshape(-1, 128, hidden)] for weight in weights]
    sources, count = len(weights[0]), sum(weight.shape[0] for weight in weights[0])
    weight_shape = pltpu.VMEM((count, width // count, hidden), BF16)
    total = call(
        self_kernel,
        jax.ShapeDtypeStruct((rows, hidden), BF16),
        [SMEM] + [HBM] * (1 + sources),
        HBM,
        [
            pltpu.VMEM((rows, width), BF16),
            weight_shape,
            pltpu.VMEM((rows, hidden), BF16),
            DMA((4,)),
            DMA((count,)),
            DMA((rows // 256,)),
        ],
        flops=2 * rows * width * hidden,
        moved=7 * rows * hidden,
    )(flip.astype(jnp.int32).reshape(1), features, *weights[0])
    span = hidden // 2
    upper = (high // (parts // 2)) % 2
    places = jnp.stack([core, flip, low, upper]).astype(jnp.int32)
    if tiled:
        out_shapes = [jax.ShapeDtypeStruct((dom_size // 2, depth, hidden), BF16)] * 4
        product_shape = (2, 2, dom_size, depth, span)
    else:
        out_shapes = [jax.ShapeDtypeStruct((width, span), BF16)] * 4
        product_shape = (2, 2, width, span)
    outs = call(
        functools.partial(layer_kernel, sources, tiled),
        out_shapes,
        [SMEM, SMEM] + [HBM] * (4 + sources),
        [HBM] * 4,
        [
            pltpu.VMEM((dom_size, block, width), BF16),
            DMA((dom_size,)),
            pltpu.VMEM((rows, hidden), BF16),
            pltpu.VMEM((rows, width), BF16),
            pltpu.VMEM((rows, hidden), BF16),
            weight_shape,
            pltpu.VMEM((rows, width), F32),
            pltpu.VMEM((2, 256, hidden), F32),
            pltpu.VMEM((rows, width), BF16),
            pltpu.VMEM((rows, hidden), BF16),
            pltpu.VMEM(product_shape, BF16),
            DMA((2, rows // 256)),
            DMA((count,)),
            DMA((4,)),
            DMA((4 * dom_size,)),
        ],
        flops=6 * rows * width * hidden,
        moved=16 * rows * hidden,
    )(places, in_block, received, total, features, cotangent, *weights[1])
    sent, kept = outs[:2], outs[2:]
    if not tiled:
        sent, kept = [
            first_pieces(jnp.concatenate(pair, axis=1), depth, which, low, upper)
            for pair, which in ((sent, 1 - core), (kept, core))
        ]
    leave, stay = [[own, swap(piece, "rep", 1)] for own, piece in zip(kept, sent)]
    held = added([*stay, turn_swap(added(leave), 0)])
    bit = jnp.where(core == 0, upper, low)
    held = added([column_half(held, bit), turn_swap(column_half(held, 1 - bit), 1)])
    both = reduce_high(held, high, parts // 4)
    summed = lax.dynamic_index_in_dim(both, place, 0, keepdims=False).astype(F32)
    for step in range(1, dom_size // 2):
        piece = lax.dynamic_index_in_dim(both, place ^ step, 0, keepdims=False)
        summed = summed + swap(piece, "dom", 2 * step).astype(F32)
    summed = summed.astype(BF16)
    whole = gather_high(summed, high)
    opposite = swap(whole, "rep", 1)
    return (
        jnp.where(core == 0, whole, opposite).astype(F32),
        jnp.where(core == 0, opposite, whole).astype(F32),
    )


def solution(mesh):
    in_specs = (
        P(("rep", "dom"), None),
        P(("rep", "dom"), None),
        P("dom", None),
        P("dom", None),
        P(("rep", "dom"), None, None),
        P(("rep", "dom")),
        P(("rep", "dom")),
        P(("rep", "dom")),
    )
    out_specs = (P("dom", None), P("dom", None))
    return jax.shard_map(shards, mesh=mesh, in_specs=in_specs, out_specs=out_specs, check_vma=False)
```

```python
import functools

import jax
import jax.numpy as jnp
from jax import lax
from jax.experimental import pallas as pl
from jax.experimental.pallas import tpu as pltpu
from jax.sharding import PartitionSpec as P

F32 = jnp.float32
BF16 = jnp.bfloat16
SCALE = 0.7978845608
CUBIC = 0.044715
MIB = 1 << 20
HBM = pl.BlockSpec(memory_space=pltpu.HBM)
SMEM = pl.BlockSpec(memory_space=pltpu.SMEM)
VMEM = pl.BlockSpec(memory_space=pltpu.VMEM)
DMA = pltpu.SemaphoreType.DMA


def swap(value, axis, step):
    size = lax.axis_size(axis)
    return lax.ppermute(value, axis, [(index, index ^ step) for index in range(size)])


def cross(value, step):
    reps, doms = lax.axis_size("rep"), lax.axis_size("dom")
    pairs = [
        (rep * doms + dom, rep * doms + (dom ^ step ^ (rep & 1))) for rep in range(reps) for dom in range(doms)
    ]
    return lax.ppermute(value, ("rep", "dom"), [(source, target) for source, target in pairs if source != target])


def split_copies(source, target, sems, count=4):
    size = source.shape[0] // count
    return [
        pltpu.make_async_copy(
            source.at[index * size : (index + 1) * size], target.at[index * size : (index + 1) * size], sems.at[index]
        )
        for index in range(count)
    ]


def slots_kernel(
    src_hbm, peer_hbm, tiles_hbm, features_hbm, out_hbm, src, peer, tiles, features, dense, out, in_sems, out_sems
):
    scalars = [
        pltpu.make_async_copy(src_hbm, src, in_sems.at[2, 0]),
        pltpu.make_async_copy(peer_hbm, peer, in_sems.at[2, 1]),
    ]
    tile_copies = split_copies(tiles_hbm, tiles, in_sems.at[0])
    feature_copies = split_copies(features_hbm, features, in_sems.at[1])
    for copy in scalars + tile_copies + feature_copies:
        copy.start()
    count, block, _ = tiles.shape
    dense[...] = jnp.zeros_like(dense)
    for copy in scalars + tile_copies:
        copy.wait()

    def place(tile, carry):
        row = pl.multiple_of(peer[tile] * block, block)
        column = pl.multiple_of(src[tile] * block, block)
        at = (pl.ds(row, block), pl.ds(column, block))
        dense[at] = dense[at] + tiles[tile].astype(F32)
        return carry

    lax.fori_loop(0, count, place, 0)
    for copy in feature_copies:
        copy.wait()
    chunk = 4 * block
    results = []
    for index in range(out.shape[0] // chunk):
        at = slice(index * chunk, (index + 1) * chunk)
        out[at, :] = jnp.dot(dense[at, :].astype(BF16), features[...], preferred_element_type=F32).astype(BF16)
        results.append(pltpu.make_async_copy(out.at[at, :], out_hbm.at[at, :], out_sems.at[index]))
        results[-1].start()
    for result in results:
        result.wait()


def weight_copies(flip, weight_hbms, weight, sems):
    sources = len(weight_hbms)
    copies = []
    for source, weight_hbm in enumerate(weight_hbms):
        for piece in range(weight_hbm.shape[0]):
            target = piece if sources == 1 else 2 * piece + (flip ^ source)
            copies.append(
                pltpu.make_async_copy(weight_hbm.at[piece], weight.at[target], sems.at[sources * piece + source])
            )
    return copies


def self_kernel(flip_ref, features_hbm, *refs):
    *weight_hbms, out_hbm, features, weight, out, feature_sems, weight_sems, out_sems = refs
    rows, width = features.shape
    hidden = out.shape[1]
    copies = weight_copies(flip_ref[0], weight_hbms, weight, weight_sems)
    copies += split_copies(features_hbm, features, feature_sems)
    for copy in copies:
        copy.start()
    for copy in copies:
        copy.wait()
    chunk = 256
    results = split_copies(out, out_hbm, out_sems, rows // chunk)
    for index, result in enumerate(results):
        at = slice(index * chunk, (index + 1) * chunk)
        out[at, :] = jnp.dot(
            features[at, :], weight[...].reshape(width, hidden), preferred_element_type=F32
        ).astype(BF16)
        result.start()
    for result in results:
        result.wait()


def layer_kernel(
    sources, pieces, places_ref, into_ref, slots_hbm, total_hbm, features_hbm, cotangent_hbm, *refs
):
    weight_hbms, out_hbms = refs[:sources], refs[sources:-15]
    slots, slot_sems = refs[-15:-13]
    total, features, cotangent, weight, summed, values, aggregate, grad, both = refs[-13:-4]
    row_sems, weight_sems, feature_sems, out_sems = refs[-4:]
    senders, block, _ = slots.shape
    rows, hidden = grad.shape
    width = aggregate.shape[1]
    core, flip, low, upper = [places_ref[index] for index in range(4)]
    chunk = 256
    parts = rows // chunk
    weights = weight_copies(flip, weight_hbms, weight, weight_sems)
    totals = split_copies(total_hbm, total, row_sems.at[0], parts)
    cotangents = split_copies(cotangent_hbm, cotangent, row_sems.at[1], parts)
    inputs = split_copies(features_hbm, features, feature_sems)
    arrivals = [
        pltpu.make_async_copy(slots_hbm.at[sender], slots.at[sender], slot_sems.at[sender]) for sender in range(senders)
    ]
    for copy in arrivals + weights + totals[:1] + cotangents[:1]:
        copy.start()

    def target(sender):
        return pl.ds(pl.multiple_of(into_ref[sender] * block, block), block)

    for index in range(rows // block):
        reached = functools.reduce(jnp.logical_or, [into_ref[sender] == index for sender in range(senders)])

        @pl.when(jnp.logical_not(reached))
        def _():
            summed[index * block : (index + 1) * block, :] = jnp.zeros((block, width), F32)

    for copy in arrivals:
        copy.wait()
    for copy in [copy for pair in zip(totals[1:], cotangents[1:]) for copy in pair] + inputs:
        copy.start()
    for sender in range(senders):
        if sender == 0:
            summed[target(0), :] = slots[0].astype(F32)
            continue
        again = functools.reduce(jnp.logical_or, [into_ref[sender] == into_ref[index] for index in range(sender)])

        @pl.when(again)
        def _():
            summed[target(sender), :] = summed[target(sender), :] + slots[sender].astype(F32)

        @pl.when(jnp.logical_not(again))
        def _():
            summed[target(sender), :] = slots[sender].astype(F32)

    aggregate[...] = summed[...].astype(BF16)
    for copy in weights:
        copy.wait()
    span = hidden // 2

    def multiply(index):
        at = slice(index * chunk, (index + 1) * chunk)
        for begin in range(0, hidden, span):
            columns = slice(begin, begin + span)
            values[index % 2, :, columns] = jnp.dot(
                aggregate[at, :], weight[:, :, columns].reshape(width, span), preferred_element_type=F32
            )

    multiply(0)
    for index in range(parts):
        if index + 1 < parts:
            multiply(index + 1)
        totals[index].wait()
        cotangents[index].wait()
        for row in range(0, chunk, 32):
            at = slice(index * chunk + row, index * chunk + row + 32)
            for begin in range(0, hidden, span):
                columns = slice(begin, begin + span)
                value = values[index % 2, row : row + 32, columns] + total[at, columns].astype(F32)
                value = value.astype(BF16)
                square = value * value
                bend = jnp.tanh(value * (square * (SCALE * CUBIC) + SCALE))
                inner = value * (square * (1.5 * SCALE * CUBIC) + 0.5 * SCALE)
                grad[at, columns] = cotangent[at, columns] * ((1.0 + bend) * (inner * (1.0 - bend) + 0.5))

    for copy in inputs:
        copy.wait()
    moves = []
    for term, which in enumerate([1 - core, core]):
        for index, target in enumerate(out_hbms[2 * term : 2 * term + 2]):
            if not pieces:
                moves.append((index, which, both.at[index, which], target))
                continue
            row_bit, column_bit = (low, upper) if index else (1 - low, 1 - upper)
            for row in range(target.shape[0]):
                for side in range(2):
                    half = jnp.where(which == 0, side, column_bit)
                    place = 2 * row + jnp.where(which == 0, row_bit, side)
                    columns = slice(side * span, (side + 1) * span)
                    moves.append((half, which, both.at[half, which, place], target.at[row, :, columns]))
    contract = (((0,), (0,)), ((), ()))
    results = [
        pltpu.make_async_copy(source, target, out_sems.at[index]) for index, (_, _, source, target) in enumerate(moves)
    ]
    for half in range(2):
        columns = slice(half * span, (half + 1) * span)
        for index, operand in enumerate([features, aggregate]):
            product = lax.dot_general(operand[...], grad[:, columns], contract, preferred_element_type=F32)
            both[half, index] = product.astype(BF16).reshape(both.shape[2:])
            for move, result in zip(moves, results):
                pl.when(jnp.logical_and(move[0] == half, move[1] == index))(result.start)
    for result in results:
        result.wait()


def call(kernel, outs, places, out_places, scratch=(), flops=0, moved=0, vmem=56):
    return pl.pallas_call(
        kernel,
        out_shape=outs,
        in_specs=places,
        out_specs=out_places,
        scratch_shapes=list(scratch),
        compiler_params=pltpu.CompilerParams(vmem_limit_bytes=vmem * MIB),
        cost_estimate=pl.CostEstimate(flops=flops, bytes_accessed=moved, transcendentals=0),
    )


def joined(held, other, upper, axis):
    return jnp.stack([jnp.where(upper, other, held), jnp.where(upper, held, other)], axis=axis)


def gather_high(held, high):
    step = 1
    while step < lax.axis_size("rep") // 2:
        other = swap(held, "rep", 2 * step)
        upper = (high & step) != 0
        held = jnp.concatenate([jnp.where(upper, other, held), jnp.where(upper, held, other)], axis=-1)
        step *= 2
    return held


def added(terms):
    return sum(term.astype(F32) for term in terms).astype(BF16)


def half_of(value, axis, which):
    size = value.shape[axis] // 2
    return lax.dynamic_slice_in_dim(value, which * size, size, axis)


def first_pieces(term, depth, core, low, upper):
    term = term.reshape(-1, 2, depth, 2, term.shape[1] // 2)
    pieces = []
    for row_bit, column_bit in ((1 - low, 1 - upper), (low, upper)):
        rows = lax.dynamic_index_in_dim(term, row_bit, 1, keepdims=False)
        columns = lax.dynamic_index_in_dim(term, column_bit, 3, keepdims=False).swapaxes(1, 2)
        pieces.append(jnp.where(core == 0, rows, columns).reshape(term.shape[0], depth, -1))
    return pieces


def turn_swap(value, turn):
    reps, doms = lax.axis_size("rep"), lax.axis_size("dom")
    pairs = []
    for rep in range(reps):
        for dom in range(doms):
            target = rep * doms + (dom ^ 1) if rep % 2 == turn else (rep ^ (reps // 2)) * doms + dom
            pairs.append((rep * doms + dom, target))
    return lax.ppermute(value, ("rep", "dom"), pairs)


def column_half(term, which):
    size = term.shape[-1] // 2
    return lax.dynamic_slice_in_dim(term, which * size, size, term.ndim - 1)


def exchanged(term, take, which, axis, step):
    return added([take(term, which), swap(take(term, 1 - which), axis, step)])


def reduce_high(term, high, step):
    while step:
        term = exchanged(term, column_half, (high // step) % 2, "rep", 2 * step)
        step //= 2
    return term


def shards(features, cotangent, w_self, w_neigh, tile_vals, tile_src, tile_peer, in_block):
    dom_size = lax.axis_size("dom")
    rows, width = features.shape
    hidden = w_self.shape[1]
    block = tile_vals.shape[1]
    me = lax.axis_index("dom")
    rep = lax.axis_index("rep")
    parts = lax.axis_size("rep") // 2
    core, high = rep & 1, rep >> 1
    low, place = me & 1, me >> 1

    share = hidden // parts
    top = dom_size // 2
    held = jnp.stack([lax.dynamic_slice_in_dim(weight, high * share, share, 1) for weight in (w_self, w_neigh)])
    near, far = cross(held, 0), cross(held, top)
    slots = call(
        slots_kernel,
        jax.ShapeDtypeStruct((dom_size * block, width), BF16),
        [HBM] * 4,
        HBM,
        [
            pltpu.SMEM(tile_src.shape, jnp.int32),
            pltpu.SMEM(tile_peer.shape, jnp.int32),
            pltpu.VMEM(tile_vals.shape, BF16),
            pltpu.VMEM(features.shape, BF16),
            pltpu.VMEM((dom_size * block, rows), F32),
            pltpu.VMEM((dom_size * block, width), BF16),
            DMA((3, 4)),
            DMA((dom_size // 4,)),
        ],
        flops=2 * dom_size * block * rows * width,
        moved=tile_vals.size * 2 + rows * width * 4,
    )(tile_src, tile_peer, tile_vals, features)
    near, far, slots = lax.optimization_barrier((near, far, slots))
    held = joined(jnp.where(core == 0, held, near), far, (me & top) != 0, 1)
    step = top // 2
    while step > 1:
        held = joined(held, swap(held, "dom", step), (me & step) != 0, 2)
        held = held.reshape(2, -1, *held.shape[3:])
        step //= 2
    received = lax.all_to_all(slots.reshape(dom_size, block, width), "dom", split_axis=0, concat_axis=0, tiled=True)
    mine = gather_high(held, high)
    depth = width // dom_size
    tiled = depth % 16 == 0
    flip = low ^ core
    weights = [[mine[index], swap(mine[index], "rep", 1)] for index in range(2)]
    if not tiled:
        weights = [[joined(*weight, flip != 0, 1).reshape(-1, 128, hidden)] for weight in weights]
    sources, count = len(weights[0]), sum(weight.shape[0] for weight in weights[0])
    weight_shape = pltpu.VMEM((count, width // count, hidden), BF16)
    total = call(
        self_kernel,
        jax.ShapeDtypeStruct((rows, hidden), BF16),
        [SMEM] + [HBM] * (1 + sources),
        HBM,
        [
            pltpu.VMEM((rows, width), BF16),
            weight_shape,
            pltpu.VMEM((rows, hidden), BF16),
            DMA((4,)),
            DMA((count,)),
            DMA((rows // 256,)),
        ],
        flops=2 * rows * width * hidden,
        moved=7 * rows * hidden,
    )(flip.astype(jnp.int32).reshape(1), features, *weights[0])
    span = hidden // 2
    upper = (high // (parts // 2)) % 2
    places = jnp.stack([core, flip, low, upper]).astype(jnp.int32)
    if tiled:
        out_shapes = [jax.ShapeDtypeStruct((dom_size // 2, depth, hidden), BF16)] * 4
        product_shape = (2, 2, dom_size, depth, span)
    else:
        out_shapes = [jax.ShapeDtypeStruct((width, span), BF16)] * 4
        product_shape = (2, 2, width, span)
    outs = call(
        functools.partial(layer_kernel, sources, tiled),
        out_shapes,
        [SMEM, SMEM] + [HBM] * (4 + sources),
        [HBM] * 4,
        [
            pltpu.VMEM((dom_size, block, width), BF16),
            DMA((dom_size,)),
            pltpu.VMEM((rows, hidden), BF16),
            pltpu.VMEM((rows, width), BF16),
            pltpu.VMEM((rows, hidden), BF16),
            weight_shape,
            pltpu.VMEM((rows, width), F32),
            pltpu.VMEM((2, 256, hidden), F32),
            pltpu.VMEM((rows, width), BF16),
            pltpu.VMEM((rows, hidden), BF16),
            pltpu.VMEM(product_shape, BF16),
            DMA((2, rows // 256)),
            DMA((count,)),
            DMA((4,)),
            DMA((4 * dom_size,)),
        ],
        flops=6 * rows * width * hidden,
        moved=16 * rows * hidden,
    )(places, in_block, received, total, features, cotangent, *weights[1])
    sent, kept = outs[:2], outs[2:]
    if not tiled:
        sent, kept = [
            first_pieces(jnp.concatenate(pair, axis=1), depth, which, low, upper)
            for pair, which in ((sent, 1 - core), (kept, core))
        ]
    leave, stay = [[own, swap(piece, "rep", 1)] for own, piece in zip(kept, sent)]
    bit = jnp.where(core == 0, upper, low)
    halves = []
    size = dom_size // 4
    for begin in (0, size):
        gone, kept = [[term[begin : begin + size] for term in terms] for terms in (leave, stay)]
        held = added([*kept, turn_swap(added(gone), 0)])
        halves.append(added([column_half(held, bit), turn_swap(column_half(held, 1 - bit), 1)]))
    held = jnp.concatenate(halves)
    both = reduce_high(held, high, parts // 4)
    summed = lax.dynamic_index_in_dim(both, place, 0, keepdims=False).astype(F32)
    for step in range(1, dom_size // 2):
        piece = lax.dynamic_index_in_dim(both, place ^ step, 0, keepdims=False)
        summed = summed + swap(piece, "dom", 2 * step).astype(F32)
    summed = summed.astype(BF16)
    whole = gather_high(summed, high)
    opposite = swap(whole, "rep", 1)
    return (
        jnp.where(core == 0, whole, opposite).astype(F32),
        jnp.where(core == 0, opposite, whole).astype(F32),
    )


def solution(mesh):
    in_specs = (
        P(("rep", "dom"), None),
        P(("rep", "dom"), None),
        P("dom", None),
        P("dom", None),
        P(("rep", "dom"), None, None),
        P(("rep", "dom")),
        P(("rep", "dom")),
        P(("rep", "dom")),
    )
    out_specs = (P("dom", None), P("dom", None))
    return jax.shard_map(shards, mesh=mesh, in_specs=in_specs, out_specs=out_specs, check_vma=False)
```

```python
import functools

import jax
import jax.numpy as jnp
from jax import lax
from jax.experimental import pallas as pl
from jax.experimental.pallas import tpu as pltpu
from jax.sharding import PartitionSpec as P

F32 = jnp.float32
BF16 = jnp.bfloat16
SCALE = 0.7978845608
CUBIC = 0.044715
MIB = 1 << 20
ANY = pl.BlockSpec(memory_space=pl.ANY)
HBM = pl.BlockSpec(memory_space=pltpu.HBM)
SMEM = pl.BlockSpec(memory_space=pltpu.SMEM)
VMEM = pl.BlockSpec(memory_space=pltpu.VMEM)
DMA = pltpu.SemaphoreType.DMA


def swap(value, axis, step):
    size = lax.axis_size(axis)
    return lax.ppermute(value, axis, [(index, index ^ step) for index in range(size)])


def cross(value, step):
    reps, doms = lax.axis_size("rep"), lax.axis_size("dom")
    pairs = [
        (rep * doms + dom, rep * doms + (dom ^ step ^ (rep & 1))) for rep in range(reps) for dom in range(doms)
    ]
    return lax.ppermute(value, ("rep", "dom"), [(source, target) for source, target in pairs if source != target])


def split_copies(source, target, sems, count=4):
    size = source.shape[0] // count
    return [
        pltpu.make_async_copy(
            source.at[index * size : (index + 1) * size], target.at[index * size : (index + 1) * size], sems.at[index]
        )
        for index in range(count)
    ]


def slots_kernel(
    src_hbm, peer_hbm, tiles_hbm, features_hbm, out_hbm, src, peer, tiles, features, dense, out, in_sems, out_sems
):
    scalars = [
        pltpu.make_async_copy(src_hbm, src, in_sems.at[2, 0]),
        pltpu.make_async_copy(peer_hbm, peer, in_sems.at[2, 1]),
    ]
    tile_copies = split_copies(tiles_hbm, tiles, in_sems.at[0])
    feature_copies = split_copies(features_hbm, features, in_sems.at[1])
    for copy in scalars + tile_copies + feature_copies:
        copy.start()
    count, block, _ = tiles.shape
    dense[...] = jnp.zeros_like(dense)
    for copy in scalars + tile_copies:
        copy.wait()

    def place(tile, carry):
        row = pl.multiple_of(peer[tile] * block, block)
        column = pl.multiple_of(src[tile] * block, block)
        at = (pl.ds(row, block), pl.ds(column, block))
        dense[at] = dense[at] + tiles[tile].astype(F32)
        return carry

    lax.fori_loop(0, count, place, 0)
    for copy in feature_copies:
        copy.wait()
    chunk = 4 * block
    results = []
    for index in range(out.shape[0] // chunk):
        at = slice(index * chunk, (index + 1) * chunk)
        out[at, :] = jnp.dot(dense[at, :].astype(BF16), features[...], preferred_element_type=F32).astype(BF16)
        results.append(pltpu.make_async_copy(out.at[at, :], out_hbm.at[at, :], out_sems.at[index]))
        results[-1].start()
    for result in results:
        result.wait()


def weight_copies(flip, weight_hbms, weight, sems):
    sources = len(weight_hbms)
    copies = []
    for source, weight_hbm in enumerate(weight_hbms):
        for piece in range(weight_hbm.shape[0]):
            target = piece if sources == 1 else 2 * piece + (flip ^ source)
            copies.append(
                pltpu.make_async_copy(weight_hbm.at[piece], weight.at[target], sems.at[sources * piece + source])
            )
    return copies


def self_kernel(flip_ref, features_hbm, *refs):
    *weight_hbms, out_hbm, features, weight, out, feature_sems, weight_sems, out_sems = refs
    rows, width = features.shape
    hidden = out.shape[1]
    copies = weight_copies(flip_ref[0], weight_hbms, weight, weight_sems)
    copies += split_copies(features_hbm, features, feature_sems)
    for copy in copies:
        copy.start()
    for copy in copies:
        copy.wait()
    chunk = 256
    results = split_copies(out, out_hbm, out_sems, rows // chunk)
    for index, result in enumerate(results):
        at = slice(index * chunk, (index + 1) * chunk)
        out[at, :] = jnp.dot(
            features[at, :], weight[...].reshape(width, hidden), preferred_element_type=F32
        ).astype(BF16)
        result.start()
    for result in results:
        result.wait()


def layer_kernel(
    sources, pieces, places_ref, into_ref, slots_hbm, total_hbm, features_hbm, cotangent_hbm, *refs
):
    weight_hbms, out_hbms = refs[:sources], refs[sources:-15]
    slots, slot_sems = refs[-15:-13]
    total, features, cotangent, weight, summed, values, aggregate, grad, both = refs[-13:-4]
    row_sems, weight_sems, feature_sems, out_sems = refs[-4:]
    senders, block, _ = slots.shape
    rows, hidden = grad.shape
    width = aggregate.shape[1]
    core, flip, low, upper = [places_ref[index] for index in range(4)]
    chunk = 256
    parts = rows // chunk
    weights = weight_copies(flip, weight_hbms, weight, weight_sems)
    totals = split_copies(total_hbm, total, row_sems.at[0], parts)
    cotangents = split_copies(cotangent_hbm, cotangent, row_sems.at[1], parts)
    inputs = split_copies(features_hbm, features, feature_sems)
    arrivals = [
        pltpu.make_async_copy(slots_hbm.at[sender], slots.at[sender], slot_sems.at[sender]) for sender in range(senders)
    ]
    for copy in arrivals + weights + totals[:1] + cotangents[:1]:
        copy.start()

    def target(sender):
        return pl.ds(pl.multiple_of(into_ref[sender] * block, block), block)

    for index in range(rows // block):
        reached = functools.reduce(jnp.logical_or, [into_ref[sender] == index for sender in range(senders)])

        @pl.when(jnp.logical_not(reached))
        def _():
            summed[index * block : (index + 1) * block, :] = jnp.zeros((block, width), F32)

    for copy in arrivals:
        copy.wait()
    for copy in [copy for pair in zip(totals[1:], cotangents[1:]) for copy in pair] + inputs:
        copy.start()
    for sender in range(senders):
        if sender == 0:
            summed[target(0), :] = slots[0].astype(F32)
            continue
        again = functools.reduce(jnp.logical_or, [into_ref[sender] == into_ref[index] for index in range(sender)])

        @pl.when(again)
        def _():
            summed[target(sender), :] = summed[target(sender), :] + slots[sender].astype(F32)

        @pl.when(jnp.logical_not(again))
        def _():
            summed[target(sender), :] = slots[sender].astype(F32)

    aggregate[...] = summed[...].astype(BF16)
    for copy in weights:
        copy.wait()
    span = hidden // 2

    def multiply(index):
        at = slice(index * chunk, (index + 1) * chunk)
        for begin in range(0, hidden, span):
            columns = slice(begin, begin + span)
            values[index % 2, :, columns] = jnp.dot(
                aggregate[at, :], weight[:, :, columns].reshape(width, span), preferred_element_type=F32
            )

    multiply(0)
    for index in range(parts):
        if index + 1 < parts:
            multiply(index + 1)
        totals[index].wait()
        cotangents[index].wait()
        for row in range(0, chunk, 32):
            at = slice(index * chunk + row, index * chunk + row + 32)
            for begin in range(0, hidden, span):
                columns = slice(begin, begin + span)
                value = values[index % 2, row : row + 32, columns] + total[at, columns].astype(F32)
                value = value.astype(BF16)
                square = value * value
                bend = jnp.tanh(value * (square * (SCALE * CUBIC) + SCALE))
                inner = value * (square * (1.5 * SCALE * CUBIC) + 0.5 * SCALE)
                grad[at, columns] = cotangent[at, columns] * ((1.0 + bend) * (inner * (1.0 - bend) + 0.5))

    for copy in inputs:
        copy.wait()
    moves = []
    for term, which in enumerate([1 - core, core]):
        for index, target in enumerate(out_hbms[2 * term : 2 * term + 2]):
            if not pieces:
                moves.append((index, which, both.at[index, which], target))
                continue
            row_bit, column_bit = (low, upper) if index else (1 - low, 1 - upper)
            for row in range(target.shape[0]):
                for side in range(2):
                    half = jnp.where(which == 0, side, column_bit)
                    place = 2 * row + jnp.where(which == 0, row_bit, side)
                    columns = slice(side * span, (side + 1) * span)
                    moves.append((half, which, both.at[half, which, place], target.at[row, :, columns]))
    contract = (((0,), (0,)), ((), ()))
    results = [
        pltpu.make_async_copy(source, target, out_sems.at[index]) for index, (_, _, source, target) in enumerate(moves)
    ]
    for half in range(2):
        columns = slice(half * span, (half + 1) * span)
        for index, operand in enumerate([features, aggregate]):
            product = lax.dot_general(operand[...], grad[:, columns], contract, preferred_element_type=F32)
            both[half, index] = product.astype(BF16).reshape(both.shape[2:])
            for move, result in zip(moves, results):
                pl.when(jnp.logical_and(move[0] == half, move[1] == index))(result.start)
    for result in results:
        result.wait()


def call(kernel, outs, places, out_places, scratch=(), flops=0, moved=0, vmem=56):
    return pl.pallas_call(
        kernel,
        out_shape=outs,
        in_specs=places,
        out_specs=out_places,
        scratch_shapes=list(scratch),
        compiler_params=pltpu.CompilerParams(vmem_limit_bytes=vmem * MIB),
        cost_estimate=pl.CostEstimate(flops=flops, bytes_accessed=moved, transcendentals=0),
    )


def joined(held, other, upper, axis):
    return jnp.stack([jnp.where(upper, other, held), jnp.where(upper, held, other)], axis=axis)


def gather_high(held, high):
    step = 1
    while step < lax.axis_size("rep") // 2:
        other = swap(held, "rep", 2 * step)
        upper = (high & step) != 0
        held = jnp.concatenate([jnp.where(upper, other, held), jnp.where(upper, held, other)], axis=-1)
        step *= 2
    return held


def added(terms):
    return sum(term.astype(F32) for term in terms).astype(BF16)


def half_of(value, axis, which):
    size = value.shape[axis] // 2
    return lax.dynamic_slice_in_dim(value, which * size, size, axis)


def first_pieces(term, depth, core, low, upper):
    term = term.reshape(-1, 2, depth, 2, term.shape[1] // 2)
    pieces = []
    for row_bit, column_bit in ((1 - low, 1 - upper), (low, upper)):
        rows = lax.dynamic_index_in_dim(term, row_bit, 1, keepdims=False)
        columns = lax.dynamic_index_in_dim(term, column_bit, 3, keepdims=False).swapaxes(1, 2)
        pieces.append(jnp.where(core == 0, rows, columns).reshape(term.shape[0], depth, -1))
    return pieces


def turn_swap(value, turn):
    reps, doms = lax.axis_size("rep"), lax.axis_size("dom")
    pairs = []
    for rep in range(reps):
        for dom in range(doms):
            target = rep * doms + (dom ^ 1) if rep % 2 == turn else (rep ^ (reps // 2)) * doms + dom
            pairs.append((rep * doms + dom, target))
    return lax.ppermute(value, ("rep", "dom"), pairs)


def column_half(term, which):
    size = term.shape[-1] // 2
    return lax.dynamic_slice_in_dim(term, which * size, size, term.ndim - 1)


def exchanged(term, take, which, axis, step):
    return added([take(term, which), swap(take(term, 1 - which), axis, step)])


def reduce_high(term, high, step):
    while step:
        term = exchanged(term, column_half, (high // step) % 2, "rep", 2 * step)
        step //= 2
    return term


def shards(features, cotangent, w_self, w_neigh, tile_vals, tile_src, tile_peer, in_block):
    dom_size = lax.axis_size("dom")
    rows, width = features.shape
    hidden = w_self.shape[1]
    block = tile_vals.shape[1]
    me = lax.axis_index("dom")
    rep = lax.axis_index("rep")
    parts = lax.axis_size("rep") // 2
    core, high = rep & 1, rep >> 1
    low, place = me & 1, me >> 1

    share = hidden // parts
    top = dom_size // 2
    held = jnp.stack([lax.dynamic_slice_in_dim(weight, high * share, share, 1) for weight in (w_self, w_neigh)])
    near, far = cross(held, 0), cross(held, top)
    slots = call(
        slots_kernel,
        jax.ShapeDtypeStruct((dom_size * block, width), BF16),
        [HBM] * 4,
        HBM,
        [
            pltpu.SMEM(tile_src.shape, jnp.int32),
            pltpu.SMEM(tile_peer.shape, jnp.int32),
            pltpu.VMEM(tile_vals.shape, BF16),
            pltpu.VMEM(features.shape, BF16),
            pltpu.VMEM((dom_size * block, rows), F32),
            pltpu.VMEM((dom_size * block, width), BF16),
            DMA((3, 4)),
            DMA((dom_size // 4,)),
        ],
        flops=2 * dom_size * block * rows * width,
        moved=tile_vals.size * 2 + rows * width * 4,
    )(tile_src, tile_peer, tile_vals, features)
    near, far, slots = lax.optimization_barrier((near, far, slots))
    held = joined(jnp.where(core == 0, held, near), far, (me & top) != 0, 1)
    step = top // 2
    while step > 1:
        held = joined(held, swap(held, "dom", step), (me & step) != 0, 2)
        held = held.reshape(2, -1, *held.shape[3:])
        step //= 2
    received = lax.all_to_all(slots.reshape(dom_size, block, width), "dom", split_axis=0, concat_axis=0, tiled=True)
    mine = gather_high(held, high)
    depth = width // dom_size
    tiled = depth % 16 == 0
    flip = low ^ core
    weights = [[mine[index], swap(mine[index], "rep", 1)] for index in range(2)]
    if not tiled:
        weights = [[joined(*weight, flip != 0, 1).reshape(-1, 128, hidden)] for weight in weights]
    sources, count = len(weights[0]), sum(weight.shape[0] for weight in weights[0])
    weight_shape = pltpu.VMEM((count, width // count, hidden), BF16)
    total = call(
        self_kernel,
        jax.ShapeDtypeStruct((rows, hidden), BF16),
        [SMEM] + [HBM] * (1 + sources),
        HBM,
        [
            pltpu.VMEM((rows, width), BF16),
            weight_shape,
            pltpu.VMEM((rows, hidden), BF16),
            DMA((4,)),
            DMA((count,)),
            DMA((rows // 256,)),
        ],
        flops=2 * rows * width * hidden,
        moved=7 * rows * hidden,
    )(flip.astype(jnp.int32).reshape(1), features, *weights[0])
    span = hidden // 2
    upper = (high // (parts // 2)) % 2
    places = jnp.stack([core, flip, low, upper]).astype(jnp.int32)
    if tiled:
        out_shapes = [jax.ShapeDtypeStruct((dom_size // 2, depth, hidden), BF16)] * 4
        product_shape = (2, 2, dom_size, depth, span)
    else:
        out_shapes = [jax.ShapeDtypeStruct((width, span), BF16)] * 4
        product_shape = (2, 2, width, span)
    outs = call(
        functools.partial(layer_kernel, sources, tiled),
        out_shapes,
        [SMEM, SMEM, ANY] + [HBM] * (3 + sources),
        [HBM] * 4,
        [
            pltpu.VMEM((dom_size, block, width), BF16),
            DMA((dom_size,)),
            pltpu.VMEM((rows, hidden), BF16),
            pltpu.VMEM((rows, width), BF16),
            pltpu.VMEM((rows, hidden), BF16),
            weight_shape,
            pltpu.VMEM((rows, width), F32),
            pltpu.VMEM((2, 256, hidden), F32),
            pltpu.VMEM((rows, width), BF16),
            pltpu.VMEM((rows, hidden), BF16),
            pltpu.VMEM(product_shape, BF16),
            DMA((2, rows // 256)),
            DMA((count,)),
            DMA((4,)),
            DMA((4 * dom_size,)),
        ],
        flops=6 * rows * width * hidden,
        moved=16 * rows * hidden,
        vmem=54,
    )(places, in_block, received, total, features, cotangent, *weights[1])
    sent, kept = outs[:2], outs[2:]
    if not tiled:
        sent, kept = [
            first_pieces(jnp.concatenate(pair, axis=1), depth, which, low, upper)
            for pair, which in ((sent, 1 - core), (kept, core))
        ]
    leave, stay = [[own, swap(piece, "rep", 1)] for own, piece in zip(kept, sent)]
    bit = jnp.where(core == 0, upper, low)
    halves = []
    size = dom_size // 4
    for begin in (0, size):
        gone, kept = [[term[begin : begin + size] for term in terms] for terms in (leave, stay)]
        gone, *leave = lax.optimization_barrier((added(gone), *leave))
        held = added([*kept, turn_swap(gone, 0)])
        halves.append(added([column_half(held, bit), turn_swap(column_half(held, 1 - bit), 1)]))
    held = jnp.concatenate(halves)
    both = reduce_high(held, high, parts // 4)
    summed = lax.dynamic_index_in_dim(both, place, 0, keepdims=False).astype(F32)
    for step in range(1, dom_size // 2):
        piece = lax.dynamic_index_in_dim(both, place ^ step, 0, keepdims=False)
        summed = summed + swap(piece, "dom", 2 * step).astype(F32)
    summed = summed.astype(BF16)
    whole = gather_high(summed, high)
    opposite = swap(whole, "rep", 1)
    return (
        jnp.where(core == 0, whole, opposite).astype(F32),
        jnp.where(core == 0, opposite, whole).astype(F32),
    )


def solution(mesh):
    in_specs = (
        P(("rep", "dom"), None),
        P(("rep", "dom"), None),
        P("dom", None),
        P("dom", None),
        P(("rep", "dom"), None, None),
        P(("rep", "dom")),
        P(("rep", "dom")),
        P(("rep", "dom")),
    )
    out_specs = (P("dom", None), P("dom", None))
    return jax.shard_map(shards, mesh=mesh, in_specs=in_specs, out_specs=out_specs, check_vma=False)
```

```python
import functools

import jax
import jax.numpy as jnp
from jax import lax
from jax.experimental import pallas as pl
from jax.experimental.pallas import tpu as pltpu
from jax.sharding import PartitionSpec as P

F32 = jnp.float32
BF16 = jnp.bfloat16
SCALE = 0.7978845608
CUBIC = 0.044715
MIB = 1 << 20
HBM = pl.BlockSpec(memory_space=pltpu.HBM)
SMEM = pl.BlockSpec(memory_space=pltpu.SMEM)
VMEM = pl.BlockSpec(memory_space=pltpu.VMEM)
DMA = pltpu.SemaphoreType.DMA


def swap(value, axis, step):
    size = lax.axis_size(axis)
    return lax.ppermute(value, axis, [(index, index ^ step) for index in range(size)])


def cross(value, step):
    reps, doms = lax.axis_size("rep"), lax.axis_size("dom")
    pairs = [
        (rep * doms + dom, rep * doms + (dom ^ step ^ (rep & 1))) for rep in range(reps) for dom in range(doms)
    ]
    return lax.ppermute(value, ("rep", "dom"), [(source, target) for source, target in pairs if source != target])


def split_copies(source, target, sems, count=4):
    size = source.shape[0] // count
    return [
        pltpu.make_async_copy(
            source.at[index * size : (index + 1) * size], target.at[index * size : (index + 1) * size], sems.at[index]
        )
        for index in range(count)
    ]


def slots_kernel(
    src_hbm, peer_hbm, tiles_hbm, features_hbm, out_hbm, src, peer, tiles, features, dense, out, in_sems, out_sems
):
    scalars = [
        pltpu.make_async_copy(src_hbm, src, in_sems.at[2, 0]),
        pltpu.make_async_copy(peer_hbm, peer, in_sems.at[2, 1]),
    ]
    tile_copies = split_copies(tiles_hbm, tiles, in_sems.at[0])
    feature_copies = split_copies(features_hbm, features, in_sems.at[1])
    for copy in scalars + tile_copies + feature_copies:
        copy.start()
    count, block, _ = tiles.shape
    dense[...] = jnp.zeros_like(dense)
    for copy in scalars + tile_copies:
        copy.wait()

    def place(tile, carry):
        row = pl.multiple_of(peer[tile] * block, block)
        column = pl.multiple_of(src[tile] * block, block)
        at = (pl.ds(row, block), pl.ds(column, block))
        dense[at] = dense[at] + tiles[tile].astype(F32)
        return carry

    lax.fori_loop(0, count, place, 0)
    for copy in feature_copies:
        copy.wait()
    chunk = 4 * block
    results = []
    for index in range(out.shape[0] // chunk):
        at = slice(index * chunk, (index + 1) * chunk)
        out[at, :] = jnp.dot(dense[at, :].astype(BF16), features[...], preferred_element_type=F32).astype(BF16)
        results.append(pltpu.make_async_copy(out.at[at, :], out_hbm.at[at, :], out_sems.at[index]))
        results[-1].start()
    for result in results:
        result.wait()


def weight_copies(flip, weight_hbms, weight, sems):
    sources = len(weight_hbms)
    copies = []
    for source, weight_hbm in enumerate(weight_hbms):
        for piece in range(weight_hbm.shape[0]):
            target = piece if sources == 1 else 2 * piece + (flip ^ source)
            copies.append(
                pltpu.make_async_copy(weight_hbm.at[piece], weight.at[target], sems.at[sources * piece + source])
            )
    return copies


def self_kernel(flip_ref, features_hbm, *refs):
    *weight_hbms, out_hbm, features, weight, out, feature_sems, weight_sems, out_sems = refs
    rows, width = features.shape
    hidden = out.shape[1]
    copies = weight_copies(flip_ref[0], weight_hbms, weight, weight_sems)
    copies += split_copies(features_hbm, features, feature_sems)
    for copy in copies:
        copy.start()
    for copy in copies:
        copy.wait()
    chunk = 256
    results = split_copies(out, out_hbm, out_sems, rows // chunk)
    for index, result in enumerate(results):
        at = slice(index * chunk, (index + 1) * chunk)
        out[at, :] = jnp.dot(
            features[at, :], weight[...].reshape(width, hidden), preferred_element_type=F32
        ).astype(BF16)
        result.start()
    for result in results:
        result.wait()


def layer_kernel(
    sources, pieces, places_ref, into_ref, slots_hbm, total_hbm, features_hbm, cotangent_hbm, *refs
):
    weight_hbms, out_hbms = refs[:sources], refs[sources:-15]
    slots, slot_sems = refs[-15:-13]
    total, features, cotangent, weight, summed, values, aggregate, grad, both = refs[-13:-4]
    row_sems, weight_sems, feature_sems, out_sems = refs[-4:]
    senders, block, _ = slots.shape
    rows, hidden = grad.shape
    width = aggregate.shape[1]
    core, flip, low, upper = [places_ref[index] for index in range(4)]
    chunk = 256
    parts = rows // chunk
    weights = weight_copies(flip, weight_hbms, weight, weight_sems)
    totals = split_copies(total_hbm, total, row_sems.at[0], parts)
    cotangents = split_copies(cotangent_hbm, cotangent, row_sems.at[1], parts)
    inputs = split_copies(features_hbm, features, feature_sems)
    arrivals = [
        pltpu.make_async_copy(slots_hbm.at[sender], slots.at[sender], slot_sems.at[sender]) for sender in range(senders)
    ]
    for copy in arrivals + weights + totals[:1] + cotangents[:1]:
        copy.start()

    def target(sender):
        return pl.ds(pl.multiple_of(into_ref[sender] * block, block), block)

    for index in range(rows // block):
        reached = functools.reduce(jnp.logical_or, [into_ref[sender] == index for sender in range(senders)])

        @pl.when(jnp.logical_not(reached))
        def _():
            summed[index * block : (index + 1) * block, :] = jnp.zeros((block, width), F32)

    for copy in arrivals:
        copy.wait()
    for copy in [copy for pair in zip(totals[1:], cotangents[1:]) for copy in pair] + inputs:
        copy.start()
    for sender in range(senders):
        if sender == 0:
            summed[target(0), :] = slots[0].astype(F32)
            continue
        again = functools.reduce(jnp.logical_or, [into_ref[sender] == into_ref[index] for index in range(sender)])

        @pl.when(again)
        def _():
            summed[target(sender), :] = summed[target(sender), :] + slots[sender].astype(F32)

        @pl.when(jnp.logical_not(again))
        def _():
            summed[target(sender), :] = slots[sender].astype(F32)

    aggregate[...] = summed[...].astype(BF16)
    for copy in weights:
        copy.wait()
    span = hidden // 2

    def multiply(index):
        at = slice(index * chunk, (index + 1) * chunk)
        for begin in range(0, hidden, span):
            columns = slice(begin, begin + span)
            values[index % 2, :, columns] = jnp.dot(
                aggregate[at, :], weight[:, :, columns].reshape(width, span), preferred_element_type=F32
            )

    multiply(0)
    for index in range(parts):
        if index + 1 < parts:
            multiply(index + 1)
        totals[index].wait()
        cotangents[index].wait()
        for row in range(0, chunk, 16):
            at = slice(index * chunk + row, index * chunk + row + 16)
            for begin in range(0, hidden, span):
                columns = slice(begin, begin + span)
                value = values[index % 2, row : row + 16, columns] + total[at, columns].astype(F32)
                square = value * value
                bend = jnp.tanh(value * (square * (SCALE * CUBIC) + SCALE))
                inner = value * (square * (1.5 * SCALE * CUBIC) + 0.5 * SCALE)
                slope = (1.0 + bend) * (inner * (1.0 - bend) + 0.5)
                grad[at, columns] = (cotangent[at, columns].astype(F32) * slope).astype(BF16)

    for copy in inputs:
        copy.wait()
    moves = []
    for term, which in enumerate([1 - core, core]):
        for index, target in enumerate(out_hbms[2 * term : 2 * term + 2]):
            if not pieces:
                moves.append((index, which, both.at[index, which], target))
                continue
            row_bit, column_bit = (low, upper) if index else (1 - low, 1 - upper)
            for row in range(target.shape[0]):
                for side in range(2):
                    half = jnp.where(which == 0, side, column_bit)
                    place = 2 * row + jnp.where(which == 0, row_bit, side)
                    columns = slice(side * span, (side + 1) * span)
                    moves.append((half, which, both.at[half, which, place], target.at[row, :, columns]))
    contract = (((0,), (0,)), ((), ()))
    results = [
        pltpu.make_async_copy(source, target, out_sems.at[index]) for index, (_, _, source, target) in enumerate(moves)
    ]
    for half in range(2):
        columns = slice(half * span, (half + 1) * span)
        for index, operand in enumerate([features, aggregate]):
            product = lax.dot_general(operand[...], grad[:, columns], contract, preferred_element_type=F32)
            both[half, index] = product.astype(BF16).reshape(both.shape[2:])
            for move, result in zip(moves, results):
                pl.when(jnp.logical_and(move[0] == half, move[1] == index))(result.start)
    for result in results:
        result.wait()


def call(kernel, outs, places, out_places, scratch=(), flops=0, moved=0, vmem=56):
    return pl.pallas_call(
        kernel,
        out_shape=outs,
        in_specs=places,
        out_specs=out_places,
        scratch_shapes=list(scratch),
        compiler_params=pltpu.CompilerParams(vmem_limit_bytes=vmem * MIB),
        cost_estimate=pl.CostEstimate(flops=flops, bytes_accessed=moved, transcendentals=0),
    )


def joined(held, other, upper, axis):
    return jnp.stack([jnp.where(upper, other, held), jnp.where(upper, held, other)], axis=axis)


def gather_high(held, high):
    step = 1
    while step < lax.axis_size("rep") // 2:
        other = swap(held, "rep", 2 * step)
        upper = (high & step) != 0
        held = jnp.concatenate([jnp.where(upper, other, held), jnp.where(upper, held, other)], axis=-1)
        step *= 2
    return held


def added(terms):
    return sum(term.astype(F32) for term in terms).astype(BF16)


def half_of(value, axis, which):
    size = value.shape[axis] // 2
    return lax.dynamic_slice_in_dim(value, which * size, size, axis)


def first_pieces(term, depth, core, low, upper):
    term = term.reshape(-1, 2, depth, 2, term.shape[1] // 2)
    pieces = []
    for row_bit, column_bit in ((1 - low, 1 - upper), (low, upper)):
        rows = lax.dynamic_index_in_dim(term, row_bit, 1, keepdims=False)
        columns = lax.dynamic_index_in_dim(term, column_bit, 3, keepdims=False).swapaxes(1, 2)
        pieces.append(jnp.where(core == 0, rows, columns).reshape(term.shape[0], depth, -1))
    return pieces


def turn_swap(value, turn):
    reps, doms = lax.axis_size("rep"), lax.axis_size("dom")
    pairs = []
    for rep in range(reps):
        for dom in range(doms):
            target = rep * doms + (dom ^ 1) if rep % 2 == turn else (rep ^ (reps // 2)) * doms + dom
            pairs.append((rep * doms + dom, target))
    return lax.ppermute(value, ("rep", "dom"), pairs)


def column_half(term, which):
    size = term.shape[-1] // 2
    return lax.dynamic_slice_in_dim(term, which * size, size, term.ndim - 1)


def exchanged(term, take, which, axis, step):
    return added([take(term, which), swap(take(term, 1 - which), axis, step)])


def reduce_high(term, high, step):
    while step:
        term = exchanged(term, column_half, (high // step) % 2, "rep", 2 * step)
        step //= 2
    return term


def shards(features, cotangent, w_self, w_neigh, tile_vals, tile_src, tile_peer, in_block):
    dom_size = lax.axis_size("dom")
    rows, width = features.shape
    hidden = w_self.shape[1]
    block = tile_vals.shape[1]
    me = lax.axis_index("dom")
    rep = lax.axis_index("rep")
    parts = lax.axis_size("rep") // 2
    core, high = rep & 1, rep >> 1
    low, place = me & 1, me >> 1

    share = hidden // parts
    top = dom_size // 2
    held = jnp.stack([lax.dynamic_slice_in_dim(weight, high * share, share, 1) for weight in (w_self, w_neigh)])
    near, far = cross(held, 0), cross(held, top)
    slots = call(
        slots_kernel,
        jax.ShapeDtypeStruct((dom_size * block, width), BF16),
        [HBM] * 4,
        HBM,
        [
            pltpu.SMEM(tile_src.shape, jnp.int32),
            pltpu.SMEM(tile_peer.shape, jnp.int32),
            pltpu.VMEM(tile_vals.shape, BF16),
            pltpu.VMEM(features.shape, BF16),
            pltpu.VMEM((dom_size * block, rows), F32),
            pltpu.VMEM((dom_size * block, width), BF16),
            DMA((3, 4)),
            DMA((dom_size // 4,)),
        ],
        flops=2 * dom_size * block * rows * width,
        moved=tile_vals.size * 2 + rows * width * 4,
    )(tile_src, tile_peer, tile_vals, features)
    near, far, slots = lax.optimization_barrier((near, far, slots))
    held = joined(jnp.where(core == 0, held, near), far, (me & top) != 0, 1)
    step = top // 2
    while step > 1:
        held = joined(held, swap(held, "dom", step), (me & step) != 0, 2)
        held = held.reshape(2, -1, *held.shape[3:])
        step //= 2
    received = lax.all_to_all(slots.reshape(dom_size, block, width), "dom", split_axis=0, concat_axis=0, tiled=True)
    mine = gather_high(held, high)
    depth = width // dom_size
    tiled = depth % 16 == 0
    flip = low ^ core
    weights = [[mine[index], swap(mine[index], "rep", 1)] for index in range(2)]
    if not tiled:
        weights = [[joined(*weight, flip != 0, 1).reshape(-1, 128, hidden)] for weight in weights]
    sources, count = len(weights[0]), sum(weight.shape[0] for weight in weights[0])
    weight_shape = pltpu.VMEM((count, width // count, hidden), BF16)
    total = call(
        self_kernel,
        jax.ShapeDtypeStruct((rows, hidden), BF16),
        [SMEM] + [HBM] * (1 + sources),
        HBM,
        [
            pltpu.VMEM((rows, width), BF16),
            weight_shape,
            pltpu.VMEM((rows, hidden), BF16),
            DMA((4,)),
            DMA((count,)),
            DMA((rows // 256,)),
        ],
        flops=2 * rows * width * hidden,
        moved=7 * rows * hidden,
    )(flip.astype(jnp.int32).reshape(1), features, *weights[0])
    span = hidden // 2
    upper = (high // (parts // 2)) % 2
    places = jnp.stack([core, flip, low, upper]).astype(jnp.int32)
    if tiled:
        out_shapes = [jax.ShapeDtypeStruct((dom_size // 2, depth, hidden), BF16)] * 4
        product_shape = (2, 2, dom_size, depth, span)
    else:
        out_shapes = [jax.ShapeDtypeStruct((width, span), BF16)] * 4
        product_shape = (2, 2, width, span)
    outs = call(
        functools.partial(layer_kernel, sources, tiled),
        out_shapes,
        [SMEM, SMEM] + [HBM] * (4 + sources),
        [HBM] * 4,
        [
            pltpu.VMEM((dom_size, block, width), BF16),
            DMA((dom_size,)),
            pltpu.VMEM((rows, hidden), BF16),
            pltpu.VMEM((rows, width), BF16),
            pltpu.VMEM((rows, hidden), BF16),
            weight_shape,
            pltpu.VMEM((rows, width), F32),
            pltpu.VMEM((2, 256, hidden), F32),
            pltpu.VMEM((rows, width), BF16),
            pltpu.VMEM((rows, hidden), BF16),
            pltpu.VMEM(product_shape, BF16),
            DMA((2, rows // 256)),
            DMA((count,)),
            DMA((4,)),
            DMA((4 * dom_size,)),
        ],
        flops=6 * rows * width * hidden,
        moved=16 * rows * hidden,
    )(places, in_block, received, total, features, cotangent, *weights[1])
    sent, kept = outs[:2], outs[2:]
    if not tiled:
        sent, kept = [
            first_pieces(jnp.concatenate(pair, axis=1), depth, which, low, upper)
            for pair, which in ((sent, 1 - core), (kept, core))
        ]
    leave, stay = [[own, swap(piece, "rep", 1)] for own, piece in zip(kept, sent)]
    bit = jnp.where(core == 0, upper, low)
    halves = []
    size = dom_size // 4
    for begin in (0, size):
        gone, kept = [[term[begin : begin + size] for term in terms] for terms in (leave, stay)]
        held = added([*kept, turn_swap(added(gone), 0)])
        halves.append(added([column_half(held, bit), turn_swap(column_half(held, 1 - bit), 1)]))
    held = jnp.concatenate(halves)
    both = reduce_high(held, high, parts // 4)
    summed = lax.dynamic_index_in_dim(both, place, 0, keepdims=False).astype(F32)
    for step in range(1, dom_size // 2):
        piece = lax.dynamic_index_in_dim(both, place ^ step, 0, keepdims=False)
        summed = summed + swap(piece, "dom", 2 * step).astype(F32)
    summed = summed.astype(BF16)
    whole = gather_high(summed, high)
    opposite = swap(whole, "rep", 1)
    return (
        jnp.where(core == 0, whole, opposite).astype(F32),
        jnp.where(core == 0, opposite, whole).astype(F32),
    )


def solution(mesh):
    in_specs = (
        P(("rep", "dom"), None),
        P(("rep", "dom"), None),
        P("dom", None),
        P("dom", None),
        P(("rep", "dom"), None, None),
        P(("rep", "dom")),
        P(("rep", "dom")),
        P(("rep", "dom")),
    )
    out_specs = (P("dom", None), P("dom", None))
    return jax.shard_map(shards, mesh=mesh, in_specs=in_specs, out_specs=out_specs, check_vma=False)
```

```python
import functools

import jax
import jax.numpy as jnp
from jax import lax
from jax.experimental import pallas as pl
from jax.experimental.pallas import tpu as pltpu
from jax.sharding import PartitionSpec as P

F32 = jnp.float32
BF16 = jnp.bfloat16
SCALE = 0.7978845608
CUBIC = 0.044715
MIB = 1 << 20
HBM = pl.BlockSpec(memory_space=pltpu.HBM)
SMEM = pl.BlockSpec(memory_space=pltpu.SMEM)
VMEM = pl.BlockSpec(memory_space=pltpu.VMEM)
DMA = pltpu.SemaphoreType.DMA


def swap(value, axis, step):
    size = lax.axis_size(axis)
    return lax.ppermute(value, axis, [(index, index ^ step) for index in range(size)])


def cross(value, step):
    reps, doms = lax.axis_size("rep"), lax.axis_size("dom")
    pairs = [
        (rep * doms + dom, rep * doms + (dom ^ step ^ (rep & 1))) for rep in range(reps) for dom in range(doms)
    ]
    return lax.ppermute(value, ("rep", "dom"), [(source, target) for source, target in pairs if source != target])


def split_copies(source, target, sems, count=4):
    size = source.shape[0] // count
    return [
        pltpu.make_async_copy(
            source.at[index * size : (index + 1) * size], target.at[index * size : (index + 1) * size], sems.at[index]
        )
        for index in range(count)
    ]


def slots_kernel(
    src_hbm, peer_hbm, tiles_hbm, features_hbm, out_hbm, src, peer, tiles, features, dense, out, in_sems, out_sems
):
    scalars = [
        pltpu.make_async_copy(src_hbm, src, in_sems.at[2, 0]),
        pltpu.make_async_copy(peer_hbm, peer, in_sems.at[2, 1]),
    ]
    tile_copies = split_copies(tiles_hbm, tiles, in_sems.at[0])
    feature_copies = split_copies(features_hbm, features, in_sems.at[1])
    for copy in scalars + tile_copies + feature_copies:
        copy.start()
    count, block, _ = tiles.shape
    dense[...] = jnp.zeros_like(dense)
    for copy in scalars + tile_copies:
        copy.wait()

    def place(tile, carry):
        row = pl.multiple_of(peer[tile] * block, block)
        column = pl.multiple_of(src[tile] * block, block)
        at = (pl.ds(row, block), pl.ds(column, block))
        dense[at] = dense[at] + tiles[tile].astype(F32)
        return carry

    lax.fori_loop(0, count, place, 0)
    for copy in feature_copies:
        copy.wait()
    chunk = 4 * block
    results = []
    for index in range(out.shape[0] // chunk):
        at = slice(index * chunk, (index + 1) * chunk)
        out[at, :] = jnp.dot(dense[at, :].astype(BF16), features[...], preferred_element_type=F32).astype(BF16)
        results.append(pltpu.make_async_copy(out.at[at, :], out_hbm.at[at, :], out_sems.at[index]))
        results[-1].start()
    for result in results:
        result.wait()


def weight_copies(flip, weight_hbms, weight, sems):
    sources = len(weight_hbms)
    copies = []
    for source, weight_hbm in enumerate(weight_hbms):
        for piece in range(weight_hbm.shape[0]):
            target = piece if sources == 1 else 2 * piece + (flip ^ source)
            copies.append(
                pltpu.make_async_copy(weight_hbm.at[piece], weight.at[target], sems.at[sources * piece + source])
            )
    return copies


def self_kernel(flip_ref, features_hbm, *refs):
    *weight_hbms, out_hbm, features, weight, out, feature_sems, weight_sems, out_sems = refs
    rows, width = features.shape
    hidden = out.shape[1]
    copies = weight_copies(flip_ref[0], weight_hbms, weight, weight_sems)
    copies += split_copies(features_hbm, features, feature_sems)
    for copy in copies:
        copy.start()
    for copy in copies:
        copy.wait()
    chunk = 256
    results = split_copies(out, out_hbm, out_sems, rows // chunk)
    for index, result in enumerate(results):
        at = slice(index * chunk, (index + 1) * chunk)
        out[at, :] = jnp.dot(
            features[at, :], weight[...].reshape(width, hidden), preferred_element_type=F32
        ).astype(BF16)
        result.start()
    for result in results:
        result.wait()


def layer_kernel(
    sources, pieces, places_ref, into_ref, slots_hbm, total_hbm, features_hbm, cotangent_hbm, *refs
):
    weight_hbms, out_hbms = refs[:sources], refs[sources:-15]
    slots, slot_sems = refs[-15:-13]
    total, features, cotangent, weight, summed, values, aggregate, grad, both = refs[-13:-4]
    row_sems, weight_sems, feature_sems, out_sems = refs[-4:]
    senders, block, _ = slots.shape
    rows, hidden = grad.shape
    width = aggregate.shape[1]
    core, flip, low, upper = [places_ref[index] for index in range(4)]
    chunk = 256
    parts = rows // chunk
    weights = weight_copies(flip, weight_hbms, weight, weight_sems)
    totals = split_copies(total_hbm, total, row_sems.at[0], parts)
    cotangents = split_copies(cotangent_hbm, cotangent, row_sems.at[1], parts)
    inputs = split_copies(features_hbm, features, feature_sems)
    arrivals = [
        pltpu.make_async_copy(slots_hbm.at[sender], slots.at[sender], slot_sems.at[sender]) for sender in range(senders)
    ]
    for copy in arrivals + weights + totals[:1] + cotangents[:1]:
        copy.start()

    def target(sender):
        return pl.ds(pl.multiple_of(into_ref[sender] * block, block), block)

    for index in range(rows // block):
        reached = functools.reduce(jnp.logical_or, [into_ref[sender] == index for sender in range(senders)])

        @pl.when(jnp.logical_not(reached))
        def _():
            summed[index * block : (index + 1) * block, :] = jnp.zeros((block, width), F32)

    for copy in arrivals:
        copy.wait()
    for copy in [copy for pair in zip(totals[1:], cotangents[1:]) for copy in pair]:
        copy.start()
    for sender in range(senders):
        if sender == 0:
            summed[target(0), :] = slots[0].astype(F32)
            continue
        again = functools.reduce(jnp.logical_or, [into_ref[sender] == into_ref[index] for index in range(sender)])

        @pl.when(again)
        def _():
            summed[target(sender), :] = summed[target(sender), :] + slots[sender].astype(F32)

        @pl.when(jnp.logical_not(again))
        def _():
            summed[target(sender), :] = slots[sender].astype(F32)

    aggregate[...] = summed[...].astype(BF16)
    for copy in weights:
        copy.wait()
    span = hidden // 2

    def multiply(index):
        at = slice(index * chunk, (index + 1) * chunk)
        for begin in range(0, hidden, span):
            columns = slice(begin, begin + span)
            values[index % 2, :, columns] = jnp.dot(
                aggregate[at, :], weight[:, :, columns].reshape(width, span), preferred_element_type=F32
            )

    multiply(0)
    for index in range(parts):
        if index + 1 < parts:
            multiply(index + 1)
        totals[index].wait()
        cotangents[index].wait()
        if index == 0:
            for copy in inputs:
                copy.start()
        for row in range(0, chunk, 16):
            at = slice(index * chunk + row, index * chunk + row + 16)
            for begin in range(0, hidden, span):
                columns = slice(begin, begin + span)
                value = values[index % 2, row : row + 16, columns] + total[at, columns].astype(F32)
                square = value * value
                bend = jnp.tanh(value * (square * (SCALE * CUBIC) + SCALE))
                inner = value * (square * (1.5 * SCALE * CUBIC) + 0.5 * SCALE)
                slope = (1.0 + bend) * (inner * (1.0 - bend) + 0.5)
                grad[at, columns] = (cotangent[at, columns].astype(F32) * slope).astype(BF16)

    for copy in inputs:
        copy.wait()
    moves = []
    for term, which in enumerate([1 - core, core]):
        for index, target in enumerate(out_hbms[2 * term : 2 * term + 2]):
            if not pieces:
                moves.append((index, which, both.at[index, which], target))
                continue
            row_bit, column_bit = (low, upper) if index else (1 - low, 1 - upper)
            for row in range(target.shape[0]):
                for side in range(2):
                    half = jnp.where(which == 0, side, column_bit)
                    place = 2 * row + jnp.where(which == 0, row_bit, side)
                    columns = slice(side * span, (side + 1) * span)
                    moves.append((half, which, both.at[half, which, place], target.at[row, :, columns]))
    contract = (((0,), (0,)), ((), ()))
    results = [
        pltpu.make_async_copy(source, target, out_sems.at[index]) for index, (_, _, source, target) in enumerate(moves)
    ]
    for half in range(2):
        columns = slice(half * span, (half + 1) * span)
        for index, operand in enumerate([features, aggregate]):
            product = lax.dot_general(operand[...], grad[:, columns], contract, preferred_element_type=F32)
            both[half, index] = product.astype(BF16).reshape(both.shape[2:])
            for move, result in zip(moves, results):
                pl.when(jnp.logical_and(move[0] == half, move[1] == index))(result.start)
    for result in results:
        result.wait()


def call(kernel, outs, places, out_places, scratch=(), flops=0, moved=0, vmem=56):
    return pl.pallas_call(
        kernel,
        out_shape=outs,
        in_specs=places,
        out_specs=out_places,
        scratch_shapes=list(scratch),
        compiler_params=pltpu.CompilerParams(vmem_limit_bytes=vmem * MIB),
        cost_estimate=pl.CostEstimate(flops=flops, bytes_accessed=moved, transcendentals=0),
    )


def joined(held, other, upper, axis):
    return jnp.stack([jnp.where(upper, other, held), jnp.where(upper, held, other)], axis=axis)


def gather_high(held, high):
    step = 1
    while step < lax.axis_size("rep") // 2:
        other = swap(held, "rep", 2 * step)
        upper = (high & step) != 0
        held = jnp.concatenate([jnp.where(upper, other, held), jnp.where(upper, held, other)], axis=-1)
        step *= 2
    return held


def added(terms):
    return sum(term.astype(F32) for term in terms).astype(BF16)


def half_of(value, axis, which):
    size = value.shape[axis] // 2
    return lax.dynamic_slice_in_dim(value, which * size, size, axis)


def first_pieces(term, depth, core, low, upper):
    term = term.reshape(-1, 2, depth, 2, term.shape[1] // 2)
    pieces = []
    for row_bit, column_bit in ((1 - low, 1 - upper), (low, upper)):
        rows = lax.dynamic_index_in_dim(term, row_bit, 1, keepdims=False)
        columns = lax.dynamic_index_in_dim(term, column_bit, 3, keepdims=False).swapaxes(1, 2)
        pieces.append(jnp.where(core == 0, rows, columns).reshape(term.shape[0], depth, -1))
    return pieces


def turn_swap(value, turn):
    reps, doms = lax.axis_size("rep"), lax.axis_size("dom")
    pairs = []
    for rep in range(reps):
        for dom in range(doms):
            target = rep * doms + (dom ^ 1) if rep % 2 == turn else (rep ^ (reps // 2)) * doms + dom
            pairs.append((rep * doms + dom, target))
    return lax.ppermute(value, ("rep", "dom"), pairs)


def column_half(term, which):
    size = term.shape[-1] // 2
    return lax.dynamic_slice_in_dim(term, which * size, size, term.ndim - 1)


def exchanged(term, take, which, axis, step):
    return added([take(term, which), swap(take(term, 1 - which), axis, step)])


def reduce_high(term, high, step):
    while step:
        term = exchanged(term, column_half, (high // step) % 2, "rep", 2 * step)
        step //= 2
    return term


def shards(features, cotangent, w_self, w_neigh, tile_vals, tile_src, tile_peer, in_block):
    dom_size = lax.axis_size("dom")
    rows, width = features.shape
    hidden = w_self.shape[1]
    block = tile_vals.shape[1]
    me = lax.axis_index("dom")
    rep = lax.axis_index("rep")
    parts = lax.axis_size("rep") // 2
    core, high = rep & 1, rep >> 1
    low, place = me & 1, me >> 1

    share = hidden // parts
    top = dom_size // 2
    held = jnp.stack([lax.dynamic_slice_in_dim(weight, high * share, share, 1) for weight in (w_self, w_neigh)])
    near, far = cross(held, 0), cross(held, top)
    slots = call(
        slots_kernel,
        jax.ShapeDtypeStruct((dom_size * block, width), BF16),
        [HBM] * 4,
        HBM,
        [
            pltpu.SMEM(tile_src.shape, jnp.int32),
            pltpu.SMEM(tile_peer.shape, jnp.int32),
            pltpu.VMEM(tile_vals.shape, BF16),
            pltpu.VMEM(features.shape, BF16),
            pltpu.VMEM((dom_size * block, rows), F32),
            pltpu.VMEM((dom_size * block, width), BF16),
            DMA((3, 4)),
            DMA((dom_size // 4,)),
        ],
        flops=2 * dom_size * block * rows * width,
        moved=tile_vals.size * 2 + rows * width * 4,
    )(tile_src, tile_peer, tile_vals, features)
    near, far, slots = lax.optimization_barrier((near, far, slots))
    held = joined(jnp.where(core == 0, held, near), far, (me & top) != 0, 1)
    step = top // 2
    while step > 1:
        held = joined(held, swap(held, "dom", step), (me & step) != 0, 2)
        held = held.reshape(2, -1, *held.shape[3:])
        step //= 2
    received = lax.all_to_all(slots.reshape(dom_size, block, width), "dom", split_axis=0, concat_axis=0, tiled=True)
    mine = gather_high(held, high)
    depth = width // dom_size
    tiled = depth % 16 == 0
    flip = low ^ core
    weights = [[mine[index], swap(mine[index], "rep", 1)] for index in range(2)]
    if not tiled:
        weights = [[joined(*weight, flip != 0, 1).reshape(-1, 128, hidden)] for weight in weights]
    sources, count = len(weights[0]), sum(weight.shape[0] for weight in weights[0])
    weight_shape = pltpu.VMEM((count, width // count, hidden), BF16)
    total = call(
        self_kernel,
        jax.ShapeDtypeStruct((rows, hidden), BF16),
        [SMEM] + [HBM] * (1 + sources),
        HBM,
        [
            pltpu.VMEM((rows, width), BF16),
            weight_shape,
            pltpu.VMEM((rows, hidden), BF16),
            DMA((4,)),
            DMA((count,)),
            DMA((rows // 256,)),
        ],
        flops=2 * rows * width * hidden,
        moved=7 * rows * hidden,
    )(flip.astype(jnp.int32).reshape(1), features, *weights[0])
    span = hidden // 2
    upper = (high // (parts // 2)) % 2
    places = jnp.stack([core, flip, low, upper]).astype(jnp.int32)
    if tiled:
        out_shapes = [jax.ShapeDtypeStruct((dom_size // 2, depth, hidden), BF16)] * 4
        product_shape = (2, 2, dom_size, depth, span)
    else:
        out_shapes = [jax.ShapeDtypeStruct((width, span), BF16)] * 4
        product_shape = (2, 2, width, span)
    outs = call(
        functools.partial(layer_kernel, sources, tiled),
        out_shapes,
        [SMEM, SMEM] + [HBM] * (4 + sources),
        [HBM] * 4,
        [
            pltpu.VMEM((dom_size, block, width), BF16),
            DMA((dom_size,)),
            pltpu.VMEM((rows, hidden), BF16),
            pltpu.VMEM((rows, width), BF16),
            pltpu.VMEM((rows, hidden), BF16),
            weight_shape,
            pltpu.VMEM((rows, width), F32),
            pltpu.VMEM((2, 256, hidden), F32),
            pltpu.VMEM((rows, width), BF16),
            pltpu.VMEM((rows, hidden), BF16),
            pltpu.VMEM(product_shape, BF16),
            DMA((2, rows // 256)),
            DMA((count,)),
            DMA((4,)),
            DMA((4 * dom_size,)),
        ],
        flops=6 * rows * width * hidden,
        moved=16 * rows * hidden,
    )(places, in_block, received, total, features, cotangent, *weights[1])
    sent, kept = outs[:2], outs[2:]
    if not tiled:
        sent, kept = [
            first_pieces(jnp.concatenate(pair, axis=1), depth, which, low, upper)
            for pair, which in ((sent, 1 - core), (kept, core))
        ]
    leave, stay = [[own, swap(piece, "rep", 1)] for own, piece in zip(kept, sent)]
    bit = jnp.where(core == 0, upper, low)
    halves = []
    size = dom_size // 4
    for begin in (0, size):
        gone, kept = [[term[begin : begin + size] for term in terms] for terms in (leave, stay)]
        held = added([*kept, turn_swap(added(gone), 0)])
        halves.append(added([column_half(held, bit), turn_swap(column_half(held, 1 - bit), 1)]))
    held = jnp.concatenate(halves)
    both = reduce_high(held, high, parts // 4)
    summed = lax.dynamic_index_in_dim(both, place, 0, keepdims=False).astype(F32)
    for step in range(1, dom_size // 2):
        piece = lax.dynamic_index_in_dim(both, place ^ step, 0, keepdims=False)
        summed = summed + swap(piece, "dom", 2 * step).astype(F32)
    summed = summed.astype(BF16)
    whole = gather_high(summed, high)
    opposite = swap(whole, "rep", 1)
    return (
        jnp.where(core == 0, whole, opposite).astype(F32),
        jnp.where(core == 0, opposite, whole).astype(F32),
    )


def solution(mesh):
    in_specs = (
        P(("rep", "dom"), None),
        P(("rep", "dom"), None),
        P("dom", None),
        P("dom", None),
        P(("rep", "dom"), None, None),
        P(("rep", "dom")),
        P(("rep", "dom")),
        P(("rep", "dom")),
    )
    out_specs = (P("dom", None), P("dom", None))
    return jax.shard_map(shards, mesh=mesh, in_specs=in_specs, out_specs=out_specs, check_vma=False)
```

```python
import functools

import jax
import jax.numpy as jnp
from jax import lax
from jax.experimental import pallas as pl
from jax.experimental.pallas import tpu as pltpu
from jax.sharding import PartitionSpec as P

F32 = jnp.float32
BF16 = jnp.bfloat16
SCALE = 0.7978845608
CUBIC = 0.044715
MIB = 1 << 20
HBM = pl.BlockSpec(memory_space=pltpu.HBM)
SMEM = pl.BlockSpec(memory_space=pltpu.SMEM)
VMEM = pl.BlockSpec(memory_space=pltpu.VMEM)
DMA = pltpu.SemaphoreType.DMA


def swap(value, axis, step):
    size = lax.axis_size(axis)
    return lax.ppermute(value, axis, [(index, index ^ step) for index in range(size)])


def cross(value, step):
    reps, doms = lax.axis_size("rep"), lax.axis_size("dom")
    pairs = [
        (rep * doms + dom, rep * doms + (dom ^ step ^ (rep & 1))) for rep in range(reps) for dom in range(doms)
    ]
    return lax.ppermute(value, ("rep", "dom"), [(source, target) for source, target in pairs if source != target])


def split_copies(source, target, sems, count=4):
    size = source.shape[0] // count
    return [
        pltpu.make_async_copy(
            source.at[index * size : (index + 1) * size], target.at[index * size : (index + 1) * size], sems.at[index]
        )
        for index in range(count)
    ]


def slots_kernel(
    src_hbm, peer_hbm, tiles_hbm, features_hbm, out_hbm, src, peer, tiles, features, dense, out, in_sems, out_sems
):
    scalars = [
        pltpu.make_async_copy(src_hbm, src, in_sems.at[2, 0]),
        pltpu.make_async_copy(peer_hbm, peer, in_sems.at[2, 1]),
    ]
    tile_copies = split_copies(tiles_hbm, tiles, in_sems.at[0])
    feature_copies = split_copies(features_hbm, features, in_sems.at[1])
    for copy in scalars + tile_copies + feature_copies:
        copy.start()
    count, block, _ = tiles.shape
    dense[...] = jnp.zeros_like(dense)
    for copy in scalars + tile_copies:
        copy.wait()

    def place(tile, carry):
        row = pl.multiple_of(peer[tile] * block, block)
        column = pl.multiple_of(src[tile] * block, block)
        at = (pl.ds(row, block), pl.ds(column, block))
        dense[at] = dense[at] + tiles[tile].astype(F32)
        return carry

    lax.fori_loop(0, count, place, 0)
    for copy in feature_copies:
        copy.wait()
    chunk = 4 * block
    results = []
    for index in range(out.shape[0] // chunk):
        at = slice(index * chunk, (index + 1) * chunk)
        out[at, :] = jnp.dot(dense[at, :].astype(BF16), features[...], preferred_element_type=F32).astype(BF16)
        results.append(pltpu.make_async_copy(out.at[at, :], out_hbm.at[at, :], out_sems.at[index]))
        results[-1].start()
    for result in results:
        result.wait()


def weight_copies(flip, weight_hbms, weight, sems):
    sources = len(weight_hbms)
    copies = []
    for source, weight_hbm in enumerate(weight_hbms):
        for piece in range(weight_hbm.shape[0]):
            target = piece if sources == 1 else 2 * piece + (flip ^ source)
            copies.append(
                pltpu.make_async_copy(weight_hbm.at[piece], weight.at[target], sems.at[sources * piece + source])
            )
    return copies


def self_kernel(flip_ref, features_hbm, *refs):
    *weight_hbms, out_hbm, features, weight, out, feature_sems, weight_sems, out_sems = refs
    rows, width = features.shape
    hidden = out.shape[1]
    copies = weight_copies(flip_ref[0], weight_hbms, weight, weight_sems)
    copies += split_copies(features_hbm, features, feature_sems)
    for copy in copies:
        copy.start()
    for copy in copies:
        copy.wait()
    chunk = 256
    results = split_copies(out, out_hbm, out_sems, rows // chunk)
    for index, result in enumerate(results):
        at = slice(index * chunk, (index + 1) * chunk)
        out[at, :] = jnp.dot(
            features[at, :], weight[...].reshape(width, hidden), preferred_element_type=F32
        ).astype(BF16)
        result.start()
    for result in results:
        result.wait()


def layer_kernel(
    sources, pieces, places_ref, into_ref, slots_hbm, total_hbm, features_hbm, cotangent_hbm, *refs
):
    weight_hbms, out_hbms = refs[:sources], refs[sources:-15]
    slots, slot_sems = refs[-15:-13]
    total, features, cotangent, weight, summed, values, aggregate, grad, both = refs[-13:-4]
    row_sems, weight_sems, feature_sems, out_sems = refs[-4:]
    senders, block, _ = slots.shape
    rows, hidden = grad.shape
    width = aggregate.shape[1]
    core, flip, low, upper = [places_ref[index] for index in range(4)]
    chunk = 256
    parts = rows // chunk
    weights = weight_copies(flip, weight_hbms, weight, weight_sems)
    totals = split_copies(total_hbm, total, row_sems.at[0], parts)
    cotangents = split_copies(cotangent_hbm, cotangent, row_sems.at[1], parts)
    inputs = split_copies(features_hbm, features, feature_sems)
    arrivals = [
        pltpu.make_async_copy(slots_hbm.at[sender], slots.at[sender], slot_sems.at[sender]) for sender in range(senders)
    ]
    for copy in arrivals + weights + totals[:1] + cotangents[:1]:
        copy.start()

    def target(sender):
        return pl.ds(pl.multiple_of(into_ref[sender] * block, block), block)

    for index in range(rows // block):
        reached = functools.reduce(jnp.logical_or, [into_ref[sender] == index for sender in range(senders)])

        @pl.when(jnp.logical_not(reached))
        def _():
            summed[index * block : (index + 1) * block, :] = jnp.zeros((block, width), F32)

    for copy in arrivals:
        copy.wait()
    for copy in [copy for pair in zip(totals[1:], cotangents[1:]) for copy in pair] + inputs:
        copy.start()
    for sender in range(senders):
        if sender == 0:
            summed[target(0), :] = slots[0].astype(F32)
            continue
        again = functools.reduce(jnp.logical_or, [into_ref[sender] == into_ref[index] for index in range(sender)])

        @pl.when(again)
        def _():
            summed[target(sender), :] = summed[target(sender), :] + slots[sender].astype(F32)

        @pl.when(jnp.logical_not(again))
        def _():
            summed[target(sender), :] = slots[sender].astype(F32)

    aggregate[...] = summed[...].astype(BF16)
    for copy in weights:
        copy.wait()
    span = hidden // 2

    def multiply(index):
        at = slice(index * chunk, (index + 1) * chunk)
        for begin in range(0, hidden, span):
            columns = slice(begin, begin + span)
            values[index % 2, :, columns] = jnp.dot(
                aggregate[at, :], weight[:, :, columns].reshape(width, span), preferred_element_type=F32
            )

    multiply(0)
    for index in range(parts):
        if index + 1 < parts:
            multiply(index + 1)
        totals[index].wait()
        cotangents[index].wait()
        for row in range(0, chunk, 16):
            at = slice(index * chunk + row, index * chunk + row + 16)
            for begin in range(0, hidden, 256):
                columns = slice(begin, begin + 256)
                value = values[index % 2, row : row + 16, columns] + total[at, columns].astype(F32)
                square = value * value
                bend = jnp.tanh(value * (square * (SCALE * CUBIC) + SCALE))
                inner = value * (square * (1.5 * SCALE * CUBIC) + 0.5 * SCALE)
                slope = (1.0 + bend) * (inner * (1.0 - bend) + 0.5)
                grad[at, columns] = (cotangent[at, columns].astype(F32) * slope).astype(BF16)

    for copy in inputs:
        copy.wait()
    moves = []
    for term, which in enumerate([1 - core, core]):
        for index, target in enumerate(out_hbms[2 * term : 2 * term + 2]):
            if not pieces:
                moves.append((index, which, both.at[index, which], target))
                continue
            row_bit, column_bit = (low, upper) if index else (1 - low, 1 - upper)
            for row in range(target.shape[0]):
                for side in range(2):
                    half = jnp.where(which == 0, side, column_bit)
                    place = 2 * row + jnp.where(which == 0, row_bit, side)
                    columns = slice(side * span, (side + 1) * span)
                    moves.append((half, which, both.at[half, which, place], target.at[row, :, columns]))
    contract = (((0,), (0,)), ((), ()))
    results = [
        pltpu.make_async_copy(source, target, out_sems.at[index]) for index, (_, _, source, target) in enumerate(moves)
    ]
    for half in range(2):
        columns = slice(half * span, (half + 1) * span)
        for index, operand in enumerate([features, aggregate]):
            product = lax.dot_general(operand[...], grad[:, columns], contract, preferred_element_type=F32)
            both[half, index] = product.astype(BF16).reshape(both.shape[2:])
            for move, result in zip(moves, results):
                pl.when(jnp.logical_and(move[0] == half, move[1] == index))(result.start)
    for result in results:
        result.wait()


def call(kernel, outs, places, out_places, scratch=(), flops=0, moved=0, vmem=56):
    return pl.pallas_call(
        kernel,
        out_shape=outs,
        in_specs=places,
        out_specs=out_places,
        scratch_shapes=list(scratch),
        compiler_params=pltpu.CompilerParams(vmem_limit_bytes=vmem * MIB),
        cost_estimate=pl.CostEstimate(flops=flops, bytes_accessed=moved, transcendentals=0),
    )


def joined(held, other, upper, axis):
    return jnp.stack([jnp.where(upper, other, held), jnp.where(upper, held, other)], axis=axis)


def gather_high(held, high):
    step = 1
    while step < lax.axis_size("rep") // 2:
        other = swap(held, "rep", 2 * step)
        upper = (high & step) != 0
        held = jnp.concatenate([jnp.where(upper, other, held), jnp.where(upper, held, other)], axis=-1)
        step *= 2
    return held


def added(terms):
    return sum(term.astype(F32) for term in terms).astype(BF16)


def half_of(value, axis, which):
    size = value.shape[axis] // 2
    return lax.dynamic_slice_in_dim(value, which * size, size, axis)


def first_pieces(term, depth, core, low, upper):
    term = term.reshape(-1, 2, depth, 2, term.shape[1] // 2)
    pieces = []
    for row_bit, column_bit in ((1 - low, 1 - upper), (low, upper)):
        rows = lax.dynamic_index_in_dim(term, row_bit, 1, keepdims=False)
        columns = lax.dynamic_index_in_dim(term, column_bit, 3, keepdims=False).swapaxes(1, 2)
        pieces.append(jnp.where(core == 0, rows, columns).reshape(term.shape[0], depth, -1))
    return pieces


def turn_swap(value, turn):
    reps, doms = lax.axis_size("rep"), lax.axis_size("dom")
    pairs = []
    for rep in range(reps):
        for dom in range(doms):
            target = rep * doms + (dom ^ 1) if rep % 2 == turn else (rep ^ (reps // 2)) * doms + dom
            pairs.append((rep * doms + dom, target))
    return lax.ppermute(value, ("rep", "dom"), pairs)


def column_half(term, which):
    size = term.shape[-1] // 2
    return lax.dynamic_slice_in_dim(term, which * size, size, term.ndim - 1)


def exchanged(term, take, which, axis, step):
    return added([take(term, which), swap(take(term, 1 - which), axis, step)])


def reduce_high(term, high, step):
    while step:
        term = exchanged(term, column_half, (high // step) % 2, "rep", 2 * step)
        step //= 2
    return term


def shards(features, cotangent, w_self, w_neigh, tile_vals, tile_src, tile_peer, in_block):
    dom_size = lax.axis_size("dom")
    rows, width = features.shape
    hidden = w_self.shape[1]
    block = tile_vals.shape[1]
    me = lax.axis_index("dom")
    rep = lax.axis_index("rep")
    parts = lax.axis_size("rep") // 2
    core, high = rep & 1, rep >> 1
    low, place = me & 1, me >> 1

    share = hidden // parts
    top = dom_size // 2
    held = jnp.stack([lax.dynamic_slice_in_dim(weight, high * share, share, 1) for weight in (w_self, w_neigh)])
    near, far = cross(held, 0), cross(held, top)
    slots = call(
        slots_kernel,
        jax.ShapeDtypeStruct((dom_size * block, width), BF16),
        [HBM] * 4,
        HBM,
        [
            pltpu.SMEM(tile_src.shape, jnp.int32),
            pltpu.SMEM(tile_peer.shape, jnp.int32),
            pltpu.VMEM(tile_vals.shape, BF16),
            pltpu.VMEM(features.shape, BF16),
            pltpu.VMEM((dom_size * block, rows), F32),
            pltpu.VMEM((dom_size * block, width), BF16),
            DMA((3, 4)),
            DMA((dom_size // 4,)),
        ],
        flops=2 * dom_size * block * rows * width,
        moved=tile_vals.size * 2 + rows * width * 4,
    )(tile_src, tile_peer, tile_vals, features)
    near, far, slots = lax.optimization_barrier((near, far, slots))
    held = joined(jnp.where(core == 0, held, near), far, (me & top) != 0, 1)
    step = top // 2
    while step > 1:
        held = joined(held, swap(held, "dom", step), (me & step) != 0, 2)
        held = held.reshape(2, -1, *held.shape[3:])
        step //= 2
    received = lax.all_to_all(slots.reshape(dom_size, block, width), "dom", split_axis=0, concat_axis=0, tiled=True)
    mine = gather_high(held, high)
    depth = width // dom_size
    tiled = depth % 16 == 0
    flip = low ^ core
    weights = [[mine[index], swap(mine[index], "rep", 1)] for index in range(2)]
    if not tiled:
        weights = [[joined(*weight, flip != 0, 1).reshape(-1, 128, hidden)] for weight in weights]
    sources, count = len(weights[0]), sum(weight.shape[0] for weight in weights[0])
    weight_shape = pltpu.VMEM((count, width // count, hidden), BF16)
    total = call(
        self_kernel,
        jax.ShapeDtypeStruct((rows, hidden), BF16),
        [SMEM] + [HBM] * (1 + sources),
        HBM,
        [
            pltpu.VMEM((rows, width), BF16),
            weight_shape,
            pltpu.VMEM((rows, hidden), BF16),
            DMA((4,)),
            DMA((count,)),
            DMA((rows // 256,)),
        ],
        flops=2 * rows * width * hidden,
        moved=7 * rows * hidden,
    )(flip.astype(jnp.int32).reshape(1), features, *weights[0])
    span = hidden // 2
    upper = (high // (parts // 2)) % 2
    places = jnp.stack([core, flip, low, upper]).astype(jnp.int32)
    if tiled:
        out_shapes = [jax.ShapeDtypeStruct((dom_size // 2, depth, hidden), BF16)] * 4
        product_shape = (2, 2, dom_size, depth, span)
    else:
        out_shapes = [jax.ShapeDtypeStruct((width, span), BF16)] * 4
        product_shape = (2, 2, width, span)
    outs = call(
        functools.partial(layer_kernel, sources, tiled),
        out_shapes,
        [SMEM, SMEM] + [HBM] * (4 + sources),
        [HBM] * 4,
        [
            pltpu.VMEM((dom_size, block, width), BF16),
            DMA((dom_size,)),
            pltpu.VMEM((rows, hidden), BF16),
            pltpu.VMEM((rows, width), BF16),
            pltpu.VMEM((rows, hidden), BF16),
            weight_shape,
            pltpu.VMEM((rows, width), F32),
            pltpu.VMEM((2, 256, hidden), F32),
            pltpu.VMEM((rows, width), BF16),
            pltpu.VMEM((rows, hidden), BF16),
            pltpu.VMEM(product_shape, BF16),
            DMA((2, rows // 256)),
            DMA((count,)),
            DMA((4,)),
            DMA((4 * dom_size,)),
        ],
        flops=6 * rows * width * hidden,
        moved=16 * rows * hidden,
    )(places, in_block, received, total, features, cotangent, *weights[1])
    sent, kept = outs[:2], outs[2:]
    if not tiled:
        sent, kept = [
            first_pieces(jnp.concatenate(pair, axis=1), depth, which, low, upper)
            for pair, which in ((sent, 1 - core), (kept, core))
        ]
    leave, stay = [[own, swap(piece, "rep", 1)] for own, piece in zip(kept, sent)]
    bit = jnp.where(core == 0, upper, low)
    halves = []
    size = dom_size // 4
    for begin in (0, size):
        gone, kept = [[term[begin : begin + size] for term in terms] for terms in (leave, stay)]
        held = added([*kept, turn_swap(added(gone), 0)])
        halves.append(added([column_half(held, bit), turn_swap(column_half(held, 1 - bit), 1)]))
    held = jnp.concatenate(halves)
    both = reduce_high(held, high, parts // 4)
    summed = lax.dynamic_index_in_dim(both, place, 0, keepdims=False).astype(F32)
    for step in range(1, dom_size // 2):
        piece = lax.dynamic_index_in_dim(both, place ^ step, 0, keepdims=False)
        summed = summed + swap(piece, "dom", 2 * step).astype(F32)
    summed = summed.astype(BF16)
    whole = gather_high(summed, high)
    opposite = swap(whole, "rep", 1)
    return (
        jnp.where(core == 0, whole, opposite).astype(F32),
        jnp.where(core == 0, opposite, whole).astype(F32),
    )


def solution(mesh):
    in_specs = (
        P(("rep", "dom"), None),
        P(("rep", "dom"), None),
        P("dom", None),
        P("dom", None),
        P(("rep", "dom"), None, None),
        P(("rep", "dom")),
        P(("rep", "dom")),
        P(("rep", "dom")),
    )
    out_specs = (P("dom", None), P("dom", None))
    return jax.shard_map(shards, mesh=mesh, in_specs=in_specs, out_specs=out_specs, check_vma=False)
```
